32 devices in a mesh: context: 4 (over y, x), expert: 8 (over z, core).
Axes of the slice: x: 2, y: 2, z: 4, core: 2. Of those that a mesh axis runs over, the one named last changes fastest.
Arguments:
- tokens_in: bfloat16 [8, 1024, 2048], P('expert', 'context'), may hold values from -6 to 6
- positions: int32 [8, 1024], P('expert'), may hold values from 0 to 1023, as said below
- routes: int32 [8, 1024, 8], P('expert', 'context'), may hold values from 0 to 15, all different within a row; in each aligned block of 256 rows (0 to 255, 256 to 511, ..., all dimensions but the last counted through in order) at most 256 rows name the same one
- cotangent: bfloat16 [8, 1024, 2048], P('expert', 'context'), may hold values from -6 to 6
- w_query: bfloat16 [2048, 2048], P(('context', 'expert')), may hold values from -0.125 to 0.125
- w_key: bfloat16 [2048, 2048], P(('context', 'expert')), may hold values from -0.125 to 0.125
- w_value: bfloat16 [2048, 2048], P(('context', 'expert')), may hold values from -0.125 to 0.125
- w_output: bfloat16 [2048, 2048], P(('context', 'expert')), may hold values from -1 to 1
- router: bfloat16 [2048, 16], P(('context', 'expert')), may hold values from -0.0625 to 0.0625
- attn_gain: bfloat16 [2048], P(('context', 'expert')), may hold values from 0.099609375 to 1.8984375
- query_gain: bfloat16 [2048], P(('context', 'expert')), may hold values from 0.099609375 to 1.8984375
- key_gain: bfloat16 [2048], P(('context', 'expert')), may hold values from 0.099609375 to 1.8984375
- moe_gain: bfloat16 [2048], P(('context', 'expert')), may hold values from 0.099609375 to 1.8984375
- expert_gate: bfloat16 [16, 2048, 1024], P('expert', 'context'), may hold values from -0.125 to 0.125
- expert_up: bfloat16 [16, 2048, 1024], P('expert', 'context'), may hold values from -0.125 to 0.125
- expert_down: bfloat16 [16, 1024, 2048], P('expert', 'context'), may hold values from -3 to 3
Outputs:
- output: bfloat16 [8, 1024, 2048], P('expert', 'context')
- input_grad: float32 [8, 1024, 2048], P('expert', 'context')
- grad_w_query: float32 [2048, 2048], P(('context', 'expert'))
- grad_w_key: float32 [2048, 2048], P(('context', 'expert'))
- grad_w_value: float32 [2048, 2048], P(('context', 'expert'))
- grad_w_output: float32 [2048, 2048], P(('context', 'expert'))
- grad_router: float32 [2048, 16], P(('context', 'expert'))
- grad_attn_gain: float32 [2048], P(('context', 'expert'))
- grad_query_gain: float32 [2048], P(('context', 'expert'))
- grad_key_gain: float32 [2048], P(('context', 'expert'))
- grad_moe_gain: float32 [2048], P(('context', 'expert'))
- grad_expert_gate: float32 [16, 2048, 1024], P('expert', 'context')
- grad_expert_up: float32 [16, 2048, 1024], P('expert', 'context')
- grad_expert_down: float32 [16, 1024, 2048], P('expert', 'context')
The draws below stay inside these ranges and needn't reach their ends.
Inputs may be any that keep to these rules, and one draw needn't show every extreme that they name: `routes`: each row names 8 different experts; in the rows of one device no expert is named more than 256 times. Within each sequence a permutation of its positions; each device's 256 rows are a run of 128 consecutive positions followed by the run at the mirror place from the sequence's end.
All inputs are finite; a program needn't handle non-finite values.
Results may differ from the reference program's by a relative error of at most 0.02.
Values may be sent and summed in bfloat16 or wider, within the bound.
No kernel may reach another device: no remote copies, remote signals or barrier semaphores. Data moves between devices by JAX's collectives and lax.ppermute only.
A program may use at most 512 MiB of HBM per device.

```python
import math
import jax
import jax.numpy as jnp
import numpy as np
from jax import lax

D = 2048
HEADS = 16
HEAD_DIM = 128
FF = 1024
TOPK = 8
SEQ = 1024
TOK_DEV = 256
NSEQ = 8
EXPERTS = 16
CAP = 256
N_CONTEXT = 4


def draw_positions(key, part):
    key = jax.random.fold_in(key, 7)
    groups = SEQ // TOK_DEV
    run_length = TOK_DEV // 2
    seed_list = jax.random.split(key, NSEQ)

    def one_sequence(seed_key):
        block_order = jax.random.permutation(seed_key, groups)
        run_starts = jnp.stack([block_order, 2 * groups - 1 - block_order], axis=1)
        return (run_starts[:, :, None] * run_length + jnp.arange(run_length)[None, None, :]).reshape(SEQ)
    return jax.vmap(one_sequence)(seed_list).astype(jnp.int32)


def block_scale(own_key, extent, shards, smallest, high):
    def one(dim, parts):
        heights = jax.random.uniform(jax.random.fold_in(jax.random.fold_in(own_key, 6), dim), (parts,), jnp.float32, smallest / len(shards), high / len(shards))
        return jnp.repeat(jnp.exp(heights), extent[dim] // parts).reshape((-1,) + (1,) * (len(extent) - dim - 1))

    gain = one(*shards[0])
    for cut in shards[1:]:
        gain = gain * one(*cut)
    return gain


def assign_block(stream_key, own, number, rows, number_of, top, most, slope):
    sequence = jax.random.permutation(stream_key, number_of)
    crowded, ordinary = shares(number_of, rows * top, most, slope, True), shares(number_of, rows * top, most, slope, False)
    places = jnp.arange(number_of)

    def named(tallies, rotation):
        used = int((tallies > 0).sum())
        fixed = max(1, used // 4)
        passed = fixed + (places - fixed + rotation * (used - fixed)) % max(1, number_of - fixed)
        return jnp.zeros((number_of,), jnp.int32).at[sequence[jnp.where(places < fixed, places, passed)]].set(jnp.asarray(tallies, jnp.int32))

    tallies = jnp.where(number % 4 == 0, named(crowded, number // 4), named(ordinary, number - number // 4 - 1))
    mixed = jax.random.permutation(jax.random.fold_in(own, 3), number_of)
    donor, taker = mixed[0:number_of // 2 * 2:2], mixed[1:number_of // 2 * 2:2]
    slack = jnp.minimum(tallies[donor] - 1, most - tallies[taker]) // 2
    slack = jnp.where((donor == sequence[0]) | (taker == sequence[0]) | (tallies[taker] == 0), 0, jnp.maximum(slack, 0))
    passed = jax.random.randint(jax.random.fold_in(own, 4), (number_of // 2,), 0, 1 << 20) % (slack + 1)
    tallies = tallies.at[donor].add(-passed).at[taker].add(passed)
    labels = jnp.searchsorted(jnp.cumsum(tallies), jnp.arange(rows * top), side="right").astype(jnp.int32)
    listing = labels.reshape(top, rows).T
    listing = listing[jax.random.permutation(jax.random.fold_in(own, 1), rows)]
    rotation = jax.random.randint(jax.random.fold_in(own, 2), (rows, 1), 0, top)
    return jnp.take_along_axis(listing, (jnp.arange(top)[None, :] + rotation) % top, axis=1)


def shares(count, total, limit, skew, full):
    weights = [(1 << 20) // math.isqrt(rank ** skew) + 1 for rank in range(1, count + 1)]
    largest = limit if full else min(limit, max(-(-total // count), total * weights[0] // sum(weights)))
    least = 1 if total - largest >= count - 1 else 0
    holding, spare = [largest] + [least] * (count - 1), total - largest - least * (count - 1)
    while spare > 0:
        free = [i for i in range(1, count) if holding[i] < largest] or [i for i in range(1, count) if holding[i] < limit]
        pool, budget = sum([weights[i] for i in free]), spare
        for i in free:
            more = min(limit - holding[i], max(1, budget * weights[i] // pool), spare)
            holding[i] = holding[i] + more
            spare = spare - more
    return np.array(holding)


def bell_draw(key, dims, width, limit, cuts=(), held_as=jnp.bfloat16):
    loudness = block_scale(key, dims, cuts, -0.22, 0.18) if cuts else 1.0
    entries = jax.random.normal(key, dims, jnp.float32) * width * loudness
    return jnp.minimum(jnp.maximum(entries, -limit), limit).astype(held_as)


def setup_inputs(seed: int = 0) -> dict:
    key_of = jax.random.split(jax.random.key(seed), 17)
    tokens_in = bell_draw(key_of[0], (NSEQ, SEQ, D), 1.0, 6.0, ((0, 8), (1, 4)))
    positions = draw_positions(jax.random.fold_in(key_of[16], 71), 0)
    routes_keys = jax.random.split(jax.random.fold_in(key_of[2], 1), NSEQ * SEQ // TOK_DEV)
    routes_turns = jax.random.permutation(jax.random.fold_in(key_of[2], 3), NSEQ * SEQ // TOK_DEV)
    routes = jax.vmap(lambda own, number: assign_block(jax.random.fold_in(key_of[2], 2), own, number, TOK_DEV, EXPERTS, TOPK, CAP, 1))(routes_keys, routes_turns).reshape((NSEQ, SEQ, TOPK))
    cotangent = bell_draw(key_of[3], (NSEQ, SEQ, D), 1.0, 6.0, ((0, 8), (1, 4)))
    w_query = bell_draw(key_of[4], (D, D), D ** -0.5, 0.125, ((0, 32),))
    w_key = bell_draw(key_of[5], (D, D), D ** -0.5, 0.125, ((0, 32),))
    w_value = bell_draw(key_of[6], (D, D), D ** -0.5, 0.125, ((0, 32),))
    w_output = bell_draw(key_of[7], (D, D), (max(D // 64, 1)) ** -0.5, 1.0, ((0, 32),))
    router = bell_draw(key_of[8], (D, EXPERTS), (4 * D) ** -0.5, 0.0625, ((0, 32),))
    attn_gain = jnp.clip(1.0 + 0.18 * jax.random.normal(key_of[9], (D,), jnp.float32), 0.099609375, 1.8984375).astype(jnp.bfloat16)
    query_gain = jnp.clip(1.0 + 0.18 * jax.random.normal(key_of[10], (D,), jnp.float32), 0.099609375, 1.8984375).astype(jnp.bfloat16)
    key_gain = jnp.clip(1.0 + 0.18 * jax.random.normal(key_of[11], (D,), jnp.float32), 0.099609375, 1.8984375).astype(jnp.bfloat16)
    moe_gain = jnp.clip(1.0 + 0.18 * jax.random.normal(key_of[12], (D,), jnp.float32), 0.099609375, 1.8984375).astype(jnp.bfloat16)
    expert_gate = bell_draw(key_of[13], (EXPERTS, D, FF), D ** -0.5, 0.125, ((0, 8), (1, 4)))
    expert_up = bell_draw(key_of[14], (EXPERTS, D, FF), D ** -0.5, 0.125, ((0, 8), (1, 4)))
    expert_down = bell_draw(key_of[15], (EXPERTS, FF, D), (max(FF // 256, 1)) ** -0.5, 3.0, ((0, 8), (1, 4)))
    return dict(tokens_in=tokens_in, positions=positions, routes=routes, cotangent=cotangent, w_query=w_query, w_key=w_key, w_value=w_value, w_output=w_output, router=router, attn_gain=attn_gain, query_gain=query_gain, key_gain=key_gain, moe_gain=moe_gain, expert_gate=expert_gate, expert_up=expert_up, expert_down=expert_down)


epsilon = 1e-05
rope_base = 10000.0
highest = lax.Precision.HIGHEST

@jax.custom_vjp
def low(v):
    return lax.optimization_barrier(v.astype(jnp.bfloat16)).astype(jnp.float32)

@jax.custom_vjp
def low_back(v):
    return v

def low_keep(v):
    return (low(v), None)

def low_pass(kept, grad):
    return (grad,)

def back_keep(v):
    return (v, None)

def back_low(kept, grad):
    return (low(grad),)
low.defvjp(low_keep, low_pass)
low_back.defvjp(back_keep, back_low)

def rms_apply(values, gain_vector):
    return values * lax.rsqrt(lax.optimization_barrier(jnp.mean(values * values, axis=-1, keepdims=True)) + epsilon) * gain_vector

def rotate(values, places):
    row_count = values.shape[0]
    half_dim = HEAD_DIM // 2
    frequency = jnp.exp(jnp.arange(half_dim, dtype=jnp.float32) * (-2.0 * math.log(rope_base) / HEAD_DIM))
    angles = places.astype(jnp.float32)[:, None] * frequency[None, :]
    cosine = jnp.cos(angles)[:, None, :]
    sine_part = jnp.sin(angles)[:, None, :]
    head_view = values.reshape(row_count, HEADS, HEAD_DIM)
    first_half = head_view[:, :, :half_dim]
    second_half = head_view[:, :, half_dim:]
    turned = jnp.concatenate([first_half * cosine - second_half * sine_part, second_half * cosine + first_half * sine_part], axis=-1)
    return turned.reshape(row_count, HEADS * HEAD_DIM)

def attend(query, keyv, value, places):
    row_count = query.shape[0]
    query_heads = query.reshape(row_count, HEADS, HEAD_DIM).transpose(1, 0, 2)
    key_heads = keyv.reshape(row_count, HEADS, HEAD_DIM).transpose(1, 0, 2)
    value_heads = value.reshape(row_count, HEADS, HEAD_DIM).transpose(1, 0, 2)
    allowed = places[None, :] <= places[:, None]

    def one_head(head_item):
        query_one, key_one, value_one = head_item
        scores = low_back(jnp.dot(query_one, key_one.T, precision=highest) * HEAD_DIM ** (-0.5))
        weights = jax.nn.softmax(jnp.where(allowed, scores, -1e+30), axis=-1)
        return jnp.dot(low(weights), value_one, precision=highest)
    attended = lax.map(jax.checkpoint(one_head), (query_heads, key_heads, value_heads))
    return attended.transpose(1, 0, 2).reshape(row_count, HEADS * HEAD_DIM)

def experts_apply(mixed_rows, route_rows, router_w, gate_w, up_w, down_w):
    row_count = mixed_rows.shape[0]
    expert_count = gate_w.shape[0]
    rows_each = N_CONTEXT * CAP
    logits = low_back(jnp.dot(mixed_rows, router_w, precision=highest))
    router_probs = jax.nn.softmax(logits, axis=-1)
    chosen = route_rows[:, :, None] == jnp.arange(expert_count, dtype=jnp.int32)[None, None, :]
    gate_values = lax.optimization_barrier(jnp.sum(router_probs[:, None, :] * chosen.astype(router_probs.dtype), axis=-1))
    chosen_int = chosen.reshape(row_count * TOPK, expert_count).astype(jnp.int32)
    rank_index = lax.optimization_barrier(jnp.sum((jnp.cumsum(chosen_int, axis=0).astype(jnp.int32) - chosen_int) * chosen_int, axis=-1)).astype(jnp.int32)
    slot_index = (route_rows.reshape(-1).astype(jnp.int32) * rows_each + rank_index).astype(jnp.int32)
    source_rows = jnp.repeat(mixed_rows, TOPK, axis=0)
    buffer_rows = jnp.zeros((expert_count * rows_each, mixed_rows.shape[1]), mixed_rows.dtype).at[slot_index].set(source_rows)
    buffer_rows = low_back(buffer_rows).reshape(expert_count, rows_each, mixed_rows.shape[1])

    def one_expert(expert_item):
        rows_in, gate_one, up_one, down_one = expert_item
        gate_act = low_back(jnp.dot(rows_in, gate_one, precision=highest))
        up_act = low_back(jnp.dot(rows_in, up_one, precision=highest))
        hidden = low(jax.nn.silu(gate_act) * up_act)
        return low(low_back(jnp.dot(hidden, down_one, precision=highest)))
    expert_out = lax.map(jax.checkpoint(one_expert), (buffer_rows, gate_w, up_w, down_w))
    expert_out = expert_out.reshape(expert_count * rows_each, mixed_rows.shape[1])
    picked = expert_out[slot_index].reshape(row_count, TOPK, mixed_rows.shape[1])
    return lax.optimization_barrier(jnp.sum(gate_values[:, :, None] * picked, axis=1))

def layer(hidden_in, weights, places, route_rows):
    query_w, key_w, value_w, output_w, router_w, attn_scale, query_scale, key_scale, moe_scale, gate_w, up_w, down_w = weights
    normed = low(rms_apply(hidden_in, attn_scale))
    query_proj = low_back(jnp.dot(normed, query_w, precision=highest))
    key_proj = low_back(jnp.dot(normed, key_w, precision=highest))
    value_rows = low(low_back(jnp.dot(normed, value_w, precision=highest)))
    query = low(rotate(rms_apply(query_proj, query_scale), places))
    keyv = low(rotate(rms_apply(key_proj, key_scale), places))
    attended = attend(query, keyv, value_rows, places)
    branch = low_back(jnp.dot(low(low_back(attended)), output_w, precision=highest))
    middle = hidden_in + branch
    mixed_rows = low(rms_apply(middle, moe_scale))
    return middle + experts_apply(mixed_rows, route_rows, router_w, gate_w, up_w, down_w)

def reference(tokens_in, positions, routes, cotangent, w_query, w_key, w_value, w_output, router, attn_gain, query_gain, key_gain, moe_gain, expert_gate, expert_up, expert_down):
    parameters = tuple((item.astype(jnp.float32) for item in (w_query, w_key, w_value, w_output, router, attn_gain, query_gain, key_gain, moe_gain, expert_gate, expert_up, expert_down)))
    zero_grads = tuple((jnp.zeros(item.shape, jnp.float32) for item in parameters))

    def per_sequence(totals, sequence_item):
        hidden_seq, place_seq, route_seq, back_seq = sequence_item

        def forward(hidden_in, *weights):
            return layer(hidden_in, weights, place_seq, route_seq)
        layer_out, pull_back = jax.vjp(forward, hidden_seq.astype(jnp.float32), *parameters)
        gradients = pull_back(back_seq.astype(jnp.float32))
        totals = tuple((total + grad for total, grad in zip(totals, gradients[1:])))
        return (totals, (layer_out.astype(jnp.bfloat16), gradients[0]))
    totals, (outputs, input_grads) = lax.scan(per_sequence, zero_grads, (tokens_in, positions, routes, cotangent))
    return (outputs, input_grads, totals[0], totals[1], totals[2], totals[3], totals[4], totals[5], totals[6], totals[7], totals[8], totals[9], totals[10], totals[11])
```

```python
import math

import jax
import jax.numpy as jnp
from jax import lax
from jax.sharding import PartitionSpec as P

HEADS = 16
HEAD_DIM = 128
EXP_DEV = 2
EXTRA = 128

epsilon = 1e-05
rope_base = 10000.0
masked_value = -1e30
bf16 = jnp.bfloat16
f32 = jnp.float32


def dot(left, right, dims):
    return lax.dot_general(left, right, (dims, ((), ())), preferred_element_type=f32)


def cuts(extent, parts):
    unit = 16 if extent % 16 == 0 and extent // 16 >= parts else 1
    units = extent // unit
    sizes = [(units // parts + (1 if i < units % parts else 0)) * unit for i in range(parts)]
    points = [0]
    for size in sizes:
        points.append(points[-1] + size)
    return points


def swap(value, axis, count, bit):
    return lax.ppermute(value, axis, [(i, i ^ bit) for i in range(count)])


def gather_xor(shard, axis, count, dim):
    steps = count.bit_length() - 1
    points = cuts(shard.shape[dim], steps)
    found = [[] for _ in range(count)]
    for part in range(steps):
        held = {0: lax.slice_in_dim(shard, points[part], points[part + 1], axis=dim)}
        for step in range(steps):
            bit = 1 << ((part + step) % steps)
            for place in list(held):
                held[place ^ bit] = swap(held[place], axis, count, bit)
        for place in range(count):
            found[place].append(held[place])
    return [jnp.concatenate(parts, axis=dim) for parts in found]


def scatter_xor(pieces, axis, count, dim):
    steps = count.bit_length() - 1
    points = cuts(pieces[0].shape[dim], steps)
    sums = []
    for part in range(steps):
        held = {
            place: lax.slice_in_dim(piece, points[part], points[part + 1], axis=dim)
            for place, piece in enumerate(pieces)
        }
        for step in range(steps):
            bit = 1 << ((part + steps - 1 - step) % steps)
            for place in [p for p in held if p & bit]:
                came = swap(held.pop(place).astype(bf16), axis, count, bit)
                held[place ^ bit] = held[place ^ bit].astype(f32) + came.astype(f32)
        sums.append(held[0])
    return jnp.concatenate(sums, axis=dim)


def xor_blocks(value, own, count, dim):
    width = value.shape[dim] // count
    return jnp.concatenate(
        [lax.dynamic_slice_in_dim(value, (own ^ k) * width, width, dim) for k in range(count)], axis=dim
    )


def rotate(values, cosine, sine, heads):
    rows = values.shape[0]
    view = values.reshape(rows, heads, HEAD_DIM)
    first, second = view[:, :, : HEAD_DIM // 2], view[:, :, HEAD_DIM // 2 :]
    turned = jnp.concatenate(
        [first * cosine - second * sine, second * cosine + first * sine], axis=-1
    )
    return turned.reshape(rows, heads * HEAD_DIM)


def inverse_rms(values):
    return lax.rsqrt(jnp.mean(values * values, axis=-1, keepdims=True) + epsilon)


def shards(
    tokens_in,
    positions,
    routes,
    cotangent,
    w_query,
    w_key,
    w_value,
    w_output,
    router,
    attn_gain,
    query_gain,
    key_gain,
    moe_gain,
    expert_gate,
    expert_up,
    expert_down,
):
    n_ctx, n_exp = lax.axis_size("context"), lax.axis_size("expert")
    own_ctx, own_exp = lax.axis_index("context"), lax.axis_index("expert")
    own_rows = tokens_in[0]
    tokens, width = own_rows.shape
    sequence = positions.shape[1]
    experts = EXP_DEV * n_exp
    heads = HEADS // n_ctx
    columns = heads * HEAD_DIM
    part = w_query.shape[0]

    def psum_rows(stats):
        stats = lax.psum(xor_blocks(stats, own_ctx, n_ctx, 1), "context")
        return xor_blocks(stats, own_ctx, n_ctx, 1)

    small = jnp.concatenate(
        [attn_gain[:, None], moe_gain[:, None], query_gain[:, None], key_gain[:, None], router], axis=1
    )
    small = jnp.pad(small, ((0, 0), (0, EXTRA - small.shape[1])))
    packed = jnp.concatenate(
        [w.reshape(part, n_ctx, columns).transpose(1, 0, 2) for w in (w_query, w_key, w_value)]
        + [jnp.broadcast_to(small[None], (n_ctx, part, EXTRA))],
        axis=2,
    )
    packed = lax.all_to_all(packed, "context", 0, 0, tiled=True)
    packed = lax.all_gather(packed, "expert", axis=0, tiled=False)
    packed = packed.transpose(1, 0, 2, 3).reshape(width, 3 * columns + EXTRA)
    w_qkv = packed[:, : 3 * columns]
    small_full = packed[:, 3 * columns :]
    small_rows = small_full[:, :4].T.astype(f32)
    attn_scale, moe_scale = small_rows[0], small_rows[1]
    query_scale = lax.dynamic_slice_in_dim(small_rows[2], own_ctx * columns, columns)
    key_scale = lax.dynamic_slice_in_dim(small_rows[3], own_ctx * columns, columns)
    router_full = small_full[:, 4 : 4 + experts]
    w_out = lax.all_gather(w_output, "expert", axis=0, tiled=True)

    inputs = jnp.concatenate(gather_xor(own_rows, "context", n_ctx, 0), axis=0).astype(f32)
    places = xor_blocks(positions[0], own_ctx, n_ctx, 0)

    named = jnp.sum(
        (routes[0][:, :, None] == jnp.arange(experts, dtype=jnp.int32)[None, None, :]).astype(f32), axis=1
    )
    named_all = lax.all_gather(named.astype(bf16), "expert", axis=0, tiled=True).astype(f32)
    pull = lax.all_gather(cotangent[0], "expert", axis=0, tiled=True)

    gate_w = jnp.concatenate(gather_xor(expert_gate, "context", n_ctx, 1), axis=1)
    up_w = jnp.concatenate(gather_xor(expert_up, "context", n_ctx, 1), axis=1)
    down_w = xor_blocks(
        jnp.concatenate(gather_xor(expert_down, "context", n_ctx, 1), axis=1), own_ctx, n_ctx, 1
    )

    input_r = inverse_rms(inputs)
    normed = (inputs * input_r * attn_scale).astype(bf16)
    projected = dot(normed, w_qkv, ((1,), (0,)))
    query_p, key_p = projected[:, :columns], projected[:, columns : 2 * columns]
    value = projected[:, 2 * columns :].astype(bf16)
    squares = jnp.stack([jnp.sum(query_p * query_p, axis=1), jnp.sum(key_p * key_p, axis=1)])
    squares = psum_rows(squares)
    r_both = lax.rsqrt(squares / width + epsilon)
    query_r, key_r = r_both[0][:, None], r_both[1][:, None]
    frequency = jnp.exp(
        jnp.arange(HEAD_DIM // 2, dtype=f32) * (-2.0 * math.log(rope_base) / HEAD_DIM)
    )
    angles = places.astype(f32)[:, None] * frequency[None, :]
    cosine, sine = jnp.cos(angles)[:, None, :], jnp.sin(angles)[:, None, :]
    query = rotate(query_p * query_r * query_scale, cosine, sine, heads).astype(bf16)
    keyv = rotate(key_p * key_r * key_scale, cosine, sine, heads).astype(bf16)
    score_scale = HEAD_DIM ** (-0.5)
    query_h, key_h, value_h = (v.reshape(sequence, heads, HEAD_DIM) for v in (query, keyv, value))
    allowed = (places[None, :] <= places[:, None])[None]

    def scores_of():
        raw = jnp.einsum("qhd,khd->hqk", query_h, key_h, preferred_element_type=f32)
        return jnp.where(allowed, raw * score_scale, masked_value)

    scores = scores_of()
    peak = jnp.max(scores, axis=-1, keepdims=True)
    exponent = jnp.exp(scores - peak)
    total = jnp.sum(exponent, axis=-1, keepdims=True)
    log_total = peak + jnp.log(total)
    attended = (
        jnp.einsum(
            "hqk,khd->qhd", (exponent / total).astype(bf16), value_h, preferred_element_type=f32
        )
        .reshape(sequence, columns)
        .astype(bf16)
    )
    branch = dot(attended, w_out, ((1,), (0,))).astype(bf16)
    branch_own = scatter_xor(jnp.split(branch, n_ctx, axis=0), "context", n_ctx, 0)
    middle = own_rows.astype(f32) + branch_own
    middle_r = inverse_rms(middle)
    mixed_own = (middle * middle_r * moe_scale).astype(bf16)

    mixed = lax.all_gather(xor_blocks(mixed_own, own_ctx, n_ctx, 1), "expert", axis=0, tiled=True)
    router_x = xor_blocks(router_full, own_ctx, n_ctx, 0)
    router_probs = jax.nn.softmax(dot(mixed, router_x, ((1,), (0,))), axis=-1)
    local = own_exp * EXP_DEV
    gates = lax.dynamic_slice_in_dim(router_probs * named_all, local, EXP_DEV, 1)
    hidden_g, d_gate_act, d_up_act, d_gates = [], [], [], []
    for e in range(EXP_DEV):
        gate = gates[:, e : e + 1]
        gate_act = dot(mixed, gate_w[e], ((1,), (0,)))
        up_act = dot(mixed, up_w[e], ((1,), (0,)))
        back = dot(pull, down_w[e], ((1,), (1,)))
        sig = jax.nn.sigmoid(gate_act)
        silu = gate_act * sig
        hidden = (silu * up_act).astype(bf16).astype(f32)
        d_gates.append(jnp.sum(hidden * back, axis=1, keepdims=True))
        hidden_g.append((gate * hidden).astype(bf16))
        d_hidden = gate * back
        d_gate_act.append((d_hidden * up_act * sig * (1.0 + gate_act * (1.0 - sig))).astype(bf16))
        d_up_act.append((d_hidden * silu).astype(bf16))

    slots = jnp.arange(experts, dtype=jnp.int32)[None, :]
    drp = sum(
        jnp.where(slots == local + e, d_gates[e] * named_all, 0.0) for e in range(EXP_DEV)
    )
    d_logits = (
        router_probs * (drp - jnp.sum(router_probs * drp, axis=-1, keepdims=True))
    ).astype(bf16)

    d_mixed_part = (
        dot(
            jnp.concatenate(d_gate_act + d_up_act, axis=1),
            jnp.concatenate([gate_w[e] for e in range(EXP_DEV)] + [up_w[e] for e in range(EXP_DEV)], axis=1),
            ((1,), (1,)),
        )
        + dot(d_logits, router_x, ((1,), (1,)))
    ).astype(bf16)
    d_mixed = lax.psum_scatter(d_mixed_part, "expert", scatter_dimension=0, tiled=True).astype(f32)
    d_mixed = xor_blocks(d_mixed, own_ctx, n_ctx, 1)
    out_part = dot(
        jnp.concatenate(hidden_g, axis=1), down_w.reshape(-1, width), ((1,), (0,))
    ).astype(bf16)
    out_own = lax.psum_scatter(out_part, "expert", scatter_dimension=0, tiled=True).astype(f32)
    result = (middle + out_own).astype(bf16)

    g_gate = jnp.stack([dot(mixed, d_gate_act[e], ((0,), (0,))).astype(bf16) for e in range(EXP_DEV)])
    g_up = jnp.stack([dot(mixed, d_up_act[e], ((0,), (0,))).astype(bf16) for e in range(EXP_DEV)])
    g_down = jnp.stack([dot(hidden_g[e], pull, ((0,), (0,))).astype(bf16) for e in range(EXP_DEV)])
    g_gate = scatter_xor(jnp.split(g_gate, n_ctx, axis=1), "context", n_ctx, 1)
    g_up = scatter_xor(jnp.split(g_up, n_ctx, axis=1), "context", n_ctx, 1)
    g_down = scatter_xor(
        jnp.split(xor_blocks(g_down, own_ctx, n_ctx, 1), n_ctx, axis=1), "context", n_ctx, 1
    )
    g_router = xor_blocks(dot(mixed, d_logits, ((0,), (0,))), own_ctx, n_ctx, 0)

    scaled = d_mixed * moe_scale
    g_moe = jnp.sum(d_mixed * middle * middle_r, axis=0)
    d_middle = (
        cotangent[0].astype(f32)
        + middle_r * scaled
        - middle * (middle_r**3 * jnp.mean(scaled * middle, axis=-1, keepdims=True))
    )
    d_branch = jnp.concatenate(gather_xor(d_middle.astype(bf16), "context", n_ctx, 0), axis=0)
    g_output = lax.psum_scatter(
        dot(attended, d_branch, ((0,), (0,))).astype(bf16), "expert", scatter_dimension=0, tiled=True
    ).astype(f32)

    d_attended = dot(d_branch, w_out, ((1,), (1,))).astype(bf16).reshape(sequence, heads, HEAD_DIM)
    probs = jnp.exp(scores_of() - log_total)
    d_probs = jnp.einsum("qhd,khd->hqk", d_attended, value_h, preferred_element_type=f32)
    d_value = jnp.einsum("hqk,qhd->khd", probs.astype(bf16), d_attended, preferred_element_type=f32)
    inner = jnp.sum(probs * d_probs, axis=-1, keepdims=True)
    d_scores = (probs * (d_probs - inner)).astype(bf16)
    d_query = jnp.einsum("hqk,khd->qhd", d_scores, key_h, preferred_element_type=f32)
    d_key = jnp.einsum("hqk,qhd->khd", d_scores, query_h, preferred_element_type=f32)
    d_query = rotate(d_query.reshape(sequence, columns) * score_scale, cosine, -sine, heads)
    d_key = rotate(d_key.reshape(sequence, columns) * score_scale, cosine, -sine, heads)
    inner_q = jnp.sum(query_scale * d_query * query_p, axis=1)
    inner_k = jnp.sum(key_scale * d_key * key_p, axis=1)
    inner_both = psum_rows(jnp.stack([inner_q, inner_k])) / width
    g_query_gain = jnp.sum(d_query * query_p * query_r, axis=0)
    g_key_gain = jnp.sum(d_key * key_p * key_r, axis=0)
    d_query_p = query_r * (query_scale * d_query) - query_p * (query_r**3 * inner_both[0][:, None])
    d_key_p = key_r * (key_scale * d_key) - key_p * (key_r**3 * inner_both[1][:, None])
    d_projected = jnp.concatenate(
        [d_query_p.astype(bf16), d_key_p.astype(bf16), d_value.reshape(sequence, columns).astype(bf16)],
        axis=1,
    )
    d_normed_part = dot(d_projected, w_qkv, ((1,), (1,)))
    g_attn = jnp.sum(d_normed_part * inputs * input_r, axis=0)
    d_normed = scatter_xor(
        jnp.split(d_normed_part.astype(bf16), n_ctx, axis=0), "context", n_ctx, 0
    )
    own_in = own_rows.astype(f32)
    own_r = inverse_rms(own_in)
    scaled_in = d_normed * attn_scale
    input_grad = (
        d_middle
        + own_r * scaled_in
        - own_in * (own_r**3 * jnp.mean(scaled_in * own_in, axis=-1, keepdims=True))
    )

    g_qkv = dot(normed, d_projected, ((0,), (0,)))
    spread = jnp.zeros((2, width), f32)
    spread = lax.dynamic_update_slice(
        spread, jnp.stack([g_query_gain, g_key_gain]), (jnp.zeros_like(own_ctx), own_ctx * columns)
    )
    g_small = jnp.concatenate([jnp.stack([g_attn, g_moe], axis=1), spread.T, g_router], axis=1)
    g_small = jnp.pad(g_small, ((0, 0), (0, EXTRA - g_small.shape[1])))
    g_packed = jnp.concatenate([g_qkv.astype(bf16), g_small.astype(bf16)], axis=1)
    g_packed = g_packed.reshape(n_ctx, n_exp, part, -1).transpose(1, 0, 2, 3).reshape(width, -1)
    g_packed = lax.psum_scatter(g_packed, "expert", scatter_dimension=0, tiled=True)
    g_packed = lax.all_to_all(
        g_packed.reshape(n_ctx, part, -1), "context", 0, 0, tiled=True
    ).astype(f32)
    g_weights = [
        g_packed[:, :, i * columns : (i + 1) * columns].transpose(1, 0, 2).reshape(part, width)
        for i in range(3)
    ]
    g_small = jnp.sum(g_packed[:, :, 3 * columns :], axis=0)
    return (
        result[None],
        input_grad[None],
        *g_weights,
        g_output,
        g_small[:, 4 : 4 + experts],
        g_small[:, 0],
        g_small[:, 2],
        g_small[:, 3],
        g_small[:, 1],
        g_gate,
        g_up,
        g_down,
    )


def solution(mesh):
    rows = P("expert", "context", None)
    split = P(("context", "expert"), None)
    line = P(("context", "expert"))
    return jax.shard_map(
        shards,
        mesh=mesh,
        in_specs=(rows, P("expert", None), rows, rows) + (split,) * 5 + (line,) * 4 + (rows,) * 3,
        out_specs=(rows, rows) + (split,) * 5 + (line,) * 4 + (rows,) * 3,
        check_vma=False,
    )
```

```python
import math

import jax
import jax.numpy as jnp
from jax import lax
from jax.experimental import pallas as pl
from jax.experimental.pallas import tpu as pltpu
from jax.sharding import PartitionSpec as P

HEADS = 16
HEAD_DIM = 128
EXP_DEV = 2
EXTRA = 128
VMEM_BYTES = 56 * 1024 * 1024

epsilon = 1e-05
rope_base = 10000.0
masked_value = -1e30
bf16 = jnp.bfloat16
f32 = jnp.float32


def dot(left, right, dims):
    return lax.dot_general(left, right, (dims, ((), ())), preferred_element_type=f32)


def cuts(extent, parts):
    unit = 16 if extent % 16 == 0 and extent // 16 >= parts else 1
    units = extent // unit
    sizes = [(units // parts + (1 if i < units % parts else 0)) * unit for i in range(parts)]
    points = [0]
    for size in sizes:
        points.append(points[-1] + size)
    return points


def swap(value, axis, count, bit):
    return lax.ppermute(value, axis, [(i, i ^ bit) for i in range(count)])


def after(value, *others):
    return lax.optimization_barrier((value, others))[0]


def gather_many(shards, axis, count):
    steps = count.bit_length() - 1
    held = [{0: shard} for shard in shards]
    came = [[] for _ in range(steps)]
    for step in range(steps):
        for index, found in enumerate(held):
            bit = 1 << ((index + step) % steps)
            for place in list(found):
                found[place ^ bit] = swap(found[place], axis, count, bit)
                came[step].append(found[place ^ bit])
    return [[found[place] for place in range(count)] for found in held], came


def scatter_many(pieces, axis, count):
    steps = count.bit_length() - 1
    held = [dict(enumerate(own)) for own in pieces]
    came = [[] for _ in range(steps)]
    for step in range(steps):
        for index, found in enumerate(held):
            bit = 1 << ((index + steps - 1 - step) % steps)
            for place in [p for p in found if p & bit]:
                new = swap(found.pop(place).astype(bf16), axis, count, bit)
                came[step].append(new)
                found[place ^ bit] = found[place ^ bit].astype(f32) + new.astype(f32)
    return [found[0] for found in held], came


def slices(value, count, dim):
    points = cuts(value.shape[dim], max(count, 1))
    return [
        lax.slice_in_dim(value, points[i], points[i + 1], axis=dim) for i in range(max(count, 1))
    ]


def gather_xor(shard, axis, count, dim):
    found, _ = gather_many(slices(shard, count.bit_length() - 1, dim), axis, count)
    return jnp.concatenate([part[k] for k in range(count) for part in found], axis=dim)


def scatter_xor(pieces, axis, count, dim):
    parts = count.bit_length() - 1
    cut = [slices(piece, parts, dim) for piece in pieces]
    sums, _ = scatter_many([[own[j] for own in cut] for j in range(parts)], axis, count)
    return jnp.concatenate(sums, axis=dim)


def xor_blocks(value, own, count, dim):
    width = value.shape[dim] // count
    return jnp.concatenate(
        [lax.dynamic_slice_in_dim(value, (own ^ k) * width, width, dim) for k in range(count)], axis=dim
    )


def cost(flops, moved, exps=0):
    return pl.CostEstimate(flops=flops, bytes_accessed=moved, transcendentals=exps)


def params(steps):
    return pltpu.CompilerParams(
        dimension_semantics=("arbitrary",) * steps, vmem_limit_bytes=VMEM_BYTES
    )


def turn(values, cosine, sine):
    return values * cosine + pltpu.roll(values, HEAD_DIM // 2, 1) * sine


def attend_kernel(
    chunk, query_p, key_p, value, stats, scale, cosine, sine, place_col, place_row,
    attended, query_out, key_out, log_total,
):
    cos, sin = cosine[...], sine[...]
    scales = scale[0]
    query = turn(query_p[...] * stats[:, 0:1] * scales[0:1], cos, sin).astype(bf16)
    keyv = turn(key_p[...] * stats[:, 1:2] * scales[1:2], cos, sin).astype(bf16)
    query_out[...] = query
    key_out[...] = keyv
    values = value[...].astype(bf16)
    for start in range(0, query_p.shape[0], chunk):
        rows = slice(start, start + chunk)
        scores = dot(query[rows], keyv, ((1,), (1,))) * HEAD_DIM ** (-0.5)
        scores = jnp.where(place_row[...] <= place_col[rows], scores, masked_value)
        peak = jnp.max(scores, axis=1, keepdims=True)
        exponent = jnp.exp(scores - peak)
        total = jnp.sum(exponent, axis=1, keepdims=True)
        weights = (exponent * (1.0 / total)).astype(bf16)
        attended[rows] = dot(weights, values, ((1,), (0,))).astype(bf16)
        log_total[0, rows] = peak + jnp.log(total)


def attend(projected, stats, scales, cosine, sine, places, heads):
    rows = projected.shape[0]
    head = lambda offset: pl.BlockSpec((rows, HEAD_DIM), lambda h: (0, offset + h))
    whole = lambda shape: pl.BlockSpec(shape, lambda h: (0,) * len(shape))
    low = jax.ShapeDtypeStruct((rows, heads * HEAD_DIM), bf16)
    return pl.pallas_call(
        lambda *refs: attend_kernel(min(256, rows), *refs),
        grid=(heads,),
        in_specs=[
            head(0), head(heads), head(2 * heads),
            whole((rows, 2)),
            pl.BlockSpec((1, 2, HEAD_DIM), lambda h: (h, 0, 0)),
            whole((rows, HEAD_DIM)), whole((rows, HEAD_DIM)),
            whole((rows, 1)), whole((1, rows)),
        ],
        out_specs=[head(0), head(0), head(0), pl.BlockSpec((1, rows, 1), lambda h: (h, 0, 0))],
        out_shape=[low, low, low, jax.ShapeDtypeStruct((heads, rows, 1), f32)],
        compiler_params=params(1),
        cost_estimate=cost(4 * heads * rows * rows * HEAD_DIM, 24 * low.size // 2, heads * rows * rows),
        name="attend",
    )(projected, projected, projected, stats, scales, cosine, sine, places[:, None], places[None, :])


def attend_back_kernel(
    chunk, query_p, key_p, value, query, keyv, d_attended, log_total, stats, scale, cosine, sine,
    place_col, place_row, d_query, d_key, d_value, inner_q, inner_k, gains,
):
    values = value[...].astype(bf16)
    keys = keyv[...]
    for start in range(0, query_p.shape[0], chunk):
        rows = slice(start, start + chunk)
        queries, pull = query[rows], d_attended[rows]
        scores = dot(queries, keys, ((1,), (1,))) * HEAD_DIM ** (-0.5)
        scores = jnp.where(place_row[...] <= place_col[rows], scores, masked_value)
        probs = jnp.exp(scores - log_total[0, rows])
        d_probs = dot(pull, values, ((1,), (1,)))
        inner = jnp.sum(probs * d_probs, axis=1, keepdims=True)
        d_scores = (probs * (d_probs - inner)).astype(bf16)
        d_query[rows] = dot(d_scores, keys, ((1,), (0,)))
        more_key = dot(d_scores, queries, ((0,), (0,)))
        more_value = dot(probs.astype(bf16), pull, ((0,), (0,)))
        if start == 0:
            d_key[...] = more_key
            sums = more_value
        else:
            d_key[...] += more_key
            sums = sums + more_value
    d_value[...] = sums.astype(bf16)
    cos, sin = cosine[...], -sine[...]
    scales = scale[0]
    for index, (grad, before, inner_out) in enumerate(
        ((d_query, query_p, inner_q), (d_key, key_p, inner_k))
    ):
        back = turn(grad[...] * HEAD_DIM ** (-0.5), cos, sin)
        grad[...] = back
        moved = back * before[...]
        inner_out[0] = jnp.sum(moved * scales[index : index + 1], axis=1, keepdims=True)
        gains[0, index : index + 1] = jnp.sum(moved * stats[:, index : index + 1], axis=0, keepdims=True)


def attend_back(projected, query, keyv, d_attended, log_total, stats, scales, cosine, sine, places, heads):
    rows = projected.shape[0]
    head = lambda offset: pl.BlockSpec((rows, HEAD_DIM), lambda h: (0, offset + h))
    whole = lambda shape: pl.BlockSpec(shape, lambda h: (0,) * len(shape))
    column = pl.BlockSpec((1, rows, 1), lambda h: (h, 0, 0))
    pair = pl.BlockSpec((1, 2, HEAD_DIM), lambda h: (h, 0, 0))
    full = (rows, heads * HEAD_DIM)
    return pl.pallas_call(
        lambda *refs: attend_back_kernel(min(256, rows), *refs),
        grid=(heads,),
        in_specs=[
            head(0), head(heads), head(2 * heads), head(0), head(0), head(0),
            column, whole((rows, 2)), pair,
            whole((rows, HEAD_DIM)), whole((rows, HEAD_DIM)),
            whole((rows, 1)), whole((1, rows)),
        ],
        out_specs=[head(0), head(0), head(0), column, column, pair],
        out_shape=[
            jax.ShapeDtypeStruct(full, f32),
            jax.ShapeDtypeStruct(full, f32),
            jax.ShapeDtypeStruct(full, bf16),
            jax.ShapeDtypeStruct((heads, rows, 1), f32),
            jax.ShapeDtypeStruct((heads, rows, 1), f32),
            jax.ShapeDtypeStruct((heads, 2, HEAD_DIM), f32),
        ],
        compiler_params=params(1),
        cost_estimate=cost(
            10 * heads * rows * rows * HEAD_DIM, 30 * rows * heads * HEAD_DIM, heads * rows * rows
        ),
        name="attend_back",
    )(
        projected, projected, projected, query, keyv, d_attended, log_total, stats, scales,
        cosine, sine, places[:, None], places[None, :],
    )


def experts_kernel(e, mixed, pull, gates, gate_w, up_w, down_w, hidden_g, d_acts, d_gates):
    gate = gates[:, e : e + 1]
    width = gate_w.shape[1]
    gate_act = dot(mixed[...], gate_w[...], ((1,), (0,)))
    up_act = dot(mixed[...], up_w[...], ((1,), (0,)))
    back = dot(pull[...], down_w[...], ((1,), (1,)))
    sig = jax.nn.sigmoid(gate_act)
    silu = gate_act * sig
    hidden = (silu * up_act).astype(bf16).astype(f32)
    d_gates[...] = jnp.sum(hidden * back, axis=1, keepdims=True)
    hidden_g[...] = (gate * hidden).astype(bf16)
    d_hidden = gate * back
    d_acts[:, :width] = (d_hidden * up_act * sig * (1.0 + gate_act * (1.0 - sig))).astype(bf16)
    d_acts[:, width:] = (d_hidden * silu).astype(bf16)


def run_experts(mixed, pull, gates, gate_w, up_w, down_w, e):
    rows, (width, hidden) = mixed.shape[0], gate_w.shape
    block = min(256, rows)
    here = lambda n: pl.BlockSpec((block, n), lambda i: (i, 0))
    whole = lambda w: pl.BlockSpec(w.shape, lambda i: (0, 0))
    return pl.pallas_call(
        lambda *refs: experts_kernel(e, *refs),
        grid=(rows // block,),
        in_specs=[
            here(width), here(width), here(gates.shape[1]), whole(gate_w), whole(up_w), whole(down_w),
        ],
        out_specs=[here(hidden), here(2 * hidden), here(1)],
        out_shape=[
            jax.ShapeDtypeStruct((rows, hidden), bf16),
            jax.ShapeDtypeStruct((rows, 2 * hidden), bf16),
            jax.ShapeDtypeStruct((rows, 1), f32),
        ],
        compiler_params=params(1),
        cost_estimate=cost(
            6 * rows * width * hidden, 2 * (2 * rows * width + 3 * width * hidden + 3 * rows * hidden), rows * hidden
        ),
        name="expert",
    )(mixed, pull, gates, gate_w, up_w, down_w)


def rows_back_kernel(count, *refs):
    d_acts, gate_w, up_w = refs[:count], refs[count : 2 * count], refs[2 * count : 3 * count]
    d_logits, router, out = refs[3 * count :]
    hidden = gate_w[0].shape[1]
    total = dot(d_logits[...], router[...], ((1,), (1,)))
    for e in range(count):
        total += dot(d_acts[e][:, :hidden], gate_w[e][...], ((1,), (1,)))
        total += dot(d_acts[e][:, hidden:], up_w[e][...], ((1,), (1,)))
    out[...] = total.astype(bf16)


def rows_back(d_acts, d_logits, gate_w, up_w, router):
    rows = d_logits.shape[0]
    count = len(d_acts)
    width, hidden = gate_w[0].shape
    block, cut = min(512, rows), min(512, width)
    weight = pl.BlockSpec((cut, hidden), lambda j, i: (j, 0))
    return pl.pallas_call(
        lambda *refs: rows_back_kernel(count, *refs),
        grid=(width // cut, rows // block),
        in_specs=[pl.BlockSpec((block, 2 * hidden), lambda j, i: (i, 0))] * count
        + [weight] * (2 * count)
        + [
            pl.BlockSpec((block, d_logits.shape[1]), lambda j, i: (i, 0)),
            pl.BlockSpec((cut, router.shape[1]), lambda j, i: (j, 0)),
        ],
        out_specs=pl.BlockSpec((block, cut), lambda j, i: (i, j)),
        out_shape=jax.ShapeDtypeStruct((rows, width), bf16),
        compiler_params=params(2),
        cost_estimate=cost(
            4 * count * rows * width * hidden, 4 * count * hidden * (4 * rows + width) + 2 * rows * width
        ),
        name="rows_back",
    )(*d_acts, *gate_w, *up_w, d_logits, router)


def inverse_rms(values):
    return lax.rsqrt(jnp.mean(values * values, axis=-1, keepdims=True) + epsilon)


def shards(
    tokens_in,
    positions,
    routes,
    cotangent,
    w_query,
    w_key,
    w_value,
    w_output,
    router,
    attn_gain,
    query_gain,
    key_gain,
    moe_gain,
    expert_gate,
    expert_up,
    expert_down,
):
    n_ctx, n_exp = lax.axis_size("context"), lax.axis_size("expert")
    own_ctx, own_exp = lax.axis_index("context"), lax.axis_index("expert")
    own_rows = tokens_in[0]
    tokens, width = own_rows.shape
    sequence = positions.shape[1]
    experts = EXP_DEV * n_exp
    heads = HEADS // n_ctx
    columns = heads * HEAD_DIM
    part = w_query.shape[0]

    def psum_rows(stats):
        stats = lax.psum(xor_blocks(stats, own_ctx, n_ctx, 1), "context")
        return xor_blocks(stats, own_ctx, n_ctx, 1)

    small = jnp.concatenate(
        [attn_gain[:, None], moe_gain[:, None], query_gain[:, None], key_gain[:, None], router], axis=1
    )
    small = jnp.pad(small, ((0, 0), (0, EXTRA - small.shape[1])))

    def packed_for(owner):
        cut = [lax.dynamic_slice_in_dim(w, owner * columns, columns, 1) for w in (w_query, w_key, w_value)]
        return jnp.concatenate(cut + [small], axis=1)

    def trade(blocks):
        return [blocks[0]] + [swap(blocks[k], "context", n_ctx, k) for k in range(1, n_ctx)]

    packed = jnp.stack(trade([packed_for(own_ctx ^ k) for k in range(n_ctx)]))
    packed = xor_blocks(packed, own_ctx, n_ctx, 0)
    packed = lax.all_gather(packed, "expert", axis=0, tiled=False)
    packed = packed.transpose(1, 0, 2, 3).reshape(width, 3 * columns + EXTRA)
    w_qkv = packed[:, : 3 * columns]
    small_full = packed[:, 3 * columns :]
    small_rows = small_full[:, :4].T.astype(f32)
    attn_scale, moe_scale = small_rows[0], small_rows[1]
    query_scale = lax.dynamic_slice_in_dim(small_rows[2], own_ctx * columns, columns)
    key_scale = lax.dynamic_slice_in_dim(small_rows[3], own_ctx * columns, columns)
    router_full = jnp.pad(small_full[:, 4 : 4 + experts], ((0, 0), (0, EXTRA - experts)))

    inputs = gather_xor(own_rows, "context", n_ctx, 0).astype(f32)
    places = xor_blocks(positions[0], own_ctx, n_ctx, 0)
    named = jnp.sum(
        (routes[0][:, :, None] == jnp.arange(experts, dtype=jnp.int32)[None, None, :]).astype(f32), axis=1
    )
    w_out = lax.all_gather(after(w_output, packed), "expert", axis=0, tiled=True)

    def fetch_expert(e, *first):
        shards = expert_gate[e], expert_up[e], expert_down[e]
        if first:
            shards = after(shards, *first)
        halves = slices(shards[2], n_ctx.bit_length() - 1, 0)
        found, came = gather_many([shards[0], shards[1], *halves], "context", n_ctx)
        return (found[0], found[1], found[2:]), came

    def whole_expert(gate_k, up_k, down_k):
        down = jnp.concatenate([half[k] for k in range(n_ctx) for half in down_k])
        return jnp.concatenate(gate_k), jnp.concatenate(up_k), xor_blocks(down, own_ctx, n_ctx, 0)

    fetched, came = fetch_expert(0)

    inputs = after(inputs, came[0])
    input_r = inverse_rms(inputs)
    normed = (inputs * input_r * attn_scale).astype(bf16)
    projected = dot(normed, w_qkv, ((1,), (0,)))
    query_p, key_p = projected[:, :columns], projected[:, columns : 2 * columns]
    squares = jnp.stack([jnp.sum(query_p * query_p, axis=1), jnp.sum(key_p * key_p, axis=1)])
    squares = psum_rows(after(squares, came[1][0:4:2]))
    pull = lax.all_gather(after(cotangent[0], squares), "expert", axis=0, tiled=True)
    r_both = lax.rsqrt(squares / width + epsilon)
    query_r, key_r = r_both[0][:, None], r_both[1][:, None]
    frequency = jnp.exp(
        jnp.arange(HEAD_DIM // 2, dtype=f32) * (-2.0 * math.log(rope_base) / HEAD_DIM)
    )
    angles = places.astype(f32)[:, None] * frequency[None, :]
    cosine, sine = jnp.cos(angles), jnp.sin(angles)
    cosine, sine = jnp.concatenate([cosine, cosine], 1), jnp.concatenate([-sine, sine], 1)
    stats = after(r_both.T, came[1][1:4:2])
    scales = jnp.stack(
        [query_scale.reshape(heads, HEAD_DIM), key_scale.reshape(heads, HEAD_DIM)], axis=1
    )
    attended, query, keyv, log_total = attend(
        projected, stats, scales, cosine, sine, places, heads
    )
    branch = dot(attended, w_out, ((1,), (0,))).astype(bf16)
    weights = [whole_expert(*after(fetched, branch))]
    branch = after(branch, fetched)
    branch_own = scatter_xor(jnp.split(branch, n_ctx, axis=0), "context", n_ctx, 0)
    fetched, came = zip(*(fetch_expert(e, branch_own) for e in range(1, EXP_DEV)))
    middle = own_rows.astype(f32) + branch_own
    middle_r = inverse_rms(middle)
    mixed_own = (middle * middle_r * moe_scale).astype(bf16)

    own_probs = jax.nn.softmax(dot(mixed_own, router_full, ((1,), (0,)))[:, :experts], axis=-1)
    probs_high = own_probs.astype(bf16)
    probs_low = (own_probs - probs_high.astype(f32)).astype(bf16)
    beside = jnp.concatenate([probs_high, probs_low, named.astype(bf16)], axis=1)
    beside = jnp.pad(beside, ((0, 0), (0, EXTRA - beside.shape[1])))
    mixed_own = jnp.concatenate([xor_blocks(mixed_own, own_ctx, n_ctx, 1), beside], axis=1)
    mixed_wide = lax.all_gather(after(mixed_own, pull), "expert", axis=0, tiled=True)
    mixed_wide = after(mixed_wide, [(more[0], more[1][:4]) for more in came])
    mixed, beside = mixed_wide[:, :width], mixed_wide[:, width:].astype(f32)
    router_x = xor_blocks(router_full, own_ctx, n_ctx, 0)
    router_probs = beside[:, :experts] + beside[:, experts : 2 * experts]
    named_all = beside[:, 2 * experts : 3 * experts]
    local = own_exp * EXP_DEV
    gates = lax.dynamic_slice_in_dim(router_probs * named_all, local, EXP_DEV, 1)
    acts = [run_experts(mixed_wide, pull, gates, *weights[0], 0)]
    for e in range(1, EXP_DEV):
        weights.append(whole_expert(*after(fetched[e - 1], acts)))
        acts.append(run_experts(after(mixed_wide, acts), pull, gates, *weights[e], e))
    hidden_g, d_acts, d_gates = zip(*acts)
    ff = weights[0][0].shape[1]

    slots = jnp.arange(experts, dtype=jnp.int32)[None, :]
    drp = sum(
        jnp.where(slots == local + e, d_gates[e] * named_all, 0.0) for e in range(EXP_DEV)
    )
    d_logits = (
        router_probs * (drp - jnp.sum(router_probs * drp, axis=-1, keepdims=True))
    ).astype(bf16)
    d_logits = jnp.pad(d_logits, ((0, 0), (0, EXTRA - experts)))

    d_mixed_part = rows_back(d_acts, d_logits, [w[0] for w in weights], [w[1] for w in weights], router_x)
    d_mixed = lax.psum_scatter(d_mixed_part, "expert", scatter_dimension=0, tiled=True).astype(f32)
    d_mixed = xor_blocks(d_mixed, own_ctx, n_ctx, 1)

    def weight_grads(e, hidden, grads):
        gate_g = dot(mixed, grads[:, :ff], ((0,), (0,))).astype(bf16)
        up_g = dot(mixed, grads[:, ff:], ((0,), (0,))).astype(bf16)
        down_g = xor_blocks(dot(hidden, pull, ((0,), (0,))).astype(bf16), own_ctx, n_ctx, 0)
        return gate_g, up_g, down_g

    def reduce_grads(gate_g, up_g, down_g):
        parts = n_ctx.bit_length() - 1
        cut = [slices(piece, parts, 0) for piece in jnp.split(down_g, n_ctx)]
        halves = [[own[j] for own in cut] for j in range(parts)]
        sums, came = scatter_many(
            [jnp.split(gate_g, n_ctx), jnp.split(up_g, n_ctx), *halves], "context", n_ctx
        )
        return (sums[0], sums[1], jnp.concatenate(sums[2:])), came

    g_first = weight_grads(0, *after((hidden_g[0], d_acts[0]), d_mixed_part))
    g_expert, came = reduce_grads(*g_first)
    g_experts = [g_expert]
    out_part = dot(after(hidden_g[0], g_first), weights[0][2], ((1,), (0,)))
    for e in range(1, EXP_DEV):
        out_part += dot(after(hidden_g[e], out_part, came[0][0:4:2]), weights[e][2], ((1,), (0,)))
    out_part = out_part.astype(bf16)
    out_own = lax.psum_scatter(out_part, "expert", scatter_dimension=0, tiled=True).astype(f32)
    d_mixed = after(d_mixed, came[0][1:4:2], out_part)
    g_router = xor_blocks(dot(mixed, d_logits, ((0,), (0,)))[:, :experts], own_ctx, n_ctx, 0)

    scaled = d_mixed * moe_scale
    g_moe = jnp.sum(d_mixed * middle * middle_r, axis=0)
    d_middle = (
        cotangent[0].astype(f32)
        + middle_r * scaled
        - middle * (middle_r**3 * jnp.mean(scaled * middle, axis=-1, keepdims=True))
    )
    d_branch = gather_xor(d_middle.astype(bf16), "context", n_ctx, 0)
    g_raw = [weight_grads(e, *after((hidden_g[e], d_acts[e]), d_middle)) for e in range(1, EXP_DEV)]
    d_branch = after(d_branch, g_raw, g_experts)
    came = []
    for raw in g_raw:
        g_expert, more = reduce_grads(*after(raw, d_branch))
        g_experts.append(g_expert)
        came.append(more)
    g_output = lax.psum_scatter(
        dot(attended, d_branch, ((0,), (0,))).astype(bf16), "expert", scatter_dimension=0, tiled=True
    ).astype(f32)

    d_attended = dot(d_branch, w_out, ((1,), (1,))).astype(bf16)
    d_query, d_key, d_value, inner_q, inner_k, g_heads = attend_back(
        projected, query, keyv, d_attended, log_total, stats, scales, cosine, sine, places, heads
    )
    result = (middle + after(out_own, d_query)).astype(bf16)
    inner_q, inner_k = jnp.sum(inner_q[:, :, 0], axis=0), jnp.sum(inner_k[:, :, 0], axis=0)
    inner_both = jnp.stack([inner_q, inner_k])
    inner_both = psum_rows(after(inner_both, [more[0][0:4:2] for more in came])) / width
    g_heads = g_heads.transpose(1, 0, 2).reshape(2, columns)
    d_query_p = query_r * (query_scale * d_query) - query_p * (query_r**3 * inner_both[0][:, None])
    d_key_p = key_r * (key_scale * d_key) - key_p * (key_r**3 * inner_both[1][:, None])
    d_projected = jnp.concatenate(
        [d_query_p.astype(bf16), d_key_p.astype(bf16), d_value], axis=1
    )
    d_projected = after(d_projected, [more[0][1:4:2] for more in came])
    d_normed_part = dot(d_projected, w_qkv, ((1,), (1,)))
    g_attn = jnp.sum(d_normed_part * inputs * input_r, axis=0)
    d_normed = after(d_normed_part.astype(bf16), [more[0] for more in came])
    d_normed = scatter_xor(jnp.split(d_normed, n_ctx, axis=0), "context", n_ctx, 0)
    own_in = own_rows.astype(f32)
    own_r = inverse_rms(own_in)
    scaled_in = d_normed * attn_scale
    input_grad = (
        d_middle
        + own_r * scaled_in
        - own_in * (own_r**3 * jnp.mean(scaled_in * own_in, axis=-1, keepdims=True))
    )

    g_qkv = dot(normed, d_projected, ((0,), (0,)))
    spread = jnp.zeros((2, width), f32)
    spread = lax.dynamic_update_slice(
        spread, g_heads, (jnp.zeros_like(own_ctx), own_ctx * columns)
    )
    g_small = jnp.concatenate([jnp.stack([g_attn, g_moe], axis=1), spread.T, g_router], axis=1)
    g_small = jnp.pad(g_small, ((0, 0), (0, EXTRA - g_small.shape[1])))
    g_packed = jnp.concatenate([g_qkv.astype(bf16), g_small.astype(bf16)], axis=1)
    g_packed = g_packed.reshape(n_ctx, n_exp, part, -1).transpose(1, 0, 2, 3).reshape(width, -1)
    g_packed = lax.psum_scatter(g_packed, "expert", scatter_dimension=0, tiled=True)
    g_packed = xor_blocks(g_packed.reshape(n_ctx, part, -1), own_ctx, n_ctx, 0)
    g_packed = jnp.stack(trade([g_packed[k] for k in range(n_ctx)])).astype(f32)
    g_packed = xor_blocks(g_packed, own_ctx, n_ctx, 0)
    g_weights = [
        g_packed[:, :, i * columns : (i + 1) * columns].transpose(1, 0, 2).reshape(part, width)
        for i in range(3)
    ]
    g_small = jnp.sum(g_packed[:, :, 3 * columns :], axis=0)
    return (
        result[None],
        input_grad[None],
        *g_weights,
        g_output,
        g_small[:, 4 : 4 + experts],
        g_small[:, 0],
        g_small[:, 2],
        g_small[:, 3],
        g_small[:, 1],
        *(jnp.stack([grads[i] for grads in g_experts]) for i in range(3)),
    )


def solution(mesh):
    rows = P("expert", "context", None)
    split = P(("context", "expert"), None)
    line = P(("context", "expert"))
    return jax.shard_map(
        shards,
        mesh=mesh,
        in_specs=(rows, P("expert", None), rows, rows) + (split,) * 5 + (line,) * 4 + (rows,) * 3,
        out_specs=(rows, rows) + (split,) * 5 + (line,) * 4 + (rows,) * 3,
        check_vma=False,
    )
```

```python
import math

import jax
import jax.numpy as jnp
from jax import lax
from jax.experimental import pallas as pl
from jax.experimental.pallas import tpu as pltpu
from jax.sharding import PartitionSpec as P

HEADS = 16
HEAD_DIM = 128
EXP_DEV = 2
EXTRA = 128
VMEM_BYTES = 56 * 1024 * 1024

epsilon = 1e-05
rope_base = 10000.0
masked_value = -1e30
bf16 = jnp.bfloat16
f32 = jnp.float32


def dot(left, right, dims):
    return lax.dot_general(left, right, (dims, ((), ())), preferred_element_type=f32)


def cuts(extent, parts):
    unit = 16 if extent % 16 == 0 and extent // 16 >= parts else 1
    units = extent // unit
    sizes = [(units // parts + (1 if i < units % parts else 0)) * unit for i in range(parts)]
    points = [0]
    for size in sizes:
        points.append(points[-1] + size)
    return points


def swap(value, axis, count, bit):
    return lax.ppermute(value, axis, [(i, i ^ bit) for i in range(count)])


def after(value, *others):
    return lax.optimization_barrier((value, others))[0]


def gather_direct(shard, axis, count):
    return [shard] + [swap(shard, axis, count, k) for k in range(1, count)]


def gather_step(state, axis, count, *first):
    steps = count.bit_length() - 1
    came = []
    for index, (arrays, found) in enumerate(state):
        bit = 1 << ((index + len(arrays) - 1) % steps)
        send = arrays[0] if len(arrays) == 1 else jnp.concatenate(arrays)
        new = swap(after(send, *first) if first else send, axis, count, bit)
        for block, place in enumerate(list(found)):
            found[place ^ bit] = (new, block)
        arrays.append(new)
        came.append(new)
    return came


def gather_start(shards):
    return [([shard], {0: (shard, 0)}) for shard in shards]


def gathered(state):
    return [
        [(*found[place], arrays[0].shape[0]) for place in range(len(found))] for arrays, found in state
    ]


def scatter_step(state, axis, count, step, *first):
    steps = count.bit_length() - 1
    sends = []
    for index, found in enumerate(state):
        bit = 1 << ((index + steps - 1 - step) % steps)
        away = [p for p in sorted(found) if p & bit]
        send = [found.pop(p).astype(bf16) for p in away]
        sends.append((bit, away, jnp.concatenate(send) if len(send) > 1 else send[0]))
    if first:
        held = after([send for _, _, send in sends], *first)
        sends = [(bit, away, send) for (bit, away, _), send in zip(sends, held)]
    came = [swap(send, axis, count, bit) for bit, _, send in sends]
    for found, (bit, away, _), new in zip(state, sends, came):
        rows = found[0].shape[0]
        for block, p in enumerate(away):
            part = lax.slice_in_dim(new, block * rows, (block + 1) * rows, axis=0)
            found[p ^ bit] = found[p ^ bit].astype(f32) + part.astype(f32)
    return came


def scatter_state(pieces):
    return [dict(enumerate(own)) for own in pieces]


def row_parts(pieces, parts):
    points = cuts(pieces[0].shape[0], parts)
    return [[piece[points[j] : points[j + 1]] for piece in pieces] for j in range(parts)]


def scatter_xor(pieces, axis, count):
    parts = count.bit_length() - 1
    state = scatter_state(row_parts(pieces, parts))
    came = ()
    for step in range(parts):
        came = scatter_step(state, axis, count, step, *came)
    return jnp.concatenate([found[0] for found in state])


def xor_blocks(value, own, count, dim):
    width = value.shape[dim] // count
    return jnp.concatenate(
        [lax.dynamic_slice_in_dim(value, (own ^ k) * width, width, dim) for k in range(count)], axis=dim
    )


def cost(flops, moved, exps=0):
    return pl.CostEstimate(flops=flops, bytes_accessed=moved, transcendentals=exps)


def params(steps):
    return pltpu.CompilerParams(
        dimension_semantics=("arbitrary",) * steps, vmem_limit_bytes=VMEM_BYTES
    )


def turn(values, cosine, sine):
    return values * cosine + pltpu.roll(values, HEAD_DIM // 2, 1) * sine


def project_kernel(columns, tokens, scale, gain, weights, projected, normed, squares):
    low = (tokens[...].astype(f32) * scale[...] * gain[...]).astype(bf16)
    normed[...] = low
    part = weights[...].reshape(low.shape[1], weights.shape[3])[:, : 3 * columns]
    new = dot(low, part, ((1,), (0,)))
    step = pl.program_id(0)

    @pl.when(step == 0)
    def _():
        projected[...] = new

    @pl.when(step > 0)
    def _():
        projected[...] += new

    @pl.when(step == pl.num_programs(0) - 1)
    def _():
        ones = jnp.ones((8, columns), bf16)
        for i in range(2):
            own = projected[:, i * columns : (i + 1) * columns]
            full = own * own
            high = full.astype(bf16)
            low = (full - high.astype(f32)).astype(bf16)
            total = dot(ones, high, ((1,), (1,))) + dot(ones, low, ((1,), (1,)))
            squares[i : i + 1] = total[0:1]


def project(tokens, scale, gain, packed, columns):
    rows, width = tokens.shape
    n_exp, n_ctx, part, wide = packed.shape
    cut = n_exp * part
    return pl.pallas_call(
        lambda *refs: project_kernel(columns, *refs),
        grid=(n_ctx,),
        in_specs=[
            pl.BlockSpec((rows, cut), lambda c: (0, c)),
            pl.BlockSpec((rows, 1), lambda c: (0, 0)),
            pl.BlockSpec((1, cut), lambda c: (0, c)),
            pl.BlockSpec((n_exp, 1, part, wide), lambda c: (0, c, 0, 0)),
        ],
        out_specs=[
            pl.BlockSpec((rows, 3 * columns), lambda c: (0, 0)),
            pl.BlockSpec((rows, cut), lambda c: (0, c)),
            pl.BlockSpec((2, rows), lambda c: (0, 0)),
        ],
        out_shape=[
            jax.ShapeDtypeStruct((rows, 3 * columns), f32),
            jax.ShapeDtypeStruct((rows, width), bf16),
            jax.ShapeDtypeStruct((2, rows), f32),
        ],
        compiler_params=params(1),
        cost_estimate=cost(6 * rows * width * columns, 4 * rows * width + 2 * packed.size + 12 * rows * columns),
        name="project",
    )(tokens, scale, gain, packed)


def side_grads_kernel(columns, normed, d_value, attended, d_branch, out):
    shape = (*out.shape[:3], columns)
    grad = dot(normed[...], d_value[...], ((0,), (0,))).astype(bf16)
    out[:, :, :, :columns] = grad.reshape(shape)
    grad = dot(attended[...], d_branch[...], ((0,), (0,))).astype(bf16)
    out[:, :, :, columns:] = grad.reshape(shape)


def side_grads(normed, d_value, attended, d_branch, n_exp, n_ctx):
    rows, width = normed.shape
    columns, cut = d_value.shape[1], width // n_ctx
    part = cut // n_exp
    here = pl.BlockSpec((rows, cut), lambda c: (0, c))
    whole = pl.BlockSpec((rows, columns), lambda c: (0, 0))
    return pl.pallas_call(
        lambda *refs: side_grads_kernel(columns, *refs),
        grid=(n_ctx,),
        in_specs=[here, whole, whole, here],
        out_specs=pl.BlockSpec((n_exp, 1, part, 2 * columns), lambda c: (0, c, 0, 0)),
        out_shape=jax.ShapeDtypeStruct((n_exp, n_ctx, part, 2 * columns), bf16),
        compiler_params=params(1),
        cost_estimate=cost(4 * rows * width * columns, 6 * rows * width),
        name="side_grads",
    )(normed, d_value, attended, d_branch)


def project_back_kernel(columns, d_projected, weights, tokens, scale, normed, beside, d_normed, out):
    part = weights[...].reshape(normed.shape[1], weights.shape[3])[:, : 3 * columns]
    grad = dot(d_projected[...], part, ((1,), (1,)))
    d_normed[...] = grad.astype(bf16)
    moved = (grad * tokens[...].astype(f32) * scale[...]).astype(bf16)
    gain = dot(moved, jnp.ones((moved.shape[0], EXTRA), bf16), ((0,), (0,)))
    small = jnp.where(lax.broadcasted_iota(jnp.int32, gain.shape, 1) == 0, gain, beside[...])
    grads = dot(normed[...], d_projected[:, : 2 * columns], ((0,), (0,)))
    shape = out.shape[:3]
    out[:, :, :, : 2 * columns] = grads.astype(bf16).reshape(*shape, 2 * columns)
    out[:, :, :, 2 * columns :] = small.astype(bf16).reshape(*shape, EXTRA)


def project_back(d_projected, packed, tokens, scale, normed, beside):
    rows, width = normed.shape
    n_exp, n_ctx, part, wide = packed.shape
    columns, cut = d_projected.shape[1] // 3, n_exp * part
    here = pl.BlockSpec((rows, cut), lambda c: (0, c))
    return pl.pallas_call(
        lambda *refs: project_back_kernel(columns, *refs),
        grid=(n_ctx,),
        in_specs=[
            pl.BlockSpec((rows, 3 * columns), lambda c: (0, 0)),
            pl.BlockSpec((n_exp, 1, part, wide), lambda c: (0, c, 0, 0)),
            here,
            pl.BlockSpec((rows, 1), lambda c: (0, 0)),
            here,
            pl.BlockSpec((cut, EXTRA), lambda c: (c, 0)),
        ],
        out_specs=[
            here,
            pl.BlockSpec((n_exp, 1, part, 2 * columns + EXTRA), lambda c: (0, c, 0, 0)),
        ],
        out_shape=[
            jax.ShapeDtypeStruct((rows, width), bf16),
            jax.ShapeDtypeStruct((n_exp, n_ctx, part, 2 * columns + EXTRA), bf16),
        ],
        compiler_params=params(1),
        cost_estimate=cost(10 * rows * width * columns, 8 * rows * width + 4 * packed.size),
        name="project_back",
    )(d_projected, packed, tokens, scale, normed, beside)


def attend_kernel(
    chunk, query_p, key_p, value, stats, scale, cosine, sine, place_col, place_row,
    attended, query_out, key_out, log_total,
):
    cos, sin = cosine[...], sine[...]
    scales = scale[0]
    query = turn(query_p[...] * stats[:, 0:1] * scales[0:1], cos, sin).astype(bf16)
    keyv = turn(key_p[...] * stats[:, 1:2] * scales[1:2], cos, sin).astype(bf16)
    query_out[...] = query
    key_out[...] = keyv
    values = value[...].astype(bf16)
    for start in range(0, query_p.shape[0], chunk):
        rows = slice(start, start + chunk)
        scores = dot(query[rows], keyv, ((1,), (1,))) * HEAD_DIM ** (-0.5)
        scores = jnp.where(place_row[...] <= place_col[rows], scores, masked_value)
        peak = jnp.max(scores, axis=1, keepdims=True)
        exponent = jnp.exp(scores - peak)
        total = jnp.sum(exponent, axis=1, keepdims=True)
        weights = (exponent * (1.0 / total)).astype(bf16)
        attended[rows] = dot(weights, values, ((1,), (0,))).astype(bf16)
        log_total[0, rows] = peak + jnp.log(total)


def attend(projected, stats, scales, cosine, sine, places, heads):
    rows = projected.shape[0]
    head = lambda offset: pl.BlockSpec((rows, HEAD_DIM), lambda h: (0, offset + h))
    whole = lambda shape: pl.BlockSpec(shape, lambda h: (0,) * len(shape))
    low = jax.ShapeDtypeStruct((rows, heads * HEAD_DIM), bf16)
    return pl.pallas_call(
        lambda *refs: attend_kernel(min(256, rows), *refs),
        grid=(heads,),
        in_specs=[
            head(0), head(heads), head(2 * heads),
            whole((rows, 2)),
            pl.BlockSpec((1, 2, HEAD_DIM), lambda h: (h, 0, 0)),
            whole((rows, HEAD_DIM)), whole((rows, HEAD_DIM)),
            whole((rows, 1)), whole((1, rows)),
        ],
        out_specs=[head(0), head(0), head(0), pl.BlockSpec((1, rows, 1), lambda h: (h, 0, 0))],
        out_shape=[low, low, low, jax.ShapeDtypeStruct((heads, rows, 1), f32)],
        compiler_params=params(1),
        cost_estimate=cost(4 * heads * rows * rows * HEAD_DIM, 24 * low.size // 2, heads * rows * rows),
        name="attend",
    )(projected, projected, projected, stats, scales, cosine, sine, places[:, None], places[None, :])


def attend_back_kernel(
    chunk, query_p, key_p, value, query, keyv, d_attended, log_total, stats, scale, cosine, sine,
    place_col, place_row, d_query, d_key, d_value, inner_q, inner_k, gains,
):
    values = value[...].astype(bf16)
    keys = keyv[...]
    for start in range(0, query_p.shape[0], chunk):
        rows = slice(start, start + chunk)
        queries, pull = query[rows], d_attended[rows]
        scores = dot(queries, keys, ((1,), (1,))) * HEAD_DIM ** (-0.5)
        scores = jnp.where(place_row[...] <= place_col[rows], scores, masked_value)
        probs = jnp.exp(scores - log_total[0, rows])
        d_probs = dot(pull, values, ((1,), (1,)))
        inner = jnp.sum(probs * d_probs, axis=1, keepdims=True)
        d_scores = (probs * (d_probs - inner)).astype(bf16)
        d_query[rows] = dot(d_scores, keys, ((1,), (0,)))
        more_key = dot(d_scores, queries, ((0,), (0,)))
        more_value = dot(probs.astype(bf16), pull, ((0,), (0,)))
        if start == 0:
            d_key[...] = more_key
            sums = more_value
        else:
            d_key[...] += more_key
            sums = sums + more_value
    d_value[...] = sums.astype(bf16)
    cos, sin = cosine[...], -sine[...]
    scales = scale[0]
    for index, (grad, before, inner_out) in enumerate(
        ((d_query, query_p, inner_q), (d_key, key_p, inner_k))
    ):
        back = turn(grad[...] * HEAD_DIM ** (-0.5), cos, sin)
        grad[...] = back
        moved = back * before[...]
        inner_out[0] = jnp.sum(moved * scales[index : index + 1], axis=1, keepdims=True)
        gains[0, index : index + 1] = jnp.sum(moved * stats[:, index : index + 1], axis=0, keepdims=True)


def attend_back(projected, query, keyv, d_attended, log_total, stats, scales, cosine, sine, places, heads):
    rows = projected.shape[0]
    head = lambda offset: pl.BlockSpec((rows, HEAD_DIM), lambda h: (0, offset + h))
    whole = lambda shape: pl.BlockSpec(shape, lambda h: (0,) * len(shape))
    column = pl.BlockSpec((1, rows, 1), lambda h: (h, 0, 0))
    pair = pl.BlockSpec((1, 2, HEAD_DIM), lambda h: (h, 0, 0))
    full = (rows, heads * HEAD_DIM)
    return pl.pallas_call(
        lambda *refs: attend_back_kernel(min(256, rows), *refs),
        grid=(heads,),
        in_specs=[
            head(0), head(heads), head(2 * heads), head(0), head(0), head(0),
            column, whole((rows, 2)), pair,
            whole((rows, HEAD_DIM)), whole((rows, HEAD_DIM)),
            whole((rows, 1)), whole((1, rows)),
        ],
        out_specs=[head(0), head(0), head(0), column, column, pair],
        out_shape=[
            jax.ShapeDtypeStruct(full, f32),
            jax.ShapeDtypeStruct(full, f32),
            jax.ShapeDtypeStruct(full, bf16),
            jax.ShapeDtypeStruct((heads, rows, 1), f32),
            jax.ShapeDtypeStruct((heads, rows, 1), f32),
            jax.ShapeDtypeStruct((heads, 2, HEAD_DIM), f32),
        ],
        compiler_params=params(1),
        cost_estimate=cost(0, 8 * rows * HEAD_DIM),
        name="attend_back",
    )(
        projected, projected, projected, query, keyv, d_attended, log_total, stats, scales,
        cosine, sine, places[:, None], places[None, :],
    )


def block_of(place):
    array, block, rows = place
    return pl.BlockSpec((rows, array.shape[1]), lambda i: (block, 0))


def pull_down_kernel(places, own, pull, *refs):
    down_w, (out, down) = refs[:-2], refs[-2:]

    @pl.when(pl.program_id(0) == 0)
    def _():
        for (k, unit, offset), part in zip(places, down_w):
            start = pl.multiple_of((own[0] ^ k) * unit + offset, 16)
            down[pl.ds(start, part.shape[0]), :] = part[...]

    out[...] = dot(pull[...], down[...], ((1,), (1,)))


def pull_down(own, pull, down_k):
    rows, width = pull.shape
    sizes = [part[0][2] for part in down_k]
    unit = sum(sizes)
    hidden = unit * len(down_k[0])
    places = [
        (k, unit, sum(sizes[:j])) for j in range(len(down_k)) for k in range(len(down_k[0]))
    ]
    flat = [place for part in down_k for place in part]
    block = min(512, rows)
    here = lambda n: pl.BlockSpec((block, n), lambda i: (i, 0))
    return pl.pallas_call(
        lambda *refs: pull_down_kernel(places, *refs),
        grid=(rows // block,),
        in_specs=[pl.BlockSpec(memory_space=pltpu.SMEM), here(width)] + [block_of(w) for w in flat],
        out_specs=[here(hidden), pl.BlockSpec((hidden, width), lambda i: (0, 0))],
        out_shape=[
            jax.ShapeDtypeStruct((rows, hidden), f32),
            jax.ShapeDtypeStruct((hidden, width), bf16),
        ],
        compiler_params=params(1),
        cost_estimate=cost(2 * rows * width * hidden, 2 * rows * width + 4 * width * hidden + 4 * rows * hidden),
        name="pull_down",
    )(own, pull, *[w[0] for w in flat])


def experts_kernel(e, n_ctx, mixed, back, gates, *refs):
    gate_w, up_w = refs[:n_ctx], refs[n_ctx : 2 * n_ctx]
    hidden_g, d_acts, d_gates = refs[2 * n_ctx :]
    depth, width = gate_w[0].shape
    gate = gates[:, e : e + 1]
    gate_act = up_act = 0.0
    for k in range(n_ctx):
        rows = mixed[:, k * depth : (k + 1) * depth]
        gate_act += dot(rows, gate_w[k][...], ((1,), (0,)))
        up_act += dot(rows, up_w[k][...], ((1,), (0,)))
    sig = jax.nn.sigmoid(gate_act)
    silu = gate_act * sig
    hidden = (silu * up_act).astype(bf16).astype(f32)
    d_gates[...] = jnp.sum(hidden * back[...], axis=1, keepdims=True)
    hidden_g[...] = (gate * hidden).astype(bf16)
    d_hidden = gate * back[...]
    d_acts[:, :width] = (d_hidden * up_act * sig * (1.0 + gate_act * (1.0 - sig))).astype(bf16)
    d_acts[:, width:] = (d_hidden * silu).astype(bf16)


def run_experts(mixed, back, gates, gate_k, up_k, e):
    rows, wide = mixed.shape
    hidden = back.shape[1]
    width = gate_k[0][2] * len(gate_k)
    block = min(256, rows)
    here = lambda n: pl.BlockSpec((block, n), lambda i: (i, 0))
    return pl.pallas_call(
        lambda *refs: experts_kernel(e, len(gate_k), *refs),
        grid=(rows // block,),
        in_specs=[here(wide), here(hidden), here(gates.shape[1])] + [block_of(w) for w in (*gate_k, *up_k)],
        out_specs=[here(hidden), here(2 * hidden), here(1)],
        out_shape=[
            jax.ShapeDtypeStruct((rows, hidden), bf16),
            jax.ShapeDtypeStruct((rows, 2 * hidden), bf16),
            jax.ShapeDtypeStruct((rows, 1), f32),
        ],
        compiler_params=params(1),
        cost_estimate=cost(
            4 * rows * width * hidden, 2 * (rows * width + 2 * width * hidden + 5 * rows * hidden), rows * hidden
        ),
        name="expert",
    )(mixed, back, gates, *[w[0] for w in (*gate_k, *up_k)])


def combine_kernel(count, *refs):
    total = dot(refs[0][...], refs[count][...], ((1,), (0,)))
    for e in range(1, count):
        total += dot(refs[e][...], refs[count + e][...], ((1,), (0,)))
    refs[-1][...] = total.astype(bf16)


def combine(hidden_g, down_w):
    count, (rows, hidden), width = len(hidden_g), hidden_g[0].shape, down_w[0].shape[1]
    block = min(512, rows)
    return pl.pallas_call(
        lambda *refs: combine_kernel(count, *refs),
        grid=(rows // block,),
        in_specs=[pl.BlockSpec((block, hidden), lambda i: (i, 0))] * count
        + [pl.BlockSpec((hidden, width), lambda i: (0, 0))] * count,
        out_specs=pl.BlockSpec((block, width), lambda i: (i, 0)),
        out_shape=jax.ShapeDtypeStruct((rows, width), bf16),
        compiler_params=params(1),
        cost_estimate=cost(2 * count * rows * width * hidden, 2 * count * hidden * (rows + width) + 2 * rows * width),
        name="combine",
    )(*hidden_g, *down_w)


def rows_back_kernel(count, n_ctx, *refs):
    d_acts, weights = refs[:count], refs[count : count * (1 + 2 * n_ctx)]
    d_logits, router, out = refs[count * (1 + 2 * n_ctx) :]
    depth, hidden = weights[0].shape
    for k in range(n_ctx):
        here = slice(k * depth, (k + 1) * depth)
        total = dot(d_logits[...], router[here], ((1,), (1,)))
        for e in range(count):
            for half in range(2):
                part = weights[(2 * e + half) * n_ctx + k]
                total += dot(d_acts[e][:, half * hidden : (half + 1) * hidden], part[...], ((1,), (1,)))
        out[:, here] = total.astype(bf16)


def rows_back(d_acts, d_logits, weights, router):
    rows = d_logits.shape[0]
    count, n_ctx = len(d_acts), len(weights[0][0])
    flat = [part for pair in weights for parts in pair for part in parts]
    depth, hidden = flat[0][2], flat[0][0].shape[1]
    block = min(512, rows)
    here = lambda n: pl.BlockSpec((block, n), lambda i: (i, 0))
    return pl.pallas_call(
        lambda *refs: rows_back_kernel(count, n_ctx, *refs),
        grid=(rows // block,),
        in_specs=[here(2 * hidden)] * count
        + [block_of(w) for w in flat]
        + [here(d_logits.shape[1]), pl.BlockSpec(router.shape, lambda i: (0, 0))],
        out_specs=here(n_ctx * depth),
        out_shape=jax.ShapeDtypeStruct((rows, n_ctx * depth), bf16),
        compiler_params=params(1),
        cost_estimate=cost(0, 8 * rows * HEAD_DIM),
        name="rows_back",
    )(*d_acts, *[w[0] for w in flat], d_logits, router)


def inverse_rms(values):
    return lax.rsqrt(jnp.mean(values * values, axis=-1, keepdims=True) + epsilon)


def shards(
    tokens_in,
    positions,
    routes,
    cotangent,
    w_query,
    w_key,
    w_value,
    w_output,
    router,
    attn_gain,
    query_gain,
    key_gain,
    moe_gain,
    expert_gate,
    expert_up,
    expert_down,
):
    n_ctx, n_exp = lax.axis_size("context"), lax.axis_size("expert")
    own_ctx, own_exp = lax.axis_index("context"), lax.axis_index("expert")
    own_rows = tokens_in[0]
    tokens, width = own_rows.shape
    sequence = positions.shape[1]
    experts = EXP_DEV * n_exp
    heads = HEADS // n_ctx
    columns = heads * HEAD_DIM
    part = w_query.shape[0]

    def sum_rows(stats):
        total = stats
        for k in range(1, n_ctx):
            came = jnp.split(swap(stats, "context", n_ctx, k), n_ctx, axis=1)
            total += jnp.concatenate([came[j ^ k] for j in range(n_ctx)], axis=1)
        return total

    small = jnp.concatenate(
        [attn_gain[:, None], moe_gain[:, None], query_gain[:, None], key_gain[:, None], router], axis=1
    )
    small = jnp.pad(small, ((0, 0), (0, EXTRA - small.shape[1])))

    def packed_for(owner):
        cut = [lax.dynamic_slice_in_dim(w, owner * columns, columns, 1) for w in (w_query, w_key, w_value)]
        return jnp.concatenate(cut + [small], axis=1)

    def trade(blocks):
        return [blocks[0]] + [swap(blocks[k], "context", n_ctx, k) for k in range(1, n_ctx)]

    packed = jnp.stack(trade([packed_for(own_ctx ^ k) for k in range(n_ctx)]))
    packed = xor_blocks(packed, own_ctx, n_ctx, 0)
    packed = lax.all_gather(packed, "expert", axis=0, tiled=False)
    small_full = packed[:, :, :, 3 * columns :].transpose(1, 0, 2, 3).reshape(width, EXTRA)
    small_rows = small_full[:, :4].T.astype(f32)
    attn_scale, moe_scale = small_rows[0], small_rows[1]
    query_scale = lax.dynamic_slice_in_dim(small_rows[2], own_ctx * columns, columns)
    key_scale = lax.dynamic_slice_in_dim(small_rows[3], own_ctx * columns, columns)
    router_full = jnp.pad(small_full[:, 4 : 4 + experts], ((0, 0), (0, EXTRA - experts)))

    inputs = jnp.concatenate(gather_direct(own_rows, "context", n_ctx))
    places = xor_blocks(positions[0], own_ctx, n_ctx, 0)
    named = jnp.sum(
        (routes[0][:, :, None] == jnp.arange(experts, dtype=jnp.int32)[None, None, :]).astype(f32), axis=1
    )
    w_out = lax.all_gather(after(w_output, inputs), "expert", axis=0, tiled=True)

    steps = n_ctx.bit_length() - 1
    downs = []
    for e in range(EXP_DEV):
        points = cuts(expert_down.shape[1], steps)
        downs.append(
            gather_start([expert_down[e, points[j] : points[j + 1]] for j in range(steps)])
        )
    down_came = gather_step(downs[0], "context", n_ctx)

    pull = lax.all_gather(after(cotangent[0], down_came), "expert", axis=0, tiled=True)
    down_came = [gather_step(state, "context", n_ctx, down_came) for state in downs[1:]]
    input_r = inverse_rms(inputs.astype(f32))
    projected, normed, squares = project(inputs, input_r, attn_scale[None], packed, columns)
    query_p, key_p = projected[:, :columns], projected[:, columns : 2 * columns]
    squares = sum_rows(after(squares, down_came))
    r_both = lax.rsqrt(squares / width + epsilon)
    down_came = [
        gather_step(downs[0], "context", n_ctx, r_both if step == 0 else ()) for step in range(steps - 1)
    ]
    query_r, key_r = r_both[0][:, None], r_both[1][:, None]
    frequency = jnp.exp(
        jnp.arange(HEAD_DIM // 2, dtype=f32) * (-2.0 * math.log(rope_base) / HEAD_DIM)
    )
    angles = places.astype(f32)[:, None] * frequency[None, :]
    cosine, sine = jnp.cos(angles), jnp.sin(angles)
    cosine, sine = jnp.concatenate([cosine, cosine], 1), jnp.concatenate([-sine, sine], 1)
    stats = r_both.T
    scales = jnp.stack(
        [query_scale.reshape(heads, HEAD_DIM), key_scale.reshape(heads, HEAD_DIM)], axis=1
    )
    attended, query, keyv, log_total = attend(
        projected, stats, scales, cosine, sine, places, heads
    )
    branch = dot(attended, w_out, ((1,), (0,))).astype(bf16)
    branch = after(branch, down_came)
    branch_own = scatter_xor(jnp.split(branch, n_ctx), "context", n_ctx)
    middle = own_rows.astype(f32) + branch_own
    middle_r = inverse_rms(middle)
    mixed_own = (middle * middle_r * moe_scale).astype(bf16)

    own_probs = jax.nn.softmax(dot(mixed_own, router_full, ((1,), (0,)))[:, :experts], axis=-1)
    probs_high = own_probs.astype(bf16)
    probs_low = (own_probs - probs_high.astype(f32)).astype(bf16)
    beside = jnp.concatenate([probs_high, probs_low, named.astype(bf16)], axis=1)
    beside = jnp.pad(beside, ((0, 0), (0, EXTRA - beside.shape[1])))
    mixed_own = jnp.concatenate([xor_blocks(mixed_own, own_ctx, n_ctx, 1), beside], axis=1)
    mixed_wide = lax.all_gather(after(mixed_own, pull), "expert", axis=0, tiled=True)

    own = own_ctx.astype(jnp.int32)[None]
    weights, first_came = [], []
    links_free = [branch_own]
    back, down = pull_down(own, after(pull, mixed_own), gathered(downs[0]))
    for e in range(EXP_DEV):
        if e > 0:
            for _ in range(steps - 1):
                gather_step(downs[e], "context", n_ctx, *links_free)
        pair = gather_start([expert_gate[e], expert_up[e]])
        came = [gather_step(pair, "context", n_ctx, *links_free)]
        came += [gather_step(pair, "context", n_ctx) for _ in range(steps - 1)]
        weights.append(gathered(pair))
        first_came.append(came[0])
        links_free = [branch_own, came, back]
    mixed_wide = after(mixed_wide, back)
    mixed, beside = mixed_wide[:, :width], mixed_wide[:, width:].astype(f32)
    router_x = xor_blocks(router_full, own_ctx, n_ctx, 0)
    router_probs = beside[:, :experts] + beside[:, experts : 2 * experts]
    named_all = beside[:, 2 * experts : 3 * experts]
    local = own_exp * EXP_DEV
    gates = lax.dynamic_slice_in_dim(router_probs * named_all, local, EXP_DEV, 1)
    def weight_grad(left, right):
        return dot(left, right, ((0,), (0,))).astype(bf16)

    def gate_up_grads(e, *first):
        grads = after(d_acts[e], *first)
        return weight_grad(mixed, grads[:, :ff]), weight_grad(mixed, grads[:, ff:])

    def owner_rows(grad):
        rows = ff // n_ctx
        return [lax.dynamic_slice_in_dim(grad, (own_ctx ^ k) * rows, rows, 0) for k in range(n_ctx)]

    def sums_of(state):
        return [found[0] for found in state]

    ff = back.shape[1]
    backs, down_w = [back], [down]
    hidden_g, d_acts, d_gates, g_raw = [], [], [], []
    for e in range(EXP_DEV):
        rows_in = after(mixed_wide, g_raw, backs[e])
        for kept, made in zip(
            (hidden_g, d_acts, d_gates), run_experts(rows_in, backs[e], gates, *weights[e], e)
        ):
            kept.append(made)
        if e + 1 < EXP_DEV:
            g_raw.append(gate_up_grads(e, first_came[e + 1]))
            back, down = pull_down(own, after(pull, d_acts), gathered(downs[e + 1]))
            backs.append(back)
            down_w.append(down)
    pairs = [scatter_state([jnp.split(grad, n_ctx) for grad in raw]) for raw in g_raw]
    pair_came = [scatter_step(pair, "context", n_ctx, 0) for pair in pairs]

    slots = jnp.arange(experts, dtype=jnp.int32)[None, :]
    drp = sum(
        jnp.where(slots == local + e, d_gates[e] * named_all, 0.0) for e in range(EXP_DEV)
    )
    d_logits = (
        router_probs * (drp - jnp.sum(router_probs * drp, axis=-1, keepdims=True))
    ).astype(bf16)
    d_logits = jnp.pad(d_logits, ((0, 0), (0, EXTRA - experts)))

    d_mixed_part = rows_back(d_acts, d_logits, weights, router_x)
    d_mixed_part = after(d_mixed_part, pair_came)
    pair_came = [
        scatter_step(pair, "context", n_ctx, step, pair_came) for pair in pairs for step in range(1, steps)
    ]
    d_mixed = lax.psum_scatter(d_mixed_part, "expert", scatter_dimension=0, tiled=True).astype(f32)
    d_mixed = xor_blocks(d_mixed, own_ctx, n_ctx, 1)

    raw = gate_up_grads(EXP_DEV - 1, d_mixed_part)
    pairs.append(scatter_state([jnp.split(grad, n_ctx) for grad in raw]))
    last_came = scatter_step(pairs[-1], "context", n_ctx, 0, pair_came)
    out_part = combine(after(hidden_g, raw, pair_came), down_w)
    out_part = after(out_part, last_came)
    out_own = lax.psum_scatter(out_part, "expert", scatter_dimension=0, tiled=True).astype(f32)
    d_mixed = after(d_mixed, out_part)
    g_router = xor_blocks(dot(mixed, d_logits, ((0,), (0,)))[:, :experts], own_ctx, n_ctx, 0)

    scaled = d_mixed * moe_scale
    g_moe = jnp.sum(d_mixed * middle * middle_r, axis=0)
    d_middle = (
        cotangent[0].astype(f32)
        + middle_r * scaled
        - middle * (middle_r**3 * jnp.mean(scaled * middle, axis=-1, keepdims=True))
    )
    points = cuts(tokens, steps)
    d_low = d_middle.astype(bf16)
    state = gather_start([d_low[points[j] : points[j + 1]] for j in range(steps)])
    came, down_raw = (), []
    for step in range(max(steps, EXP_DEV)):
        if step < EXP_DEV:
            down_raw.append(weight_grad(after(hidden_g[step], d_middle, *came), pull))
        if step < steps:
            came = gather_step(state, "context", n_ctx)
    d_branch = jnp.concatenate(
        [
            lax.slice_in_dim(array, block * rows, (block + 1) * rows, axis=0)
            for parts in zip(*gathered(state))
            for array, block, rows in parts
        ]
    )
    d_branch = after(d_branch, down_raw)
    last_came = [
        scatter_step(pairs[-1], "context", n_ctx, step, d_branch) for step in range(1, steps)
    ]
    down_sums = scatter_state([owner_rows(grad) for grad in down_raw])
    down_came = scatter_step(down_sums, "context", n_ctx, 0, last_came)

    d_attended = dot(d_branch, w_out, ((1,), (1,))).astype(bf16)
    d_query, d_key, d_value, inner_q, inner_k, g_heads = attend_back(
        projected, query, keyv, d_attended, log_total, stats, scales, cosine, sine, places, heads
    )
    result = (middle + after(out_own, d_query)).astype(bf16)
    inner_q, inner_k = jnp.sum(inner_q[:, :, 0], axis=0), jnp.sum(inner_k[:, :, 0], axis=0)
    g_side = side_grads(normed, after(d_value, last_came), attended, d_branch, n_exp, n_ctx).reshape(width, 2 * columns)
    g_side = lax.psum_scatter(g_side, "expert", scatter_dimension=0, tiled=True)
    inner_both = jnp.stack([inner_q, inner_k])
    inner_both = sum_rows(after(inner_both, down_came)) / width
    g_heads = g_heads.transpose(1, 0, 2).reshape(2, columns)
    d_query_p = query_r * (query_scale * d_query) - query_p * (query_r**3 * inner_both[0][:, None])
    d_key_p = key_r * (key_scale * d_key) - key_p * (key_r**3 * inner_both[1][:, None])
    d_projected = jnp.concatenate(
        [d_query_p.astype(bf16), d_key_p.astype(bf16), d_value], axis=1
    )
    spread = lax.dynamic_update_slice(
        jnp.zeros((2, width), f32), g_heads, (jnp.zeros_like(own_ctx), own_ctx * columns)
    )
    beside = jnp.concatenate([jnp.zeros((width, 1), f32), g_moe[:, None], spread.T, g_router], axis=1)
    beside = jnp.pad(beside, ((0, 0), (0, EXTRA - beside.shape[1])))
    d_normed_part, g_packed = project_back(d_projected, packed, inputs, input_r, normed, beside)
    down_came = [
        scatter_step(down_sums, "context", n_ctx, step, inner_both) for step in range(1, steps)
    ]
    d_normed = scatter_xor(jnp.split(after(d_normed_part, down_came), n_ctx), "context", n_ctx)
    own_in = own_rows.astype(f32)
    own_r = inverse_rms(own_in)
    scaled_in = d_normed * attn_scale
    input_grad = (
        d_middle
        + own_r * scaled_in
        - own_in * (own_r**3 * jnp.mean(scaled_in * own_in, axis=-1, keepdims=True))
    )

    def to_owners(grads):
        grads = xor_blocks(grads.reshape(n_ctx, part, -1), own_ctx, n_ctx, 0)
        grads = jnp.stack(trade([grads[k] for k in range(n_ctx)])).astype(f32)
        return xor_blocks(grads, own_ctx, n_ctx, 0)

    def full_rows(grads):
        return grads.transpose(1, 0, 2).reshape(part, width)

    g_packed = g_packed.reshape(width, 2 * columns + EXTRA)
    g_packed = to_owners(lax.psum_scatter(g_packed, "expert", scatter_dimension=0, tiled=True))
    g_small = jnp.sum(g_packed[:, :, 2 * columns :], axis=0)
    return (
        result[None],
        input_grad[None],
        full_rows(g_packed[:, :, :columns]),
        full_rows(g_packed[:, :, columns : 2 * columns]),
        full_rows(to_owners(g_side[:, :columns])),
        full_rows(g_side[:, columns:].astype(f32).reshape(n_ctx, part, columns)),
        g_small[:, 4 : 4 + experts],
        g_small[:, 0],
        g_small[:, 2],
        g_small[:, 3],
        g_small[:, 1],
        jnp.stack([sums_of(pair)[0] for pair in pairs]),
        jnp.stack([sums_of(pair)[1] for pair in pairs]),
        jnp.stack(sums_of(down_sums)),
    )


def solution(mesh):
    rows = P("expert", "context", None)
    split = P(("context", "expert"), None)
    line = P(("context", "expert"))
    return jax.shard_map(
        shards,
        mesh=mesh,
        in_specs=(rows, P("expert", None), rows, rows) + (split,) * 5 + (line,) * 4 + (rows,) * 3,
        out_specs=(rows, rows) + (split,) * 5 + (line,) * 4 + (rows,) * 3,
        check_vma=False,
    )
```

```python
import math

import jax
import jax.numpy as jnp
from jax import lax
from jax.experimental import pallas as pl
from jax.experimental.pallas import tpu as pltpu
from jax.sharding import PartitionSpec as P

HEADS = 16
HEAD_DIM = 128
EXP_DEV = 2
EXTRA = 128
VMEM_BYTES = 56 * 1024 * 1024

epsilon = 1e-05
rope_base = 10000.0
masked_value = -1e30
bf16 = jnp.bfloat16
f32 = jnp.float32


def dot(left, right, dims):
    return lax.dot_general(left, right, (dims, ((), ())), preferred_element_type=f32)


def cuts(extent, parts):
    unit = 16 if extent % 16 == 0 and extent // 16 >= parts else 1
    units = extent // unit
    sizes = [(units // parts + (1 if i < units % parts else 0)) * unit for i in range(parts)]
    points = [0]
    for size in sizes:
        points.append(points[-1] + size)
    return points


def swap(value, axis, count, bit):
    return lax.ppermute(value, axis, [(i, i ^ bit) for i in range(count)])


def after(value, *others):
    return lax.optimization_barrier((value, others))[0]


def gather_direct(shard, axis, count):
    return [shard] + [swap(shard, axis, count, k) for k in range(1, count)]


def gather_step(state, axis, count, *first):
    steps = count.bit_length() - 1
    came = []
    for index, (arrays, found) in enumerate(state):
        bit = 1 << ((index + len(arrays) - 1) % steps)
        send = arrays[0] if len(arrays) == 1 else jnp.concatenate(arrays)
        new = swap(after(send, *first) if first else send, axis, count, bit)
        for block, place in enumerate(list(found)):
            found[place ^ bit] = (new, block)
        arrays.append(new)
        came.append(new)
    return came


def gather_start(shards):
    return [([shard], {0: (shard, 0)}) for shard in shards]


def gathered(state):
    return [
        [(*found[place], arrays[0].shape[0]) for place in range(len(found))] for arrays, found in state
    ]


def scatter_step(state, axis, count, step, *first):
    steps = count.bit_length() - 1
    sends = []
    for index, found in enumerate(state):
        bit = 1 << ((index + steps - 1 - step) % steps)
        away = [p for p in sorted(found) if p & bit]
        send = [found.pop(p).astype(bf16) for p in away]
        sends.append((bit, away, jnp.concatenate(send) if len(send) > 1 else send[0]))
    if first:
        held = after([send for _, _, send in sends], *first)
        sends = [(bit, away, send) for (bit, away, _), send in zip(sends, held)]
    came = [swap(send, axis, count, bit) for bit, _, send in sends]
    for found, (bit, away, _), new in zip(state, sends, came):
        rows = found[0].shape[0]
        for block, p in enumerate(away):
            part = lax.slice_in_dim(new, block * rows, (block + 1) * rows, axis=0)
            if step == steps - 1:
                found[p ^ bit] = (found[p ^ bit], part)
            else:
                found[p ^ bit] = found[p ^ bit].astype(f32) + part.astype(f32)
    return came


def scatter_sums(state, *first):
    last = [found[0] for found in state]
    last = after(last, *first) if first else last
    return [one.astype(f32) + other.astype(f32) for one, other in last]


def scatter_state(pieces):
    return [dict(enumerate(own)) for own in pieces]


def row_parts(pieces, parts):
    points = cuts(pieces[0].shape[0], parts)
    return [[piece[points[j] : points[j + 1]] for piece in pieces] for j in range(parts)]


def scatter_xor(pieces, axis, count):
    parts = count.bit_length() - 1
    state = scatter_state(row_parts(pieces, parts))
    came = ()
    for step in range(parts):
        came = scatter_step(state, axis, count, step, *came)
    return jnp.concatenate(scatter_sums(state))


def xor_blocks(value, own, count, dim):
    width = value.shape[dim] // count
    return jnp.concatenate(
        [lax.dynamic_slice_in_dim(value, (own ^ k) * width, width, dim) for k in range(count)], axis=dim
    )


def cost(flops, moved, exps=0):
    return pl.CostEstimate(flops=flops, bytes_accessed=moved, transcendentals=exps)


def params(steps):
    return pltpu.CompilerParams(
        dimension_semantics=("arbitrary",) * steps, vmem_limit_bytes=VMEM_BYTES
    )


def turn(values, cosine, sine):
    return values * cosine + pltpu.roll(values, HEAD_DIM // 2, 1) * sine


def project_kernel(columns, tokens, scale, gain, weights, projected, normed, squares):
    low = (tokens[...].astype(f32) * scale[...] * gain[...]).astype(bf16)
    normed[...] = low
    part = weights[...].reshape(low.shape[1], weights.shape[3])[:, : 3 * columns]
    new = dot(low, part, ((1,), (0,)))
    step = pl.program_id(0)

    @pl.when(step == 0)
    def _():
        projected[...] = new

    @pl.when(step > 0)
    def _():
        projected[...] += new

    @pl.when(step == pl.num_programs(0) - 1)
    def _():
        ones = jnp.ones((8, columns), bf16)
        for i in range(2):
            own = projected[:, i * columns : (i + 1) * columns]
            full = own * own
            high = full.astype(bf16)
            low = (full - high.astype(f32)).astype(bf16)
            total = dot(ones, high, ((1,), (1,))) + dot(ones, low, ((1,), (1,)))
            squares[i : i + 1] = total[0:1]


def project(tokens, scale, gain, packed, columns):
    rows, width = tokens.shape
    n_exp, n_ctx, part, wide = packed.shape
    cut = n_exp * part
    return pl.pallas_call(
        lambda *refs: project_kernel(columns, *refs),
        grid=(n_ctx,),
        in_specs=[
            pl.BlockSpec((rows, cut), lambda c: (0, c)),
            pl.BlockSpec((rows, 1), lambda c: (0, 0)),
            pl.BlockSpec((1, cut), lambda c: (0, c)),
            pl.BlockSpec((n_exp, 1, part, wide), lambda c: (0, c, 0, 0)),
        ],
        out_specs=[
            pl.BlockSpec((rows, 3 * columns), lambda c: (0, 0)),
            pl.BlockSpec((rows, cut), lambda c: (0, c)),
            pl.BlockSpec((2, rows), lambda c: (0, 0)),
        ],
        out_shape=[
            jax.ShapeDtypeStruct((rows, 3 * columns), f32),
            jax.ShapeDtypeStruct((rows, width), bf16),
            jax.ShapeDtypeStruct((2, rows), f32),
        ],
        compiler_params=params(1),
        cost_estimate=cost(6 * rows * width * columns, 4 * rows * width + 2 * packed.size + 12 * rows * columns),
        name="project",
    )(tokens, scale, gain, packed)


def side_grads_kernel(columns, normed, d_value, attended, d_branch, out):
    shape = (*out.shape[:3], columns)
    grad = dot(normed[...], d_value[...], ((0,), (0,))).astype(bf16)
    out[:, :, :, :columns] = grad.reshape(shape)
    grad = dot(attended[...], d_branch[...], ((0,), (0,))).astype(bf16)
    out[:, :, :, columns:] = grad.reshape(shape)


def side_grads(normed, d_value, attended, d_branch, n_exp, n_ctx):
    rows, width = normed.shape
    columns, cut = d_value.shape[1], width // n_ctx
    part = cut // n_exp
    here = pl.BlockSpec((rows, cut), lambda c: (0, c))
    whole = pl.BlockSpec((rows, columns), lambda c: (0, 0))
    return pl.pallas_call(
        lambda *refs: side_grads_kernel(columns, *refs),
        grid=(n_ctx,),
        in_specs=[here, whole, whole, here],
        out_specs=pl.BlockSpec((n_exp, 1, part, 2 * columns), lambda c: (0, c, 0, 0)),
        out_shape=jax.ShapeDtypeStruct((n_exp, n_ctx, part, 2 * columns), bf16),
        compiler_params=params(1),
        cost_estimate=cost(4 * rows * width * columns, 6 * rows * width),
        name="side_grads",
    )(normed, d_value, attended, d_branch)


def project_back_kernel(columns, d_projected, weights, tokens, scale, normed, beside, d_normed, out):
    part = weights[...].reshape(normed.shape[1], weights.shape[3])[:, : 3 * columns]
    grad = dot(d_projected[...], part, ((1,), (1,)))
    d_normed[...] = grad.astype(bf16)
    moved = (grad * tokens[...].astype(f32) * scale[...]).astype(bf16)
    gain = dot(moved, jnp.ones((moved.shape[0], EXTRA), bf16), ((0,), (0,)))
    small = jnp.where(lax.broadcasted_iota(jnp.int32, gain.shape, 1) == 0, gain, beside[...])
    grads = dot(normed[...], d_projected[:, : 2 * columns], ((0,), (0,)))
    shape = out.shape[:3]
    out[:, :, :, : 2 * columns] = grads.astype(bf16).reshape(*shape, 2 * columns)
    out[:, :, :, 2 * columns :] = small.astype(bf16).reshape(*shape, EXTRA)


def project_back(d_projected, packed, tokens, scale, normed, beside):
    rows, width = normed.shape
    n_exp, n_ctx, part, wide = packed.shape
    columns, cut = d_projected.shape[1] // 3, n_exp * part
    here = pl.BlockSpec((rows, cut), lambda c: (0, c))
    return pl.pallas_call(
        lambda *refs: project_back_kernel(columns, *refs),
        grid=(n_ctx,),
        in_specs=[
            pl.BlockSpec((rows, 3 * columns), lambda c: (0, 0)),
            pl.BlockSpec((n_exp, 1, part, wide), lambda c: (0, c, 0, 0)),
            here,
            pl.BlockSpec((rows, 1), lambda c: (0, 0)),
            here,
            pl.BlockSpec((cut, EXTRA), lambda c: (c, 0)),
        ],
        out_specs=[
            here,
            pl.BlockSpec((n_exp, 1, part, 2 * columns + EXTRA), lambda c: (0, c, 0, 0)),
        ],
        out_shape=[
            jax.ShapeDtypeStruct((rows, width), bf16),
            jax.ShapeDtypeStruct((n_exp, n_ctx, part, 2 * columns + EXTRA), bf16),
        ],
        compiler_params=params(1),
        cost_estimate=cost(0, 8 * rows * columns),
        name="project_back",
    )(d_projected, packed, tokens, scale, normed, beside)


def causal_scores(queries, keys, start):
    scores = dot(queries, keys, ((1,), (1,))) * HEAD_DIM ** (-0.5)
    row = lax.broadcasted_iota(jnp.int32, scores.shape, 0) + start
    return jnp.where(lax.broadcasted_iota(jnp.int32, scores.shape, 1) <= row, scores, masked_value)


def attend_kernel(
    chunk, query_p, key_p, value, stats, scale, cosine, sine, attended, query_out, key_out, log_total
):
    cos, sin = cosine[...], sine[...]
    scales = scale[0]
    query = turn(query_p[...] * stats[:, 0:1] * scales[0:1], cos, sin).astype(bf16)
    keyv = turn(key_p[...] * stats[:, 1:2] * scales[1:2], cos, sin).astype(bf16)
    query_out[...] = query
    key_out[...] = keyv
    values = value[...].astype(bf16)
    for start in range(0, query_p.shape[0], chunk):
        end = start + chunk
        scores = causal_scores(query[start:end], keyv[:end], start)
        peak = jnp.max(scores, axis=1, keepdims=True)
        exponent = jnp.exp(scores - peak)
        total = jnp.sum(exponent, axis=1, keepdims=True)
        weights = (exponent * (1.0 / total)).astype(bf16)
        attended[start:end] = dot(weights, values[:end], ((1,), (0,))).astype(bf16)
        log_total[0, start:end] = peak + jnp.log(total)


def attend(projected, stats, scales, cosine, sine, heads):
    rows = projected.shape[0]
    head = lambda offset: pl.BlockSpec((rows, HEAD_DIM), lambda h: (0, offset + h))
    whole = lambda shape: pl.BlockSpec(shape, lambda h: (0,) * len(shape))
    low = jax.ShapeDtypeStruct((rows, heads * HEAD_DIM), bf16)
    return pl.pallas_call(
        lambda *refs: attend_kernel(min(256, rows), *refs),
        grid=(heads,),
        in_specs=[
            head(0), head(heads), head(2 * heads),
            whole((rows, 2)),
            pl.BlockSpec((1, 2, HEAD_DIM), lambda h: (h, 0, 0)),
            whole((rows, HEAD_DIM)), whole((rows, HEAD_DIM)),
        ],
        out_specs=[head(0), head(0), head(0), pl.BlockSpec((1, rows, 1), lambda h: (h, 0, 0))],
        out_shape=[low, low, low, jax.ShapeDtypeStruct((heads, rows, 1), f32)],
        compiler_params=params(1),
        cost_estimate=cost(4 * heads * rows * rows * HEAD_DIM, 24 * low.size // 2, heads * rows * rows),
        name="attend",
    )(projected, projected, projected, stats, scales, cosine, sine)


def attend_back_kernel(
    chunk, query_p, key_p, value, query, keyv, d_attended, log_total, stats, scale, cosine, sine,
    d_query, d_key, d_value, inner_q, inner_k, gains, value_sum,
):
    values = value[...].astype(bf16)
    keys = keyv[...]
    length = query_p.shape[0]
    for start in reversed(range(0, length, chunk)):
        end = start + chunk
        queries, pull = query[start:end], d_attended[start:end]
        probs = jnp.exp(causal_scores(queries, keys[:end], start) - log_total[0, start:end])
        d_probs = dot(pull, values[:end], ((1,), (1,)))
        inner = jnp.sum(probs * d_probs, axis=1, keepdims=True)
        d_scores = (probs * (d_probs - inner)).astype(bf16)
        d_query[start:end] = dot(d_scores, keys[:end], ((1,), (0,)))
        more_key = dot(d_scores, queries, ((0,), (0,)))
        more_value = dot(probs.astype(bf16), pull, ((0,), (0,)))
        if end == length:
            d_key[...] = more_key
            value_sum[...] = more_value
        else:
            d_key[:end] += more_key
            value_sum[:end] += more_value
    d_value[...] = value_sum[...].astype(bf16)
    cos, sin = cosine[...], -sine[...]
    scales = scale[0]
    for index, (grad, before, inner_out) in enumerate(
        ((d_query, query_p, inner_q), (d_key, key_p, inner_k))
    ):
        back = turn(grad[...] * HEAD_DIM ** (-0.5), cos, sin)
        grad[...] = back
        moved = back * before[...]
        inner_out[0] = jnp.sum(moved * scales[index : index + 1], axis=1, keepdims=True)
        gains[0, index : index + 1] = jnp.sum(moved * stats[:, index : index + 1], axis=0, keepdims=True)


def attend_back(projected, query, keyv, d_attended, log_total, stats, scales, cosine, sine, heads):
    rows = projected.shape[0]
    head = lambda offset: pl.BlockSpec((rows, HEAD_DIM), lambda h: (0, offset + h))
    whole = lambda shape: pl.BlockSpec(shape, lambda h: (0,) * len(shape))
    column = pl.BlockSpec((1, rows, 1), lambda h: (h, 0, 0))
    pair = pl.BlockSpec((1, 2, HEAD_DIM), lambda h: (h, 0, 0))
    full = (rows, heads * HEAD_DIM)
    return pl.pallas_call(
        lambda *refs: attend_back_kernel(min(256, rows), *refs),
        grid=(heads,),
        in_specs=[
            head(0), head(heads), head(2 * heads), head(0), head(0), head(0),
            column, whole((rows, 2)), pair,
            whole((rows, HEAD_DIM)), whole((rows, HEAD_DIM)),
        ],
        out_specs=[head(0), head(0), head(0), column, column, pair],
        out_shape=[
            jax.ShapeDtypeStruct(full, f32),
            jax.ShapeDtypeStruct(full, f32),
            jax.ShapeDtypeStruct(full, bf16),
            jax.ShapeDtypeStruct((heads, rows, 1), f32),
            jax.ShapeDtypeStruct((heads, rows, 1), f32),
            jax.ShapeDtypeStruct((heads, 2, HEAD_DIM), f32),
        ],
        scratch_shapes=[pltpu.VMEM((rows, HEAD_DIM), f32)],
        compiler_params=params(1),
        cost_estimate=cost(0, 8 * rows * HEAD_DIM),
        name="attend_back",
    )(
        projected, projected, projected, query, keyv, d_attended, log_total, stats, scales, cosine, sine
    )


def block_of(place):
    array, block, rows = place
    return pl.BlockSpec((rows, array.shape[1]), lambda i: (block, 0))


def pull_down_kernel(places, own, pull, *refs):
    down_w, (out, down) = refs[:-2], refs[-2:]

    @pl.when(pl.program_id(0) == 0)
    def _():
        for (k, unit, offset), part in zip(places, down_w):
            start = pl.multiple_of((own[0] ^ k) * unit + offset, 16)
            down[pl.ds(start, part.shape[0]), :] = part[...]

    out[...] = dot(pull[...], down[...], ((1,), (1,)))


def pull_down(own, pull, down_k):
    rows, width = pull.shape
    sizes = [part[0][2] for part in down_k]
    unit = sum(sizes)
    hidden = unit * len(down_k[0])
    places = [
        (k, unit, sum(sizes[:j])) for j in range(len(down_k)) for k in range(len(down_k[0]))
    ]
    flat = [place for part in down_k for place in part]
    block = min(512, rows)
    here = lambda n: pl.BlockSpec((block, n), lambda i: (i, 0))
    return pl.pallas_call(
        lambda *refs: pull_down_kernel(places, *refs),
        grid=(rows // block,),
        in_specs=[pl.BlockSpec(memory_space=pltpu.SMEM), here(width)] + [block_of(w) for w in flat],
        out_specs=[here(hidden), pl.BlockSpec((hidden, width), lambda i: (0, 0))],
        out_shape=[
            jax.ShapeDtypeStruct((rows, hidden), f32),
            jax.ShapeDtypeStruct((hidden, width), bf16),
        ],
        compiler_params=params(1),
        cost_estimate=cost(2 * rows * width * hidden, 2 * rows * width + 4 * width * hidden + 4 * rows * hidden),
        name="pull_down",
    )(own, pull, *[w[0] for w in flat])


def experts_kernel(e, n_ctx, mixed, back, gates, *refs):
    gate_w, up_w = refs[:n_ctx], refs[n_ctx : 2 * n_ctx]
    hidden_g, d_acts, d_gates = refs[2 * n_ctx :]
    depth, width = gate_w[0].shape
    gate = gates[:, e : e + 1]
    gate_act = up_act = 0.0
    for k in range(n_ctx):
        rows = mixed[:, k * depth : (k + 1) * depth]
        gate_act += dot(rows, gate_w[k][...], ((1,), (0,)))
        up_act += dot(rows, up_w[k][...], ((1,), (0,)))
    sig = jax.nn.sigmoid(gate_act)
    silu = gate_act * sig
    hidden = (silu * up_act).astype(bf16).astype(f32)
    d_gates[...] = jnp.sum(hidden * back[...], axis=1, keepdims=True)
    hidden_g[...] = (gate * hidden).astype(bf16)
    d_hidden = gate * back[...]
    d_acts[:, :width] = (d_hidden * up_act * sig * (1.0 + gate_act * (1.0 - sig))).astype(bf16)
    d_acts[:, width:] = (d_hidden * silu).astype(bf16)


def run_experts(mixed, back, gates, gate_k, up_k, e):
    rows, wide = mixed.shape
    hidden = back.shape[1]
    width = gate_k[0][2] * len(gate_k)
    block = min(256, rows)
    here = lambda n: pl.BlockSpec((block, n), lambda i: (i, 0))
    return pl.pallas_call(
        lambda *refs: experts_kernel(e, len(gate_k), *refs),
        grid=(rows // block,),
        in_specs=[here(wide), here(hidden), here(gates.shape[1])] + [block_of(w) for w in (*gate_k, *up_k)],
        out_specs=[here(hidden), here(2 * hidden), here(1)],
        out_shape=[
            jax.ShapeDtypeStruct((rows, hidden), bf16),
            jax.ShapeDtypeStruct((rows, 2 * hidden), bf16),
            jax.ShapeDtypeStruct((rows, 1), f32),
        ],
        compiler_params=params(1),
        cost_estimate=cost(
            4 * rows * width * hidden, 2 * (rows * width + 2 * width * hidden + 5 * rows * hidden), rows * hidden
        ),
        name="expert",
    )(mixed, back, gates, *[w[0] for w in (*gate_k, *up_k)])


def combine_kernel(count, *refs):
    total = dot(refs[0][...], refs[count][...], ((1,), (0,)))
    for e in range(1, count):
        total += dot(refs[e][...], refs[count + e][...], ((1,), (0,)))
    refs[-1][...] = total.astype(bf16)


def combine(hidden_g, down_w):
    count, (rows, hidden), width = len(hidden_g), hidden_g[0].shape, down_w[0].shape[1]
    block = min(512, rows)
    return pl.pallas_call(
        lambda *refs: combine_kernel(count, *refs),
        grid=(rows // block,),
        in_specs=[pl.BlockSpec((block, hidden), lambda i: (i, 0))] * count
        + [pl.BlockSpec((hidden, width), lambda i: (0, 0))] * count,
        out_specs=pl.BlockSpec((block, width), lambda i: (i, 0)),
        out_shape=jax.ShapeDtypeStruct((rows, width), bf16),
        compiler_params=params(1),
        cost_estimate=cost(2 * count * rows * width * hidden, 2 * count * hidden * (rows + width) + 2 * rows * width),
        name="combine",
    )(*hidden_g, *down_w)


def rows_back_kernel(count, n_ctx, *refs):
    d_acts, weights = refs[:count], refs[count : count * (1 + 2 * n_ctx)]
    d_logits, router, out = refs[count * (1 + 2 * n_ctx) :]
    depth, hidden = weights[0].shape
    for k in range(n_ctx):
        here = slice(k * depth, (k + 1) * depth)
        total = dot(d_logits[...], router[here], ((1,), (1,)))
        for e in range(count):
            for half in range(2):
                part = weights[(2 * e + half) * n_ctx + k]
                total += dot(d_acts[e][:, half * hidden : (half + 1) * hidden], part[...], ((1,), (1,)))
        out[:, here] = total.astype(bf16)


def rows_back(d_acts, d_logits, weights, router):
    rows = d_logits.shape[0]
    count, n_ctx = len(d_acts), len(weights[0][0])
    flat = [part for pair in weights for parts in pair for part in parts]
    depth, hidden = flat[0][2], flat[0][0].shape[1]
    block = min(512, rows)
    here = lambda n: pl.BlockSpec((block, n), lambda i: (i, 0))
    return pl.pallas_call(
        lambda *refs: rows_back_kernel(count, n_ctx, *refs),
        grid=(rows // block,),
        in_specs=[here(2 * hidden)] * count
        + [block_of(w) for w in flat]
        + [here(d_logits.shape[1]), pl.BlockSpec(router.shape, lambda i: (0, 0))],
        out_specs=here(n_ctx * depth),
        out_shape=jax.ShapeDtypeStruct((rows, n_ctx * depth), bf16),
        compiler_params=params(1),
        cost_estimate=cost(0, 8 * rows * HEAD_DIM),
        name="rows_back",
    )(*d_acts, *[w[0] for w in flat], d_logits, router)


def inverse_rms(values):
    return lax.rsqrt(jnp.mean(values * values, axis=-1, keepdims=True) + epsilon)


def shards(
    tokens_in,
    positions,
    routes,
    cotangent,
    w_query,
    w_key,
    w_value,
    w_output,
    router,
    attn_gain,
    query_gain,
    key_gain,
    moe_gain,
    expert_gate,
    expert_up,
    expert_down,
):
    n_ctx, n_exp = lax.axis_size("context"), lax.axis_size("expert")
    own_ctx, own_exp = lax.axis_index("context"), lax.axis_index("expert")
    own_rows = tokens_in[0]
    tokens, width = own_rows.shape
    sequence = positions.shape[1]
    experts = EXP_DEV * n_exp
    heads = HEADS // n_ctx
    columns = heads * HEAD_DIM
    part = w_query.shape[0]

    def sum_rows(stats):
        flat = stats.reshape(-1, 128)
        return (flat + sum(swap(flat, "context", n_ctx, k) for k in range(1, n_ctx))).reshape(stats.shape)

    run = tokens // 2
    runs = positions[0].reshape(n_ctx, 2, run)[:, :, 0] // run
    runs = [
        [lax.dynamic_index_in_dim(runs[:, j], own_ctx ^ k, keepdims=False) for j in range(2)]
        for k in range(n_ctx)
    ]

    def in_sequence(pieces):
        whole = jnp.zeros((2 * n_ctx, run, width), pieces[0].dtype)
        for piece, (first, second) in zip(pieces, runs):
            whole = lax.dynamic_update_index_in_dim(whole, piece[:run], first, 0)
            whole = lax.dynamic_update_index_in_dim(whole, piece[run:], second, 0)
        return whole.reshape(sequence, width)

    def per_device(rows):
        view = rows.reshape(2 * n_ctx, run, width)
        return [
            jnp.concatenate([lax.dynamic_index_in_dim(view, at, keepdims=False) for at in pair])
            for pair in runs
        ]

    small = jnp.concatenate(
        [attn_gain[:, None], moe_gain[:, None], query_gain[:, None], key_gain[:, None], router], axis=1
    )
    small = jnp.pad(small, ((0, 0), (0, EXTRA - small.shape[1])))

    def packed_for(owner):
        cut = [lax.dynamic_slice_in_dim(w, owner * columns, columns, 1) for w in (w_query, w_key, w_value)]
        return jnp.concatenate(cut + [small], axis=1)

    def trade(blocks):
        return [blocks[0]] + [swap(blocks[k], "context", n_ctx, k) for k in range(1, n_ctx)]

    packed = jnp.stack(trade([packed_for(own_ctx ^ k) for k in range(n_ctx)]))
    packed = xor_blocks(packed, own_ctx, n_ctx, 0)
    packed = lax.all_gather(packed, "expert", axis=0, tiled=False)
    small_full = packed[:, :, :, 3 * columns :].transpose(1, 0, 2, 3).reshape(width, EXTRA)
    small_rows = small_full[:, :4].T.astype(f32)
    attn_scale, moe_scale = small_rows[0], small_rows[1]
    query_scale = lax.dynamic_slice_in_dim(small_rows[2], own_ctx * columns, columns)
    key_scale = lax.dynamic_slice_in_dim(small_rows[3], own_ctx * columns, columns)
    router_full = jnp.pad(small_full[:, 4 : 4 + experts], ((0, 0), (0, EXTRA - experts)))

    inputs = in_sequence(gather_direct(own_rows, "context", n_ctx))
    places = xor_blocks(positions[0], own_ctx, n_ctx, 0)
    named = jnp.sum(
        (routes[0][:, :, None] == jnp.arange(experts, dtype=jnp.int32)[None, None, :]).astype(f32), axis=1
    )
    w_out = lax.all_gather(after(w_output, inputs), "expert", axis=0, tiled=True)

    steps = n_ctx.bit_length() - 1
    downs = []
    for e in range(EXP_DEV):
        points = cuts(expert_down.shape[1], steps)
        downs.append(
            gather_start([expert_down[e, points[j] : points[j + 1]] for j in range(steps)])
        )
    down_came = gather_step(downs[0], "context", n_ctx)

    pull = lax.all_gather(after(cotangent[0], down_came), "expert", axis=0, tiled=True)
    down_came = [gather_step(state, "context", n_ctx, down_came) for state in downs[1:]]
    input_r = inverse_rms(inputs.astype(f32))
    projected, normed, squares = project(inputs, input_r, attn_scale[None], packed, columns)
    query_p, key_p = projected[:, :columns], projected[:, columns : 2 * columns]
    squares = sum_rows(after(squares, down_came))
    r_both = lax.rsqrt(squares / width + epsilon)
    down_came = [gather_step(downs[0], "context", n_ctx, r_both) for _ in range(steps - 1)]
    query_r, key_r = r_both[0][:, None], r_both[1][:, None]
    frequency = jnp.exp(
        jnp.arange(HEAD_DIM // 2, dtype=f32) * (-2.0 * math.log(rope_base) / HEAD_DIM)
    )
    angles = jnp.arange(sequence, dtype=f32)[:, None] * frequency[None, :]
    cosine, sine = jnp.cos(angles), jnp.sin(angles)
    cosine, sine = jnp.concatenate([cosine, cosine], 1), jnp.concatenate([-sine, sine], 1)
    stats = r_both.T
    scales = jnp.stack(
        [query_scale.reshape(heads, HEAD_DIM), key_scale.reshape(heads, HEAD_DIM)], axis=1
    )
    attended, query, keyv, log_total = attend(
        projected, stats, scales, cosine, sine, heads
    )
    branch = dot(attended, w_out, ((1,), (0,))).astype(bf16)
    branch = after(branch, down_came)
    branch_own = scatter_xor(per_device(branch), "context", n_ctx)
    middle = own_rows.astype(f32) + branch_own
    middle_r = inverse_rms(middle)
    mixed_own = (middle * middle_r * moe_scale).astype(bf16)

    own_probs = jax.nn.softmax(dot(mixed_own, router_full, ((1,), (0,)))[:, :experts], axis=-1)
    probs_high = own_probs.astype(bf16)
    probs_low = (own_probs - probs_high.astype(f32)).astype(bf16)
    beside = jnp.concatenate([probs_high, probs_low, named.astype(bf16)], axis=1)
    beside = jnp.pad(beside, ((0, 0), (0, EXTRA - beside.shape[1])))
    mixed_own = jnp.concatenate([xor_blocks(mixed_own, own_ctx, n_ctx, 1), beside], axis=1)
    mixed_wide = lax.all_gather(mixed_own, "expert", axis=0, tiled=True)

    own = own_ctx.astype(jnp.int32)[None]
    weights, first_came = [], []
    links_free = [branch_own]
    back, down = pull_down(own, after(pull, mixed_own), gathered(downs[0]))
    for e in range(EXP_DEV):
        if e > 0:
            for _ in range(steps - 1):
                gather_step(downs[e], "context", n_ctx, *links_free)
        pair = gather_start([expert_gate[e], expert_up[e]])
        came = [gather_step(pair, "context", n_ctx, *links_free)]
        came += [gather_step(pair, "context", n_ctx) for _ in range(steps - 1)]
        weights.append(gathered(pair))
        first_came.append(came[0])
        links_free = [branch_own, came, back]
    mixed_wide = after(mixed_wide, back)
    mixed, beside = mixed_wide[:, :width], mixed_wide[:, width:].astype(f32)
    router_x = xor_blocks(router_full, own_ctx, n_ctx, 0)
    router_probs = beside[:, :experts] + beside[:, experts : 2 * experts]
    named_all = beside[:, 2 * experts : 3 * experts]
    local = own_exp * EXP_DEV
    gates = lax.dynamic_slice_in_dim(router_probs * named_all, local, EXP_DEV, 1)
    def weight_grad(left, right):
        return dot(left, right, ((0,), (0,))).astype(bf16)

    def gate_up_grads(e, *first):
        grads = after(d_acts[e], *first)
        return weight_grad(mixed, grads[:, :ff]), weight_grad(mixed, grads[:, ff:])

    def owner_rows(grad):
        rows = ff // n_ctx
        return [lax.dynamic_slice_in_dim(grad, (own_ctx ^ k) * rows, rows, 0) for k in range(n_ctx)]

    def sums_of(state):
        return scatter_sums(state, last_came)

    ff = back.shape[1]
    backs, down_w = [back], [down]
    hidden_g, d_acts, d_gates, g_raw = [], [], [], []
    for e in range(EXP_DEV):
        rows_in = after(mixed_wide, g_raw, backs[e])
        for kept, made in zip(
            (hidden_g, d_acts, d_gates), run_experts(rows_in, backs[e], gates, *weights[e], e)
        ):
            kept.append(made)
        if e + 1 < EXP_DEV:
            g_raw.append(gate_up_grads(e, first_came[e + 1]))
            back, down = pull_down(own, after(pull, d_acts), gathered(downs[e + 1]))
            backs.append(back)
            down_w.append(down)
    pairs = [scatter_state([jnp.split(grad, n_ctx) for grad in raw]) for raw in g_raw]
    pair_came = [scatter_step(pair, "context", n_ctx, 0) for pair in pairs]

    slots = jnp.arange(experts, dtype=jnp.int32)[None, :]
    drp = sum(
        jnp.where(slots == local + e, d_gates[e] * named_all, 0.0) for e in range(EXP_DEV)
    )
    d_logits = (
        router_probs * (drp - jnp.sum(router_probs * drp, axis=-1, keepdims=True))
    ).astype(bf16)
    d_logits = jnp.pad(d_logits, ((0, 0), (0, EXTRA - experts)))

    d_mixed_part = rows_back(d_acts, d_logits, weights, router_x)
    d_mixed_part = after(d_mixed_part, pair_came)
    pair_came = [
        scatter_step(pair, "context", n_ctx, step, pair_came) for pair in pairs for step in range(1, steps)
    ]
    d_mixed = lax.psum_scatter(d_mixed_part, "expert", scatter_dimension=0, tiled=True).astype(f32)
    d_mixed = xor_blocks(d_mixed, own_ctx, n_ctx, 1)

    raw = gate_up_grads(EXP_DEV - 1, d_mixed_part)
    pairs.append(scatter_state([jnp.split(grad, n_ctx) for grad in raw]))
    last_came = scatter_step(pairs[-1], "context", n_ctx, 0, pair_came)
    out_part = combine(after(hidden_g, raw, pair_came), down_w)
    out_part = after(out_part, last_came)
    out_own = lax.psum_scatter(out_part, "expert", scatter_dimension=0, tiled=True).astype(f32)
    g_router = dot(mixed, d_logits, ((0,), (0,)))
    d_mixed = after(d_mixed, out_part, g_router)

    scaled = d_mixed * moe_scale
    g_moe = jnp.sum(d_mixed * middle * middle_r, axis=0)
    d_middle = (
        cotangent[0].astype(f32)
        + middle_r * scaled
        - middle * (middle_r**3 * jnp.mean(scaled * middle, axis=-1, keepdims=True))
    )
    points = cuts(tokens, steps)
    d_low = d_middle.astype(bf16)
    state = gather_start([d_low[points[j] : points[j + 1]] for j in range(steps)])
    came, down_raw = (), []
    for step in range(max(steps, EXP_DEV)):
        if step < EXP_DEV:
            down_raw.append(weight_grad(after(hidden_g[step], d_middle, *came), pull))
        if step < steps:
            came = gather_step(state, "context", n_ctx)
    parts = gathered(state)
    d_branch = in_sequence(
        [
            jnp.concatenate([array[block * rows : (block + 1) * rows] for array, block, rows in own])
            for own in zip(*parts)
        ]
    )
    d_branch = after(d_branch, down_raw)
    downs = [scatter_state(row_parts(owner_rows(grad), steps)) for grad in down_raw]
    last_came = [
        scatter_step(pairs[-1], "context", n_ctx, step, d_branch) for step in range(1, steps)
    ]

    d_attended = dot(d_branch, w_out, ((1,), (1,))).astype(bf16)
    d_query, d_key, d_value, inner_q, inner_k, g_heads = attend_back(
        projected, query, keyv, d_attended, log_total, stats, scales, cosine, sine, heads
    )
    result = (middle + after(out_own, d_query)).astype(bf16)
    inner_q, inner_k = jnp.sum(inner_q[:, :, 0], axis=0), jnp.sum(inner_k[:, :, 0], axis=0)
    inner_both = after(jnp.stack([inner_q, inner_k]), last_came)
    inner_both = sum_rows(inner_both) / width
    g_side = side_grads(normed, after(d_value, inner_both), attended, d_branch, n_exp, n_ctx)
    g_heads = g_heads.transpose(1, 0, 2).reshape(2, columns)
    d_query_p = query_r * (query_scale * d_query) - query_p * (query_r**3 * inner_both[0][:, None])
    d_key_p = key_r * (key_scale * d_key) - key_p * (key_r**3 * inner_both[1][:, None])
    d_projected = jnp.concatenate(
        [d_query_p.astype(bf16), d_key_p.astype(bf16), d_value], axis=1
    )
    spread = lax.dynamic_update_slice(
        jnp.zeros((2, width), f32), g_heads, (jnp.zeros_like(own_ctx), own_ctx * columns)
    )
    g_router = xor_blocks(g_router[:, :experts], own_ctx, n_ctx, 0)
    beside = jnp.concatenate([jnp.zeros((width, 1), f32), g_moe[:, None], spread.T, g_router], axis=1)
    beside = jnp.pad(beside, ((0, 0), (0, EXTRA - beside.shape[1])))
    g_side_sum = lax.psum_scatter(g_side.reshape(width, 2 * columns), "expert", scatter_dimension=0, tiled=True)
    down_came = [scatter_step(downs[0], "context", n_ctx, 0, inner_both)]
    d_projected = after(d_projected, g_side)
    d_normed_part, g_packed = project_back(d_projected, packed, inputs, input_r, normed, beside)
    g_packed = after(g_packed, down_came)
    d_normed = scatter_state(row_parts(per_device(d_normed_part), steps))
    last_came = scatter_step(d_normed, "context", n_ctx, 0)
    for down in downs[1:]:
        scatter_step(down, "context", n_ctx, 0, *down_came)
    for step in range(1, steps):
        scatter_step(d_normed, "context", n_ctx, step)
        for down in downs:
            scatter_step(down, "context", n_ctx, step)
    d_normed = jnp.concatenate(scatter_sums(d_normed))
    own_in = own_rows.astype(f32)
    own_r = inverse_rms(own_in)
    scaled_in = d_normed * attn_scale
    input_grad = (
        d_middle
        + own_r * scaled_in
        - own_in * (own_r**3 * jnp.mean(scaled_in * own_in, axis=-1, keepdims=True))
    )

    def to_owners(grads):
        grads = xor_blocks(grads.reshape(n_ctx, part, -1), own_ctx, n_ctx, 0)
        grads = jnp.stack(trade([grads[k] for k in range(n_ctx)])).astype(f32)
        return xor_blocks(grads, own_ctx, n_ctx, 0)

    def full_rows(grads):
        return grads.transpose(1, 0, 2).reshape(part, width)

    g_packed = g_packed.reshape(width, 2 * columns + EXTRA)
    g_packed = lax.psum_scatter(g_packed, "expert", scatter_dimension=0, tiled=True)
    g_packed = to_owners(jnp.concatenate([g_packed, g_side_sum[:, :columns]], axis=1))
    g_small = jnp.sum(g_packed[:, :, 2 * columns : 2 * columns + EXTRA], axis=0)
    return (
        result[None],
        input_grad[None],
        full_rows(g_packed[:, :, :columns]),
        full_rows(g_packed[:, :, columns : 2 * columns]),
        full_rows(g_packed[:, :, 2 * columns + EXTRA :]),
        full_rows(g_side_sum[:, columns:].astype(f32).reshape(n_ctx, part, columns)),
        g_small[:, 4 : 4 + experts],
        g_small[:, 0],
        g_small[:, 2],
        g_small[:, 3],
        g_small[:, 1],
        jnp.stack([sums_of(pair)[0] for pair in pairs]),
        jnp.stack([sums_of(pair)[1] for pair in pairs]),
        jnp.stack([jnp.concatenate(sums_of(down)) for down in downs]),
    )


def solution(mesh):
    rows = P("expert", "context", None)
    split = P(("context", "expert"), None)
    line = P(("context", "expert"))
    return jax.shard_map(
        shards,
        mesh=mesh,
        in_specs=(rows, P("expert", None), rows, rows) + (split,) * 5 + (line,) * 4 + (rows,) * 3,
        out_specs=(rows, rows) + (split,) * 5 + (line,) * 4 + (rows,) * 3,
        check_vma=False,
    )
```

```python
import math

import jax
import jax.numpy as jnp
from jax import lax
from jax.experimental import pallas as pl
from jax.experimental.pallas import tpu as pltpu
from jax.sharding import PartitionSpec as P

HEADS = 16
HEAD_DIM = 128
EXP_DEV = 2
EXTRA = 128
VMEM_BYTES = 56 * 1024 * 1024

epsilon = 1e-05
rope_base = 10000.0
masked_value = -1e30
bf16 = jnp.bfloat16
f32 = jnp.float32


def dot(left, right, dims):
    return lax.dot_general(left, right, (dims, ((), ())), preferred_element_type=f32)


def cuts(extent, parts):
    unit = 16 if extent % 16 == 0 and extent // 16 >= parts else 1
    units = extent // unit
    sizes = [(units // parts + (1 if i < units % parts else 0)) * unit for i in range(parts)]
    points = [0]
    for size in sizes:
        points.append(points[-1] + size)
    return points


def swap(value, axis, count, bit):
    return lax.ppermute(value, axis, [(i, i ^ bit) for i in range(count)])


def after(value, *others):
    return lax.optimization_barrier((value, others))[0]


def gather_step(state, axis, count, *first):
    steps = count.bit_length() - 1
    came = []
    for index, (arrays, found) in enumerate(state):
        bit = 1 << ((index + len(arrays) - 1) % steps)
        send = arrays[0] if len(arrays) == 1 else jnp.concatenate(arrays)
        new = swap(after(send, *first) if first else send, axis, count, bit)
        for block, place in enumerate(list(found)):
            found[place ^ bit] = (new, block)
        arrays.append(new)
        came.append(new)
    return came


def gather_start(shards):
    return [([shard], {0: (shard, 0)}) for shard in shards]


def gathered(state):
    return [
        [(*found[place], arrays[0].shape[0]) for place in range(len(found))] for arrays, found in state
    ]


def scatter_step(state, axis, count, step, *first):
    steps = count.bit_length() - 1
    sends = []
    for index, found in enumerate(state):
        bit = 1 << ((index + steps - 1 - step) % steps)
        away = [p for p in sorted(found) if p & bit]
        send = [found.pop(p).astype(bf16) for p in away]
        sends.append((bit, away, jnp.concatenate(send) if len(send) > 1 else send[0]))
    if first:
        held = after([send for _, _, send in sends], *first)
        sends = [(bit, away, send) for (bit, away, _), send in zip(sends, held)]
    came = [swap(send, axis, count, bit) for bit, _, send in sends]
    for found, (bit, away, _), new in zip(state, sends, came):
        rows = found[0].shape[0]
        for block, p in enumerate(away):
            part = lax.slice_in_dim(new, block * rows, (block + 1) * rows, axis=0)
            if step == steps - 1:
                found[p ^ bit] = (found[p ^ bit], part)
            else:
                found[p ^ bit] = found[p ^ bit].astype(f32) + part.astype(f32)
    return came


def scatter_sums(state, *first):
    last = [found[0] for found in state]
    last = after(last, *first) if first else last
    return [one.astype(f32) + other.astype(f32) for one, other in last]


def scatter_state(pieces):
    return [dict(enumerate(own)) for own in pieces]


def row_parts(pieces, parts):
    points = cuts(pieces[0].shape[0], parts)
    return [[piece[points[j] : points[j + 1]] for piece in pieces] for j in range(parts)]


def scatter_xor(pieces, axis, count):
    parts = count.bit_length() - 1
    state = scatter_state(row_parts(pieces, parts))
    came = ()
    for step in range(parts):
        came = scatter_step(state, axis, count, step, *came)
    return jnp.concatenate(scatter_sums(state))


def joined(state):
    return [
        jnp.concatenate([array[block * rows : (block + 1) * rows] for array, block, rows in own])
        for own in zip(*gathered(state))
    ]


def xor_blocks(value, own, count, dim):
    width = value.shape[dim] // count
    return jnp.concatenate(
        [lax.dynamic_slice_in_dim(value, (own ^ k) * width, width, dim) for k in range(count)], axis=dim
    )


def cost(flops, moved, exps=0):
    return pl.CostEstimate(flops=flops, bytes_accessed=moved, transcendentals=exps)


def params(steps):
    return pltpu.CompilerParams(
        dimension_semantics=("arbitrary",) * steps, vmem_limit_bytes=VMEM_BYTES
    )


def turn(values, cosine, sine):
    return values * cosine + pltpu.roll(values, HEAD_DIM // 2, 1) * sine


def project_kernel(columns, tokens, scale, gain, weights, projected, normed, squares):
    low = (tokens[...].astype(f32) * scale[...] * gain[...]).astype(bf16)
    normed[...] = low
    part = weights[...].reshape(low.shape[1], weights.shape[3])[:, : 3 * columns]
    new = dot(low, part, ((1,), (0,)))
    step = pl.program_id(0)

    @pl.when(step == 0)
    def _():
        projected[...] = new

    @pl.when(step > 0)
    def _():
        projected[...] += new

    @pl.when(step == pl.num_programs(0) - 1)
    def _():
        ones = jnp.ones((8, columns), bf16)
        for i in range(2):
            own = projected[:, i * columns : (i + 1) * columns]
            full = own * own
            high = full.astype(bf16)
            low = (full - high.astype(f32)).astype(bf16)
            total = dot(ones, high, ((1,), (1,))) + dot(ones, low, ((1,), (1,)))
            squares[i : i + 1] = total[0:1]


def project(tokens, scale, gain, packed, columns):
    rows, width = tokens.shape
    n_exp, n_ctx, part, wide = packed.shape
    cut = n_exp * part
    return pl.pallas_call(
        lambda *refs: project_kernel(columns, *refs),
        grid=(n_ctx,),
        in_specs=[
            pl.BlockSpec((rows, cut), lambda c: (0, c)),
            pl.BlockSpec((rows, 1), lambda c: (0, 0)),
            pl.BlockSpec((1, cut), lambda c: (0, c)),
            pl.BlockSpec((n_exp, 1, part, wide), lambda c: (0, c, 0, 0)),
        ],
        out_specs=[
            pl.BlockSpec((rows, 3 * columns), lambda c: (0, 0)),
            pl.BlockSpec((rows, cut), lambda c: (0, c)),
            pl.BlockSpec((2, rows), lambda c: (0, 0)),
        ],
        out_shape=[
            jax.ShapeDtypeStruct((rows, 3 * columns), f32),
            jax.ShapeDtypeStruct((rows, width), bf16),
            jax.ShapeDtypeStruct((2, rows), f32),
        ],
        compiler_params=params(1),
        cost_estimate=cost(6 * rows * width * columns, 4 * rows * width + 2 * packed.size + 12 * rows * columns),
        name="project",
    )(tokens, scale, gain, packed)


def side_grads_kernel(columns, normed, d_value, attended, d_branch, out):
    shape = (*out.shape[:3], columns)
    grad = dot(normed[...], d_value[...], ((0,), (0,))).astype(bf16)
    out[:, :, :, :columns] = grad.reshape(shape)
    grad = dot(attended[...], d_branch[...], ((0,), (0,))).astype(bf16)
    out[:, :, :, columns:] = grad.reshape(shape)


def side_grads(normed, d_value, attended, d_branch, n_exp, n_ctx):
    rows, width = normed.shape
    columns, cut = d_value.shape[1], width // n_ctx
    part = cut // n_exp
    here = pl.BlockSpec((rows, cut), lambda c: (0, c))
    whole = pl.BlockSpec((rows, columns), lambda c: (0, 0))
    return pl.pallas_call(
        lambda *refs: side_grads_kernel(columns, *refs),
        grid=(n_ctx,),
        in_specs=[here, whole, whole, here],
        out_specs=pl.BlockSpec((n_exp, 1, part, 2 * columns), lambda c: (0, c, 0, 0)),
        out_shape=jax.ShapeDtypeStruct((n_exp, n_ctx, part, 2 * columns), bf16),
        compiler_params=params(1),
        cost_estimate=cost(4 * rows * width * columns, 6 * rows * width),
        name="side_grads",
    )(normed, d_value, attended, d_branch)


def project_back_kernel(columns, d_projected, weights, tokens, scale, normed, beside, d_normed, out):
    part = weights[...].reshape(normed.shape[1], weights.shape[3])[:, : 3 * columns]
    grad = dot(d_projected[...], part, ((1,), (1,)))
    d_normed[...] = grad.astype(bf16)
    moved = (grad * tokens[...].astype(f32) * scale[...]).astype(bf16)
    gain = dot(moved, jnp.ones((moved.shape[0], EXTRA), bf16), ((0,), (0,)))
    small = jnp.where(lax.broadcasted_iota(jnp.int32, gain.shape, 1) == 0, gain, beside[...])
    grads = dot(normed[...], d_projected[:, : 2 * columns], ((0,), (0,)))
    shape = out.shape[:3]
    out[:, :, :, : 2 * columns] = grads.astype(bf16).reshape(*shape, 2 * columns)
    out[:, :, :, 2 * columns :] = small.astype(bf16).reshape(*shape, EXTRA)


def project_back(d_projected, packed, tokens, scale, normed, beside):
    rows, width = normed.shape
    n_exp, n_ctx, part, wide = packed.shape
    columns, cut = d_projected.shape[1] // 3, n_exp * part
    here = pl.BlockSpec((rows, cut), lambda c: (0, c))
    return pl.pallas_call(
        lambda *refs: project_back_kernel(columns, *refs),
        grid=(n_ctx,),
        in_specs=[
            pl.BlockSpec((rows, 3 * columns), lambda c: (0, 0)),
            pl.BlockSpec((n_exp, 1, part, wide), lambda c: (0, c, 0, 0)),
            here,
            pl.BlockSpec((rows, 1), lambda c: (0, 0)),
            here,
            pl.BlockSpec((cut, EXTRA), lambda c: (c, 0)),
        ],
        out_specs=[
            here,
            pl.BlockSpec((n_exp, 1, part, 2 * columns + EXTRA), lambda c: (0, c, 0, 0)),
        ],
        out_shape=[
            jax.ShapeDtypeStruct((rows, width), bf16),
            jax.ShapeDtypeStruct((n_exp, n_ctx, part, 2 * columns + EXTRA), bf16),
        ],
        compiler_params=params(1),
        cost_estimate=cost(0, 8 * rows * columns),
        name="project_back",
    )(d_projected, packed, tokens, scale, normed, beside)


def causal_scores(queries, keys, start):
    scores = dot(queries, keys, ((1,), (1,))) * HEAD_DIM ** (-0.5)
    row = lax.broadcasted_iota(jnp.int32, scores.shape, 0) + start
    return jnp.where(lax.broadcasted_iota(jnp.int32, scores.shape, 1) <= row, scores, masked_value)


def attend_kernel(
    chunk, query_p, key_p, value, stats, scale, cosine, sine, attended, query_out, key_out, log_total
):
    cos, sin = cosine[...], sine[...]
    scales = scale[0]
    query = turn(query_p[...] * stats[:, 0:1] * scales[0:1], cos, sin).astype(bf16)
    keyv = turn(key_p[...] * stats[:, 1:2] * scales[1:2], cos, sin).astype(bf16)
    query_out[...] = query
    key_out[...] = keyv
    values = value[...].astype(bf16)
    for start in range(0, query_p.shape[0], chunk):
        end = start + chunk
        scores = causal_scores(query[start:end], keyv[:end], start)
        peak = jnp.max(scores, axis=1, keepdims=True)
        exponent = jnp.exp(scores - peak)
        total = jnp.sum(exponent, axis=1, keepdims=True)
        weights = (exponent * (1.0 / total)).astype(bf16)
        attended[start:end] = dot(weights, values[:end], ((1,), (0,))).astype(bf16)
        log_total[0, start:end] = peak + jnp.log(total)


def attend(projected, stats, scales, cosine, sine, heads):
    rows = projected.shape[0]
    head = lambda offset: pl.BlockSpec((rows, HEAD_DIM), lambda h: (0, offset + h))
    whole = lambda shape: pl.BlockSpec(shape, lambda h: (0,) * len(shape))
    low = jax.ShapeDtypeStruct((rows, heads * HEAD_DIM), bf16)
    return pl.pallas_call(
        lambda *refs: attend_kernel(min(256, rows), *refs),
        grid=(heads,),
        in_specs=[
            head(0), head(heads), head(2 * heads),
            whole((rows, 2)),
            pl.BlockSpec((1, 2, HEAD_DIM), lambda h: (h, 0, 0)),
            whole((rows, HEAD_DIM)), whole((rows, HEAD_DIM)),
        ],
        out_specs=[head(0), head(0), head(0), pl.BlockSpec((1, rows, 1), lambda h: (h, 0, 0))],
        out_shape=[low, low, low, jax.ShapeDtypeStruct((heads, rows, 1), f32)],
        compiler_params=params(1),
        cost_estimate=cost(4 * heads * rows * rows * HEAD_DIM, 24 * low.size // 2, heads * rows * rows),
        name="attend",
    )(projected, projected, projected, stats, scales, cosine, sine)


def attend_back_kernel(
    chunk, query_p, key_p, value, query, keyv, d_attended, log_total, stats, scale, cosine, sine,
    d_query, d_key, d_value, inner_q, inner_k, gains, value_sum,
):
    values = value[...].astype(bf16)
    keys = keyv[...]
    length = query_p.shape[0]
    for start in reversed(range(0, length, chunk)):
        end = start + chunk
        queries, pull = query[start:end], d_attended[start:end]
        probs = jnp.exp(causal_scores(queries, keys[:end], start) - log_total[0, start:end])
        d_probs = dot(pull, values[:end], ((1,), (1,)))
        inner = jnp.sum(probs * d_probs, axis=1, keepdims=True)
        d_scores = (probs * (d_probs - inner)).astype(bf16)
        d_query[start:end] = dot(d_scores, keys[:end], ((1,), (0,)))
        more_key = dot(d_scores, queries, ((0,), (0,)))
        more_value = dot(probs.astype(bf16), pull, ((0,), (0,)))
        if end == length:
            d_key[...] = more_key
            value_sum[...] = more_value
        else:
            d_key[:end] += more_key
            value_sum[:end] += more_value
    d_value[...] = value_sum[...].astype(bf16)
    cos, sin = cosine[...], -sine[...]
    scales = scale[0]
    for index, (grad, before, inner_out) in enumerate(
        ((d_query, query_p, inner_q), (d_key, key_p, inner_k))
    ):
        back = turn(grad[...] * HEAD_DIM ** (-0.5), cos, sin)
        grad[...] = back
        moved = back * before[...]
        inner_out[0] = jnp.sum(moved * scales[index : index + 1], axis=1, keepdims=True)
        gains[0, index : index + 1] = jnp.sum(moved * stats[:, index : index + 1], axis=0, keepdims=True)


def attend_back(projected, query, keyv, d_attended, log_total, stats, scales, cosine, sine, heads):
    rows = projected.shape[0]
    head = lambda offset: pl.BlockSpec((rows, HEAD_DIM), lambda h: (0, offset + h))
    whole = lambda shape: pl.BlockSpec(shape, lambda h: (0,) * len(shape))
    column = pl.BlockSpec((1, rows, 1), lambda h: (h, 0, 0))
    pair = pl.BlockSpec((1, 2, HEAD_DIM), lambda h: (h, 0, 0))
    full = (rows, heads * HEAD_DIM)
    return pl.pallas_call(
        lambda *refs: attend_back_kernel(min(256, rows), *refs),
        grid=(heads,),
        in_specs=[
            head(0), head(heads), head(2 * heads), head(0), head(0), head(0),
            column, whole((rows, 2)), pair,
            whole((rows, HEAD_DIM)), whole((rows, HEAD_DIM)),
        ],
        out_specs=[head(0), head(0), head(0), column, column, pair],
        out_shape=[
            jax.ShapeDtypeStruct(full, f32),
            jax.ShapeDtypeStruct(full, f32),
            jax.ShapeDtypeStruct(full, bf16),
            jax.ShapeDtypeStruct((heads, rows, 1), f32),
            jax.ShapeDtypeStruct((heads, rows, 1), f32),
            jax.ShapeDtypeStruct((heads, 2, HEAD_DIM), f32),
        ],
        scratch_shapes=[pltpu.VMEM((rows, HEAD_DIM), f32)],
        compiler_params=params(1),
        cost_estimate=cost(0, 8 * rows * HEAD_DIM),
        name="attend_back",
    )(
        projected, projected, projected, query, keyv, d_attended, log_total, stats, scales, cosine, sine
    )


def block_of(place):
    array, block, rows = place
    return pl.BlockSpec((rows, array.shape[1]), lambda i: (block, 0))


def pull_down_kernel(places, own, pull, *refs):
    down_w, (out, down) = refs[:-2], refs[-2:]

    @pl.when(pl.program_id(0) == 0)
    def _():
        for (k, unit, offset), part in zip(places, down_w):
            start = pl.multiple_of((own[0] ^ k) * unit + offset, 16)
            down[pl.ds(start, part.shape[0]), :] = part[...]

    out[...] = dot(pull[...], down[...], ((1,), (1,)))


def pull_down(own, pull, down_k):
    rows, width = pull.shape
    sizes = [part[0][2] for part in down_k]
    unit = sum(sizes)
    hidden = unit * len(down_k[0])
    places = [
        (k, unit, sum(sizes[:j])) for j in range(len(down_k)) for k in range(len(down_k[0]))
    ]
    flat = [place for part in down_k for place in part]
    block = min(512, rows)
    here = lambda n: pl.BlockSpec((block, n), lambda i: (i, 0))
    return pl.pallas_call(
        lambda *refs: pull_down_kernel(places, *refs),
        grid=(rows // block,),
        in_specs=[pl.BlockSpec(memory_space=pltpu.SMEM), here(width)] + [block_of(w) for w in flat],
        out_specs=[here(hidden), pl.BlockSpec((hidden, width), lambda i: (0, 0))],
        out_shape=[
            jax.ShapeDtypeStruct((rows, hidden), f32),
            jax.ShapeDtypeStruct((hidden, width), bf16),
        ],
        compiler_params=params(1),
        cost_estimate=cost(2 * rows * width * hidden, 2 * rows * width + 4 * width * hidden + 4 * rows * hidden),
        name="pull_down",
    )(own, pull, *[w[0] for w in flat])


def experts_kernel(e, n_ctx, mixed, back, gates, *refs):
    gate_w, up_w = refs[:n_ctx], refs[n_ctx : 2 * n_ctx]
    hidden_g, d_acts, d_gates = refs[2 * n_ctx :]
    depth, width = gate_w[0].shape
    gate = gates[:, e : e + 1]
    gate_act = up_act = 0.0
    for k in range(n_ctx):
        rows = mixed[:, k * depth : (k + 1) * depth]
        gate_act += dot(rows, gate_w[k][...], ((1,), (0,)))
        up_act += dot(rows, up_w[k][...], ((1,), (0,)))
    sig = jax.nn.sigmoid(gate_act)
    silu = gate_act * sig
    hidden = (silu * up_act).astype(bf16).astype(f32)
    d_gates[...] = jnp.sum(hidden * back[...], axis=1, keepdims=True)
    hidden_g[...] = (gate * hidden).astype(bf16)
    d_hidden = gate * back[...]
    d_acts[:, :width] = (d_hidden * up_act * sig * (1.0 + gate_act * (1.0 - sig))).astype(bf16)
    d_acts[:, width:] = (d_hidden * silu).astype(bf16)


def run_experts(mixed, back, gates, gate_k, up_k, e):
    rows, wide = mixed.shape
    hidden = back.shape[1]
    width = gate_k[0][2] * len(gate_k)
    block = min(256, rows)
    here = lambda n: pl.BlockSpec((block, n), lambda i: (i, 0))
    return pl.pallas_call(
        lambda *refs: experts_kernel(e, len(gate_k), *refs),
        grid=(rows // block,),
        in_specs=[here(wide), here(hidden), here(gates.shape[1])] + [block_of(w) for w in (*gate_k, *up_k)],
        out_specs=[here(hidden), here(2 * hidden), here(1)],
        out_shape=[
            jax.ShapeDtypeStruct((rows, hidden), bf16),
            jax.ShapeDtypeStruct((rows, 2 * hidden), bf16),
            jax.ShapeDtypeStruct((rows, 1), f32),
        ],
        compiler_params=params(1),
        cost_estimate=cost(
            4 * rows * width * hidden, 2 * (rows * width + 2 * width * hidden + 5 * rows * hidden), rows * hidden
        ),
        name="expert",
    )(mixed, back, gates, *[w[0] for w in (*gate_k, *up_k)])


def combine_kernel(count, *refs):
    total = dot(refs[0][...], refs[count][...], ((1,), (0,)))
    for e in range(1, count):
        total += dot(refs[e][...], refs[count + e][...], ((1,), (0,)))
    refs[-1][...] = total.astype(bf16)


def combine(hidden_g, down_w):
    count, (rows, hidden), width = len(hidden_g), hidden_g[0].shape, down_w[0].shape[1]
    block = min(512, rows)
    return pl.pallas_call(
        lambda *refs: combine_kernel(count, *refs),
        grid=(rows // block,),
        in_specs=[pl.BlockSpec((block, hidden), lambda i: (i, 0))] * count
        + [pl.BlockSpec((hidden, width), lambda i: (0, 0))] * count,
        out_specs=pl.BlockSpec((block, width), lambda i: (i, 0)),
        out_shape=jax.ShapeDtypeStruct((rows, width), bf16),
        compiler_params=params(1),
        cost_estimate=cost(2 * count * rows * width * hidden, 2 * count * hidden * (rows + width) + 2 * rows * width),
        name="combine",
    )(*hidden_g, *down_w)


def rows_back_kernel(count, n_ctx, *refs):
    d_acts, weights = refs[:count], refs[count : count * (1 + 2 * n_ctx)]
    d_logits, router, out = refs[count * (1 + 2 * n_ctx) :]
    depth, hidden = weights[0].shape
    for k in range(n_ctx):
        here = slice(k * depth, (k + 1) * depth)
        total = dot(d_logits[...], router[here], ((1,), (1,)))
        for e in range(count):
            for half in range(2):
                part = weights[(2 * e + half) * n_ctx + k]
                total += dot(d_acts[e][:, half * hidden : (half + 1) * hidden], part[...], ((1,), (1,)))
        out[:, here] = total.astype(bf16)


def rows_back(d_acts, d_logits, weights, router):
    rows = d_logits.shape[0]
    count, n_ctx = len(d_acts), len(weights[0][0])
    flat = [part for pair in weights for parts in pair for part in parts]
    depth, hidden = flat[0][2], flat[0][0].shape[1]
    block = min(512, rows)
    here = lambda n: pl.BlockSpec((block, n), lambda i: (i, 0))
    return pl.pallas_call(
        lambda *refs: rows_back_kernel(count, n_ctx, *refs),
        grid=(rows // block,),
        in_specs=[here(2 * hidden)] * count
        + [block_of(w) for w in flat]
        + [here(d_logits.shape[1]), pl.BlockSpec(router.shape, lambda i: (0, 0))],
        out_specs=here(n_ctx * depth),
        out_shape=jax.ShapeDtypeStruct((rows, n_ctx * depth), bf16),
        compiler_params=params(1),
        cost_estimate=cost(0, 8 * rows * HEAD_DIM),
        name="rows_back",
    )(*d_acts, *[w[0] for w in flat], d_logits, router)


def inverse_rms(values):
    return lax.rsqrt(jnp.mean(values * values, axis=-1, keepdims=True) + epsilon)


def shards(
    tokens_in,
    positions,
    routes,
    cotangent,
    w_query,
    w_key,
    w_value,
    w_output,
    router,
    attn_gain,
    query_gain,
    key_gain,
    moe_gain,
    expert_gate,
    expert_up,
    expert_down,
):
    n_ctx, n_exp = lax.axis_size("context"), lax.axis_size("expert")
    own_ctx, own_exp = lax.axis_index("context"), lax.axis_index("expert")
    own_rows = tokens_in[0]
    tokens, width = own_rows.shape
    sequence = positions.shape[1]
    experts = EXP_DEV * n_exp
    heads = HEADS // n_ctx
    columns = heads * HEAD_DIM
    part = w_query.shape[0]

    def sum_rows(stats):
        flat = stats.reshape(-1, 128)
        return (flat + sum(swap(flat, "context", n_ctx, k) for k in range(1, n_ctx))).reshape(stats.shape)

    run = tokens // 2
    runs = positions[0].reshape(n_ctx, 2, run)[:, :, 0] // run
    runs = [
        [lax.dynamic_index_in_dim(runs[:, j], own_ctx ^ k, keepdims=False) for j in range(2)]
        for k in range(n_ctx)
    ]

    def in_sequence(pieces):
        whole = jnp.zeros((2 * n_ctx, run, width), pieces[0].dtype)
        for piece, (first, second) in zip(pieces, runs):
            whole = lax.dynamic_update_index_in_dim(whole, piece[:run], first, 0)
            whole = lax.dynamic_update_index_in_dim(whole, piece[run:], second, 0)
        return whole.reshape(sequence, width)

    def per_device(rows):
        view = rows.reshape(2 * n_ctx, run, width)
        return [
            jnp.concatenate([lax.dynamic_index_in_dim(view, at, keepdims=False) for at in pair])
            for pair in runs
        ]

    small = jnp.concatenate(
        [attn_gain[:, None], moe_gain[:, None], query_gain[:, None], key_gain[:, None], router], axis=1
    )
    small = jnp.pad(small, ((0, 0), (0, EXTRA - small.shape[1])))

    def packed_for(owner):
        cut = [lax.dynamic_slice_in_dim(w, owner * columns, columns, 1) for w in (w_query, w_key, w_value)]
        return jnp.concatenate(cut + [small], axis=1)

    def trade(blocks):
        return [blocks[0]] + [swap(blocks[k], "context", n_ctx, k) for k in range(1, n_ctx)]

    packed = jnp.stack(trade([packed_for(own_ctx ^ k) for k in range(n_ctx)]))
    packed = xor_blocks(packed, own_ctx, n_ctx, 0)
    packed = lax.all_gather(packed, "expert", axis=0, tiled=False)
    small_full = packed[:, :, :, 3 * columns :].transpose(1, 0, 2, 3).reshape(width, EXTRA)
    small_rows = small_full[:, :4].T.astype(f32)
    attn_scale, moe_scale = small_rows[0], small_rows[1]
    query_scale = lax.dynamic_slice_in_dim(small_rows[2], own_ctx * columns, columns)
    key_scale = lax.dynamic_slice_in_dim(small_rows[3], own_ctx * columns, columns)
    router_full = jnp.pad(small_full[:, 4 : 4 + experts], ((0, 0), (0, EXTRA - experts)))

    steps = n_ctx.bit_length() - 1
    points = cuts(tokens, steps)
    state = gather_start([own_rows[points[j] : points[j + 1]] for j in range(steps)])
    for _ in range(steps):
        gather_step(state, "context", n_ctx)
    inputs = in_sequence(joined(state))
    places = xor_blocks(positions[0], own_ctx, n_ctx, 0)
    named = jnp.sum(
        (routes[0][:, :, None] == jnp.arange(experts, dtype=jnp.int32)[None, None, :]).astype(f32), axis=1
    )
    w_out = lax.all_gather(after(w_output, inputs), "expert", axis=0, tiled=True)

    downs = []
    for e in range(EXP_DEV):
        points = cuts(expert_down.shape[1], steps)
        downs.append(
            gather_start([expert_down[e, points[j] : points[j + 1]] for j in range(steps)])
        )
    down_came = gather_step(downs[0], "context", n_ctx)

    pull = lax.all_gather(after(cotangent[0], down_came), "expert", axis=0, tiled=True)
    down_came = [gather_step(state, "context", n_ctx, down_came) for state in downs[1:]]
    down_came = [gather_step(downs[0], "context", n_ctx, down_came) for _ in range(steps - 1)]
    input_r = inverse_rms(inputs.astype(f32))
    projected, normed, squares = project(inputs, input_r, attn_scale[None], packed, columns)
    query_p, key_p = projected[:, :columns], projected[:, columns : 2 * columns]
    squares = sum_rows(after(squares, down_came))
    r_both = lax.rsqrt(squares / width + epsilon)
    down_came = [gather_step(state, "context", n_ctx, r_both) for _ in range(steps - 1) for state in downs[1:]]
    query_r, key_r = r_both[0][:, None], r_both[1][:, None]
    frequency = jnp.exp(
        jnp.arange(HEAD_DIM // 2, dtype=f32) * (-2.0 * math.log(rope_base) / HEAD_DIM)
    )
    angles = jnp.arange(sequence, dtype=f32)[:, None] * frequency[None, :]
    cosine, sine = jnp.cos(angles), jnp.sin(angles)
    cosine, sine = jnp.concatenate([cosine, cosine], 1), jnp.concatenate([-sine, sine], 1)
    stats = r_both.T
    scales = jnp.stack(
        [query_scale.reshape(heads, HEAD_DIM), key_scale.reshape(heads, HEAD_DIM)], axis=1
    )
    attended, query, keyv, log_total = attend(
        projected, stats, scales, cosine, sine, heads
    )
    branch = dot(attended, w_out, ((1,), (0,))).astype(bf16)
    branch = after(branch, down_came)
    branch_own = scatter_xor(per_device(branch), "context", n_ctx)
    middle = own_rows.astype(f32) + branch_own
    middle_r = inverse_rms(middle)
    mixed_own = (middle * middle_r * moe_scale).astype(bf16)

    own_probs = jax.nn.softmax(dot(mixed_own, router_full, ((1,), (0,)))[:, :experts], axis=-1)
    probs_high = own_probs.astype(bf16)
    probs_low = (own_probs - probs_high.astype(f32)).astype(bf16)
    beside = jnp.concatenate([probs_high, probs_low, named.astype(bf16)], axis=1)
    beside = jnp.pad(beside, ((0, 0), (0, EXTRA - beside.shape[1])))
    mixed_own = jnp.concatenate([xor_blocks(mixed_own, own_ctx, n_ctx, 1), beside], axis=1)
    mixed_wide = lax.all_gather(mixed_own, "expert", axis=0, tiled=True)

    own = own_ctx.astype(jnp.int32)[None]
    weights, first_came, backs, down_w = [], [], [], []
    for e in range(EXP_DEV):
        back, down = pull_down(own, after(pull, mixed_own, *backs), gathered(downs[e]))
        backs.append(back)
        down_w.append(down)
    links_free = [branch_own]
    for e in range(EXP_DEV):
        pair = gather_start([expert_gate[e], expert_up[e]])
        came = [gather_step(pair, "context", n_ctx, *links_free)]
        came += [gather_step(pair, "context", n_ctx) for _ in range(steps - 1)]
        weights.append(gathered(pair))
        first_came.append(came[0])
        links_free = [branch_own, came]
    mixed_wide = after(mixed_wide, backs)
    mixed, beside = mixed_wide[:, :width], mixed_wide[:, width:].astype(f32)
    router_x = xor_blocks(router_full, own_ctx, n_ctx, 0)
    router_probs = beside[:, :experts] + beside[:, experts : 2 * experts]
    named_all = beside[:, 2 * experts : 3 * experts]
    local = own_exp * EXP_DEV
    gates = lax.dynamic_slice_in_dim(router_probs * named_all, local, EXP_DEV, 1)
    def weight_grad(left, right):
        return dot(left, right, ((0,), (0,))).astype(bf16)

    def gate_up_grads(e, *first):
        grads = after(d_acts[e], *first)
        return weight_grad(mixed, grads[:, :ff]), weight_grad(mixed, grads[:, ff:])

    def owner_rows(grad):
        rows = ff // n_ctx
        return [lax.dynamic_slice_in_dim(grad, (own_ctx ^ k) * rows, rows, 0) for k in range(n_ctx)]

    def sums_of(state):
        return scatter_sums(state, last_came)

    ff = backs[0].shape[1]
    hidden_g, d_acts, d_gates, g_raw = [], [], [], []
    for e in range(EXP_DEV):
        rows_in = after(mixed_wide, g_raw, backs[e])
        for kept, made in zip(
            (hidden_g, d_acts, d_gates), run_experts(rows_in, backs[e], gates, *weights[e], e)
        ):
            kept.append(made)
        if e + 1 < EXP_DEV:
            g_raw.append(gate_up_grads(e, first_came[e + 1]))
    pairs = [scatter_state([jnp.split(grad, n_ctx) for grad in raw]) for raw in g_raw]
    pair_came = [scatter_step(pair, "context", n_ctx, 0) for pair in pairs]

    slots = jnp.arange(experts, dtype=jnp.int32)[None, :]
    drp = sum(
        jnp.where(slots == local + e, d_gates[e] * named_all, 0.0) for e in range(EXP_DEV)
    )
    d_logits = (
        router_probs * (drp - jnp.sum(router_probs * drp, axis=-1, keepdims=True))
    ).astype(bf16)
    d_logits = jnp.pad(d_logits, ((0, 0), (0, EXTRA - experts)))

    d_mixed_part = rows_back(d_acts, d_logits, weights, router_x)
    d_mixed_part = after(d_mixed_part, pair_came)
    pair_came = [
        scatter_step(pair, "context", n_ctx, step, pair_came) for pair in pairs for step in range(1, steps)
    ]
    d_mixed = lax.psum_scatter(d_mixed_part, "expert", scatter_dimension=0, tiled=True).astype(f32)
    d_mixed = xor_blocks(d_mixed, own_ctx, n_ctx, 1)

    raw = gate_up_grads(EXP_DEV - 1, d_mixed_part)
    pairs.append(scatter_state([jnp.split(grad, n_ctx) for grad in raw]))
    last_came = scatter_step(pairs[-1], "context", n_ctx, 0, pair_came)
    down_raw = [weight_grad(after(hidden_g[0], raw), pull)]
    out_part = combine(after(hidden_g, down_raw, pair_came), down_w)
    out_part = after(out_part, last_came)
    out_own = lax.psum_scatter(out_part, "expert", scatter_dimension=0, tiled=True).astype(f32)
    d_mixed = after(d_mixed, out_part)
    downs = [scatter_state(row_parts(owner_rows(down_raw[0]), steps))]
    down_came = scatter_step(downs[0], "context", n_ctx, 0, last_came)

    scaled = d_mixed * moe_scale
    g_moe = jnp.sum(d_mixed * middle * middle_r, axis=0)
    d_middle = (
        cotangent[0].astype(f32)
        + middle_r * scaled
        - middle * (middle_r**3 * jnp.mean(scaled * middle, axis=-1, keepdims=True))
    )
    points = cuts(tokens, steps)
    d_low = after(d_middle.astype(bf16), down_came)
    state = gather_start([d_low[points[j] : points[j + 1]] for j in range(steps)])
    came = d_low
    for step in range(max(steps, EXP_DEV - 1)):
        if step < steps:
            came = gather_step(state, "context", n_ctx)
        if step + 1 < EXP_DEV:
            down_raw.append(weight_grad(after(hidden_g[step + 1], came), pull))
    g_router = dot(mixed, after(d_logits, d_low, down_raw), ((0,), (0,)))
    d_branch = after(in_sequence(joined(state)), down_raw, g_router)
    downs += [scatter_state(row_parts(owner_rows(grad), steps)) for grad in down_raw[1:]]
    last_came = [
        scatter_step(pairs[-1], "context", n_ctx, step, d_branch) for step in range(1, steps)
    ]

    d_attended = dot(d_branch, w_out, ((1,), (1,))).astype(bf16)
    d_query, d_key, d_value, inner_q, inner_k, g_heads = attend_back(
        projected, query, keyv, d_attended, log_total, stats, scales, cosine, sine, heads
    )
    result = (middle + after(out_own, d_query)).astype(bf16)
    inner_q, inner_k = jnp.sum(inner_q[:, :, 0], axis=0), jnp.sum(inner_k[:, :, 0], axis=0)
    inner_both = after(jnp.stack([inner_q, inner_k]), last_came)
    inner_both = sum_rows(inner_both) / width
    g_side = side_grads(normed, after(d_value, inner_both), attended, d_branch, n_exp, n_ctx)
    g_heads = g_heads.transpose(1, 0, 2).reshape(2, columns)
    d_query_p = query_r * (query_scale * d_query) - query_p * (query_r**3 * inner_both[0][:, None])
    d_key_p = key_r * (key_scale * d_key) - key_p * (key_r**3 * inner_both[1][:, None])
    d_projected = jnp.concatenate(
        [d_query_p.astype(bf16), d_key_p.astype(bf16), d_value], axis=1
    )
    spread = lax.dynamic_update_slice(
        jnp.zeros((2, width), f32), g_heads, (jnp.zeros_like(own_ctx), own_ctx * columns)
    )
    g_router = xor_blocks(g_router[:, :experts], own_ctx, n_ctx, 0)
    beside = jnp.concatenate([jnp.zeros((width, 1), f32), g_moe[:, None], spread.T, g_router], axis=1)
    beside = jnp.pad(beside, ((0, 0), (0, EXTRA - beside.shape[1])))
    g_side_sum = lax.psum_scatter(g_side.reshape(width, 2 * columns), "expert", scatter_dimension=0, tiled=True)
    d_projected = after(d_projected, g_side)
    d_normed_part, g_packed = project_back(d_projected, packed, inputs, input_r, normed, beside)
    down_came = [scatter_step(down, "context", n_ctx, 0, inner_both) for down in downs[1:]]
    g_packed = after(g_packed, down_came)
    d_normed = scatter_state(row_parts(per_device(d_normed_part), steps))
    last_came = scatter_step(d_normed, "context", n_ctx, 0)
    for step in range(1, steps):
        scatter_step(d_normed, "context", n_ctx, step)
        for down in downs:
            scatter_step(down, "context", n_ctx, step)
    d_normed = jnp.concatenate(scatter_sums(d_normed))
    own_in = own_rows.astype(f32)
    own_r = inverse_rms(own_in)
    scaled_in = d_normed * attn_scale
    input_grad = (
        d_middle
        + own_r * scaled_in
        - own_in * (own_r**3 * jnp.mean(scaled_in * own_in, axis=-1, keepdims=True))
    )

    def to_owners(grads):
        grads = xor_blocks(grads.reshape(n_ctx, part, -1), own_ctx, n_ctx, 0)
        grads = jnp.stack(trade([grads[k] for k in range(n_ctx)])).astype(f32)
        return xor_blocks(grads, own_ctx, n_ctx, 0)

    def full_rows(grads):
        return grads.transpose(1, 0, 2).reshape(part, width)

    g_packed = g_packed.reshape(width, 2 * columns + EXTRA)
    g_packed = lax.psum_scatter(g_packed, "expert", scatter_dimension=0, tiled=True)
    g_packed = to_owners(jnp.concatenate([g_packed, g_side_sum[:, :columns]], axis=1))
    g_small = jnp.sum(g_packed[:, :, 2 * columns : 2 * columns + EXTRA], axis=0)
    return (
        result[None],
        input_grad[None],
        full_rows(g_packed[:, :, :columns]),
        full_rows(g_packed[:, :, columns : 2 * columns]),
        full_rows(g_packed[:, :, 2 * columns + EXTRA :]),
        full_rows(g_side_sum[:, columns:].astype(f32).reshape(n_ctx, part, columns)),
        g_small[:, 4 : 4 + experts],
        g_small[:, 0],
        g_small[:, 2],
        g_small[:, 3],
        g_small[:, 1],
        jnp.stack([sums_of(pair)[0] for pair in pairs]),
        jnp.stack([sums_of(pair)[1] for pair in pairs]),
        jnp.stack([jnp.concatenate(sums_of(down)) for down in downs]),
    )


def solution(mesh):
    rows = P("expert", "context", None)
    split = P(("context", "expert"), None)
    line = P(("context", "expert"))
    return jax.shard_map(
        shards,
        mesh=mesh,
        in_specs=(rows, P("expert", None), rows, rows) + (split,) * 5 + (line,) * 4 + (rows,) * 3,
        out_specs=(rows, rows) + (split,) * 5 + (line,) * 4 + (rows,) * 3,
        check_vma=False,
    )
```

```python
import math

import jax
import jax.numpy as jnp
from jax import lax
from jax.experimental import pallas as pl
from jax.experimental.pallas import tpu as pltpu
from jax.sharding import PartitionSpec as P

HEADS = 16
HEAD_DIM = 128
EXP_DEV = 2
EXTRA = 128
VMEM_BYTES = 56 * 1024 * 1024

epsilon = 1e-05
rope_base = 10000.0
masked_value = -1e30
bf16 = jnp.bfloat16
f32 = jnp.float32


def dot(left, right, dims):
    return lax.dot_general(left, right, (dims, ((), ())), preferred_element_type=f32)


def cuts(extent, parts):
    unit = 16 if extent % 16 == 0 and extent // 16 >= parts else 1
    units = extent // unit
    sizes = [(units // parts + (1 if i < units % parts else 0)) * unit for i in range(parts)]
    points = [0]
    for size in sizes:
        points.append(points[-1] + size)
    return points


def swap(value, axis, count, bit):
    return lax.ppermute(value, axis, [(i, i ^ bit) for i in range(count)])


def after(value, *others):
    return lax.optimization_barrier((value, others))[0]


def gather_step(state, axis, count, *first):
    steps = count.bit_length() - 1
    came = []
    for index, (arrays, found) in enumerate(state):
        bit = 1 << ((index + len(arrays) - 1) % steps)
        send = arrays[0] if len(arrays) == 1 else jnp.concatenate(arrays)
        new = swap(after(send, *first) if first else send, axis, count, bit)
        for block, place in enumerate(list(found)):
            found[place ^ bit] = (new, block)
        arrays.append(new)
        came.append(new)
    return came


def gather_start(shards):
    return [([shard], {0: (shard, 0)}) for shard in shards]


def gathered(state):
    return [
        [(*found[place], arrays[0].shape[0]) for place in range(len(found))] for arrays, found in state
    ]


def scatter_step(state, axis, count, step, *first):
    steps = count.bit_length() - 1
    sends = []
    for index, found in enumerate(state):
        bit = 1 << ((index + steps - 1 - step) % steps)
        away = [p for p in sorted(found) if p & bit]
        send = [found.pop(p).astype(bf16) for p in away]
        sends.append((bit, away, jnp.concatenate(send) if len(send) > 1 else send[0]))
    if first:
        held = after([send for _, _, send in sends], *first)
        sends = [(bit, away, send) for (bit, away, _), send in zip(sends, held)]
    came = [swap(send, axis, count, bit) for bit, _, send in sends]
    for found, (bit, away, _), new in zip(state, sends, came):
        rows = found[0].shape[0]
        for block, p in enumerate(away):
            part = lax.slice_in_dim(new, block * rows, (block + 1) * rows, axis=0)
            if step == steps - 1:
                found[p ^ bit] = (found[p ^ bit], part)
            else:
                found[p ^ bit] = found[p ^ bit].astype(f32) + part.astype(f32)
    return came


def scatter_sums(state, *first):
    last = [found[0] for found in state]
    last = after(last, *first) if first else last
    return [one.astype(f32) + other.astype(f32) for one, other in last]


def scatter_state(pieces):
    return [dict(enumerate(own)) for own in pieces]


def row_parts(pieces, parts):
    points = cuts(pieces[0].shape[0], parts)
    return [[piece[points[j] : points[j + 1]] for piece in pieces] for j in range(parts)]


def scatter_xor(pieces, axis, count):
    parts = count.bit_length() - 1
    state = scatter_state(row_parts(pieces, parts))
    came = ()
    for step in range(parts):
        came = scatter_step(state, axis, count, step, *came)
    return jnp.concatenate(scatter_sums(state))


def joined(state):
    return [
        jnp.concatenate([array[block * rows : (block + 1) * rows] for array, block, rows in own])
        for own in zip(*gathered(state))
    ]


def xor_blocks(value, own, count, dim):
    width = value.shape[dim] // count
    return jnp.concatenate(
        [lax.dynamic_slice_in_dim(value, (own ^ k) * width, width, dim) for k in range(count)], axis=dim
    )


def cost(flops, moved, exps=0):
    return pl.CostEstimate(flops=flops, bytes_accessed=moved, transcendentals=exps)


def params(steps):
    return pltpu.CompilerParams(
        dimension_semantics=("arbitrary",) * steps, vmem_limit_bytes=VMEM_BYTES
    )


def turn(values, cosine, sine):
    return values * cosine + pltpu.roll(values, HEAD_DIM // 2, 1) * sine


def project_kernel(columns, tokens, scale, gain, weights, projected, normed, squares):
    low = (tokens[...].astype(f32) * scale[...] * gain[...]).astype(bf16)
    normed[...] = low
    part = weights[...].reshape(low.shape[1], weights.shape[3])[:, : 3 * columns]
    new = dot(low, part, ((1,), (0,)))
    step = pl.program_id(0)

    @pl.when(step == 0)
    def _():
        projected[...] = new

    @pl.when(step > 0)
    def _():
        projected[...] += new

    @pl.when(step == pl.num_programs(0) - 1)
    def _():
        ones = jnp.ones((8, columns), bf16)
        for i in range(2):
            own = projected[:, i * columns : (i + 1) * columns]
            full = own * own
            high = full.astype(bf16)
            low = (full - high.astype(f32)).astype(bf16)
            total = dot(ones, high, ((1,), (1,))) + dot(ones, low, ((1,), (1,)))
            squares[i : i + 1] = total[0:1]


def project(tokens, scale, gain, packed, columns):
    rows, width = tokens.shape
    n_exp, n_ctx, part, wide = packed.shape
    cut = n_exp * part
    return pl.pallas_call(
        lambda *refs: project_kernel(columns, *refs),
        grid=(n_ctx,),
        in_specs=[
            pl.BlockSpec((rows, cut), lambda c: (0, c)),
            pl.BlockSpec((rows, 1), lambda c: (0, 0)),
            pl.BlockSpec((1, cut), lambda c: (0, c)),
            pl.BlockSpec((n_exp, 1, part, wide), lambda c: (0, c, 0, 0)),
        ],
        out_specs=[
            pl.BlockSpec((rows, 3 * columns), lambda c: (0, 0)),
            pl.BlockSpec((rows, cut), lambda c: (0, c)),
            pl.BlockSpec((2, rows), lambda c: (0, 0)),
        ],
        out_shape=[
            jax.ShapeDtypeStruct((rows, 3 * columns), f32),
            jax.ShapeDtypeStruct((rows, width), bf16),
            jax.ShapeDtypeStruct((2, rows), f32),
        ],
        compiler_params=params(1),
        cost_estimate=cost(6 * rows * width * columns, 4 * rows * width + 2 * packed.size + 12 * rows * columns),
        name="project",
    )(tokens, scale, gain, packed)


def side_grads_kernel(columns, normed, d_value, attended, d_branch, out):
    shape = (*out.shape[:3], columns)
    grad = dot(normed[...], d_value[...], ((0,), (0,))).astype(bf16)
    out[:, :, :, :columns] = grad.reshape(shape)
    grad = dot(attended[...], d_branch[...], ((0,), (0,))).astype(bf16)
    out[:, :, :, columns:] = grad.reshape(shape)


def side_grads(normed, d_value, attended, d_branch, n_exp, n_ctx):
    rows, width = normed.shape
    columns, cut = d_value.shape[1], width // n_ctx
    part = cut // n_exp
    here = pl.BlockSpec((rows, cut), lambda c: (0, c))
    whole = pl.BlockSpec((rows, columns), lambda c: (0, 0))
    return pl.pallas_call(
        lambda *refs: side_grads_kernel(columns, *refs),
        grid=(n_ctx,),
        in_specs=[here, whole, whole, here],
        out_specs=pl.BlockSpec((n_exp, 1, part, 2 * columns), lambda c: (0, c, 0, 0)),
        out_shape=jax.ShapeDtypeStruct((n_exp, n_ctx, part, 2 * columns), bf16),
        compiler_params=params(1),
        cost_estimate=cost(4 * rows * width * columns, 6 * rows * width),
        name="side_grads",
    )(normed, d_value, attended, d_branch)


def project_back_kernel(columns, d_projected, weights, tokens, scale, normed, beside, d_normed, out):
    part = weights[...].reshape(normed.shape[1], weights.shape[3])[:, : 3 * columns]
    grad = dot(d_projected[...], part, ((1,), (1,)))
    d_normed[...] = grad.astype(bf16)
    moved = (grad * tokens[...].astype(f32) * scale[...]).astype(bf16)
    gain = dot(moved, jnp.ones((moved.shape[0], EXTRA), bf16), ((0,), (0,)))
    small = jnp.where(lax.broadcasted_iota(jnp.int32, gain.shape, 1) == 0, gain, beside[...])
    grads = dot(normed[...], d_projected[:, : 2 * columns], ((0,), (0,)))
    shape = out.shape[:3]
    out[:, :, :, : 2 * columns] = grads.astype(bf16).reshape(*shape, 2 * columns)
    out[:, :, :, 2 * columns :] = small.astype(bf16).reshape(*shape, EXTRA)


def project_back(d_projected, packed, tokens, scale, normed, beside):
    rows, width = normed.shape
    n_exp, n_ctx, part, wide = packed.shape
    columns, cut = d_projected.shape[1] // 3, n_exp * part
    here = pl.BlockSpec((rows, cut), lambda c: (0, c))
    return pl.pallas_call(
        lambda *refs: project_back_kernel(columns, *refs),
        grid=(n_ctx,),
        in_specs=[
            pl.BlockSpec((rows, 3 * columns), lambda c: (0, 0)),
            pl.BlockSpec((n_exp, 1, part, wide), lambda c: (0, c, 0, 0)),
            here,
            pl.BlockSpec((rows, 1), lambda c: (0, 0)),
            here,
            pl.BlockSpec((cut, EXTRA), lambda c: (c, 0)),
        ],
        out_specs=[
            here,
            pl.BlockSpec((n_exp, 1, part, 2 * columns + EXTRA), lambda c: (0, c, 0, 0)),
        ],
        out_shape=[
            jax.ShapeDtypeStruct((rows, width), bf16),
            jax.ShapeDtypeStruct((n_exp, n_ctx, part, 2 * columns + EXTRA), bf16),
        ],
        compiler_params=params(1),
        cost_estimate=cost(0, 8 * rows * columns),
        name="project_back",
    )(d_projected, packed, tokens, scale, normed, beside)


def causal_scores(queries, keys, start):
    scores = dot(queries, keys, ((1,), (1,))) * HEAD_DIM ** (-0.5)
    row = lax.broadcasted_iota(jnp.int32, scores.shape, 0) + start
    return jnp.where(lax.broadcasted_iota(jnp.int32, scores.shape, 1) <= row, scores, masked_value)


def attend_kernel(
    chunk, query_p, key_p, value, stats, scale, cosine, sine, attended, query_out, key_out, log_total
):
    cos, sin = cosine[...], sine[...]
    scales = scale[0]
    query = turn(query_p[...] * stats[:, 0:1] * scales[0:1], cos, sin).astype(bf16)
    keyv = turn(key_p[...] * stats[:, 1:2] * scales[1:2], cos, sin).astype(bf16)
    query_out[...] = query
    key_out[...] = keyv
    values = value[...].astype(bf16)
    for start in range(0, query_p.shape[0], chunk):
        end = start + chunk
        scores = causal_scores(query[start:end], keyv[:end], start)
        peak = jnp.max(scores, axis=1, keepdims=True)
        exponent = jnp.exp(scores - peak)
        total = jnp.sum(exponent, axis=1, keepdims=True)
        weights = (exponent * (1.0 / total)).astype(bf16)
        attended[start:end] = dot(weights, values[:end], ((1,), (0,))).astype(bf16)
        log_total[0, start:end] = peak + jnp.log(total)


def attend(projected, stats, scales, cosine, sine, heads):
    rows = projected.shape[0]
    head = lambda offset: pl.BlockSpec((rows, HEAD_DIM), lambda h: (0, offset + h))
    whole = lambda shape: pl.BlockSpec(shape, lambda h: (0,) * len(shape))
    low = jax.ShapeDtypeStruct((rows, heads * HEAD_DIM), bf16)
    return pl.pallas_call(
        lambda *refs: attend_kernel(min(256, rows), *refs),
        grid=(heads,),
        in_specs=[
            head(0), head(heads), head(2 * heads),
            whole((rows, 2)),
            pl.BlockSpec((1, 2, HEAD_DIM), lambda h: (h, 0, 0)),
            whole((rows, HEAD_DIM)), whole((rows, HEAD_DIM)),
        ],
        out_specs=[head(0), head(0), head(0), pl.BlockSpec((1, rows, 1), lambda h: (h, 0, 0))],
        out_shape=[low, low, low, jax.ShapeDtypeStruct((heads, rows, 1), f32)],
        compiler_params=params(1),
        cost_estimate=cost(4 * heads * rows * rows * HEAD_DIM, 24 * low.size // 2, heads * rows * rows),
        name="attend",
    )(projected, projected, projected, stats, scales, cosine, sine)


def attend_back_kernel(
    chunk, query_p, key_p, value, query, keyv, d_attended, log_total, stats, scale, cosine, sine,
    d_query, d_key, d_value, inner_q, inner_k, gains, value_sum,
):
    values = value[...].astype(bf16)
    keys = keyv[...]
    length = query_p.shape[0]
    for start in reversed(range(0, length, chunk)):
        end = start + chunk
        queries, pull = query[start:end], d_attended[start:end]
        probs = jnp.exp(causal_scores(queries, keys[:end], start) - log_total[0, start:end])
        d_probs = dot(pull, values[:end], ((1,), (1,)))
        inner = jnp.sum(probs * d_probs, axis=1, keepdims=True)
        d_scores = (probs * (d_probs - inner)).astype(bf16)
        d_query[start:end] = dot(d_scores, keys[:end], ((1,), (0,)))
        more_key = dot(d_scores, queries, ((0,), (0,)))
        more_value = dot(probs.astype(bf16), pull, ((0,), (0,)))
        if end == length:
            d_key[...] = more_key
            value_sum[...] = more_value
        else:
            d_key[:end] += more_key
            value_sum[:end] += more_value
    d_value[...] = value_sum[...].astype(bf16)
    cos, sin = cosine[...], -sine[...]
    scales = scale[0]
    for index, (grad, before, inner_out) in enumerate(
        ((d_query, query_p, inner_q), (d_key, key_p, inner_k))
    ):
        back = turn(grad[...] * HEAD_DIM ** (-0.5), cos, sin)
        grad[...] = back
        moved = back * before[...]
        inner_out[0] = jnp.sum(moved * scales[index : index + 1], axis=1, keepdims=True)
        gains[0, index : index + 1] = jnp.sum(moved * stats[:, index : index + 1], axis=0, keepdims=True)


def attend_back(projected, query, keyv, d_attended, log_total, stats, scales, cosine, sine, heads):
    rows = projected.shape[0]
    head = lambda offset: pl.BlockSpec((rows, HEAD_DIM), lambda h: (0, offset + h))
    whole = lambda shape: pl.BlockSpec(shape, lambda h: (0,) * len(shape))
    column = pl.BlockSpec((1, rows, 1), lambda h: (h, 0, 0))
    pair = pl.BlockSpec((1, 2, HEAD_DIM), lambda h: (h, 0, 0))
    full = (rows, heads * HEAD_DIM)
    return pl.pallas_call(
        lambda *refs: attend_back_kernel(min(256, rows), *refs),
        grid=(heads,),
        in_specs=[
            head(0), head(heads), head(2 * heads), head(0), head(0), head(0),
            column, whole((rows, 2)), pair,
            whole((rows, HEAD_DIM)), whole((rows, HEAD_DIM)),
        ],
        out_specs=[head(0), head(0), head(0), column, column, pair],
        out_shape=[
            jax.ShapeDtypeStruct(full, f32),
            jax.ShapeDtypeStruct(full, f32),
            jax.ShapeDtypeStruct(full, bf16),
            jax.ShapeDtypeStruct((heads, rows, 1), f32),
            jax.ShapeDtypeStruct((heads, rows, 1), f32),
            jax.ShapeDtypeStruct((heads, 2, HEAD_DIM), f32),
        ],
        scratch_shapes=[pltpu.VMEM((rows, HEAD_DIM), f32)],
        compiler_params=params(1),
        cost_estimate=cost(0, 8 * rows * HEAD_DIM),
        name="attend_back",
    )(
        projected, projected, projected, query, keyv, d_attended, log_total, stats, scales, cosine, sine
    )


def block_of(place):
    array, block, rows = place
    return pl.BlockSpec((rows, array.shape[1]), lambda i: (block, 0))


def pull_down_kernel(places, own, pull, *refs):
    down_w, (out, down) = refs[:-2], refs[-2:]

    @pl.when(pl.program_id(0) == 0)
    def _():
        for (k, unit, offset), part in zip(places, down_w):
            start = pl.multiple_of((own[0] ^ k) * unit + offset, 16)
            down[pl.ds(start, part.shape[0]), :] = part[...]

    out[...] = dot(pull[...], down[...], ((1,), (1,)))


def pull_down(own, pull, down_k):
    rows, width = pull.shape
    sizes = [part[0][2] for part in down_k]
    unit = sum(sizes)
    hidden = unit * len(down_k[0])
    places = [
        (k, unit, sum(sizes[:j])) for j in range(len(down_k)) for k in range(len(down_k[0]))
    ]
    flat = [place for part in down_k for place in part]
    block = min(512, rows)
    here = lambda n: pl.BlockSpec((block, n), lambda i: (i, 0))
    return pl.pallas_call(
        lambda *refs: pull_down_kernel(places, *refs),
        grid=(rows // block,),
        in_specs=[pl.BlockSpec(memory_space=pltpu.SMEM), here(width)] + [block_of(w) for w in flat],
        out_specs=[here(hidden), pl.BlockSpec((hidden, width), lambda i: (0, 0))],
        out_shape=[
            jax.ShapeDtypeStruct((rows, hidden), f32),
            jax.ShapeDtypeStruct((hidden, width), bf16),
        ],
        compiler_params=params(1),
        cost_estimate=cost(2 * rows * width * hidden, 2 * rows * width + 4 * width * hidden + 4 * rows * hidden),
        name="pull_down",
    )(own, pull, *[w[0] for w in flat])


def experts_kernel(e, n_ctx, mixed, back, gates, *refs):
    gate_w, up_w = refs[:n_ctx], refs[n_ctx : 2 * n_ctx]
    hidden_g, d_acts, d_gates = refs[2 * n_ctx :]
    depth, width = gate_w[0].shape
    gate = gates[:, e : e + 1]
    gate_act = up_act = 0.0
    for k in range(n_ctx):
        rows = mixed[:, k * depth : (k + 1) * depth]
        gate_act += dot(rows, gate_w[k][...], ((1,), (0,)))
        up_act += dot(rows, up_w[k][...], ((1,), (0,)))
    sig = jax.nn.sigmoid(gate_act)
    silu = gate_act * sig
    hidden = (silu * up_act).astype(bf16).astype(f32)
    d_gates[...] = jnp.sum(hidden * back[...], axis=1, keepdims=True)
    hidden_g[...] = (gate * hidden).astype(bf16)
    d_hidden = gate * back[...]
    d_acts[:, :width] = (d_hidden * up_act * sig * (1.0 + gate_act * (1.0 - sig))).astype(bf16)
    d_acts[:, width:] = (d_hidden * silu).astype(bf16)


def run_experts(mixed, back, gates, gate_k, up_k, e):
    rows, wide = mixed.shape
    hidden = back.shape[1]
    width = gate_k[0][2] * len(gate_k)
    block = min(256, rows)
    here = lambda n: pl.BlockSpec((block, n), lambda i: (i, 0))
    return pl.pallas_call(
        lambda *refs: experts_kernel(e, len(gate_k), *refs),
        grid=(rows // block,),
        in_specs=[here(wide), here(hidden), here(gates.shape[1])] + [block_of(w) for w in (*gate_k, *up_k)],
        out_specs=[here(hidden), here(2 * hidden), here(1)],
        out_shape=[
            jax.ShapeDtypeStruct((rows, hidden), bf16),
            jax.ShapeDtypeStruct((rows, 2 * hidden), bf16),
            jax.ShapeDtypeStruct((rows, 1), f32),
        ],
        compiler_params=params(1),
        cost_estimate=cost(
            4 * rows * width * hidden, 2 * (rows * width + 2 * width * hidden + 5 * rows * hidden), rows * hidden
        ),
        name="expert",
    )(mixed, back, gates, *[w[0] for w in (*gate_k, *up_k)])


def combine_kernel(count, *refs):
    total = dot(refs[0][...], refs[count][...], ((1,), (0,)))
    for e in range(1, count):
        total += dot(refs[e][...], refs[count + e][...], ((1,), (0,)))
    refs[-1][...] = total.astype(bf16)


def combine(hidden_g, down_w):
    count, (rows, hidden), width = len(hidden_g), hidden_g[0].shape, down_w[0].shape[1]
    block = min(512, rows)
    return pl.pallas_call(
        lambda *refs: combine_kernel(count, *refs),
        grid=(rows // block,),
        in_specs=[pl.BlockSpec((block, hidden), lambda i: (i, 0))] * count
        + [pl.BlockSpec((hidden, width), lambda i: (0, 0))] * count,
        out_specs=pl.BlockSpec((block, width), lambda i: (i, 0)),
        out_shape=jax.ShapeDtypeStruct((rows, width), bf16),
        compiler_params=params(1),
        cost_estimate=cost(2 * count * rows * width * hidden, 2 * count * hidden * (rows + width) + 2 * rows * width),
        name="combine",
    )(*hidden_g, *down_w)


def rows_back_kernel(count, n_ctx, *refs):
    d_acts, weights = refs[:count], refs[count : count * (1 + 2 * n_ctx)]
    d_logits, router, out = refs[count * (1 + 2 * n_ctx) :]
    depth, hidden = weights[0].shape
    for k in range(n_ctx):
        here = slice(k * depth, (k + 1) * depth)
        total = dot(d_logits[...], router[here], ((1,), (1,)))
        for e in range(count):
            for half in range(2):
                part = weights[(2 * e + half) * n_ctx + k]
                total += dot(d_acts[e][:, half * hidden : (half + 1) * hidden], part[...], ((1,), (1,)))
        out[:, here] = total.astype(bf16)


def rows_back(d_acts, d_logits, weights, router):
    rows = d_logits.shape[0]
    count, n_ctx = len(d_acts), len(weights[0][0])
    flat = [part for pair in weights for parts in pair for part in parts]
    depth, hidden = flat[0][2], flat[0][0].shape[1]
    block = min(512, rows)
    here = lambda n: pl.BlockSpec((block, n), lambda i: (i, 0))
    return pl.pallas_call(
        lambda *refs: rows_back_kernel(count, n_ctx, *refs),
        grid=(rows // block,),
        in_specs=[here(2 * hidden)] * count
        + [block_of(w) for w in flat]
        + [here(d_logits.shape[1]), pl.BlockSpec(router.shape, lambda i: (0, 0))],
        out_specs=here(n_ctx * depth),
        out_shape=jax.ShapeDtypeStruct((rows, n_ctx * depth), bf16),
        compiler_params=params(1),
        cost_estimate=cost(0, 8 * rows * HEAD_DIM),
        name="rows_back",
    )(*d_acts, *[w[0] for w in flat], d_logits, router)


def inverse_rms(values):
    return lax.rsqrt(jnp.mean(values * values, axis=-1, keepdims=True) + epsilon)


def shards(
    tokens_in,
    positions,
    routes,
    cotangent,
    w_query,
    w_key,
    w_value,
    w_output,
    router,
    attn_gain,
    query_gain,
    key_gain,
    moe_gain,
    expert_gate,
    expert_up,
    expert_down,
):
    n_ctx, n_exp = lax.axis_size("context"), lax.axis_size("expert")
    own_ctx, own_exp = lax.axis_index("context"), lax.axis_index("expert")
    own_rows = tokens_in[0]
    tokens, width = own_rows.shape
    sequence = positions.shape[1]
    experts = EXP_DEV * n_exp
    heads = HEADS // n_ctx
    columns = heads * HEAD_DIM
    part = w_query.shape[0]

    def sum_rows(stats):
        flat = stats.reshape(-1, 128)
        return (flat + sum(swap(flat, "context", n_ctx, k) for k in range(1, n_ctx))).reshape(stats.shape)

    run = tokens // 2
    runs = positions[0].reshape(n_ctx, 2, run)[:, :, 0] // run
    runs = [
        [lax.dynamic_index_in_dim(runs[:, j], own_ctx ^ k, keepdims=False) for j in range(2)]
        for k in range(n_ctx)
    ]

    def in_sequence(pieces):
        whole = jnp.zeros((2 * n_ctx, run, width), pieces[0].dtype)
        for piece, (first, second) in zip(pieces, runs):
            whole = lax.dynamic_update_index_in_dim(whole, piece[:run], first, 0)
            whole = lax.dynamic_update_index_in_dim(whole, piece[run:], second, 0)
        return whole.reshape(sequence, width)

    def per_device(rows):
        view = rows.reshape(2 * n_ctx, run, width)
        return [
            jnp.concatenate([lax.dynamic_index_in_dim(view, at, keepdims=False) for at in pair])
            for pair in runs
        ]

    small = jnp.concatenate(
        [attn_gain[:, None], moe_gain[:, None], query_gain[:, None], key_gain[:, None], router], axis=1
    )
    small = jnp.pad(small, ((0, 0), (0, EXTRA - small.shape[1])))

    def packed_for(owner):
        cut = [lax.dynamic_slice_in_dim(w, owner * columns, columns, 1) for w in (w_query, w_key, w_value)]
        return jnp.concatenate(cut + [small], axis=1)

    def trade(blocks):
        return [blocks[0]] + [swap(blocks[k], "context", n_ctx, k) for k in range(1, n_ctx)]

    packed = jnp.stack(trade([packed_for(own_ctx ^ k) for k in range(n_ctx)]))
    packed = xor_blocks(packed, own_ctx, n_ctx, 0)
    packed = lax.all_gather(packed, "expert", axis=0, tiled=False)
    small_full = packed[:, :, :, 3 * columns :].transpose(1, 0, 2, 3).reshape(width, EXTRA)
    small_rows = small_full[:, :4].T.astype(f32)
    attn_scale, moe_scale = small_rows[0], small_rows[1]
    query_scale = lax.dynamic_slice_in_dim(small_rows[2], own_ctx * columns, columns)
    key_scale = lax.dynamic_slice_in_dim(small_rows[3], own_ctx * columns, columns)
    router_full = jnp.pad(small_full[:, 4 : 4 + experts], ((0, 0), (0, EXTRA - experts)))

    steps = n_ctx.bit_length() - 1
    points = cuts(tokens, steps)
    state = gather_start([own_rows[points[j] : points[j + 1]] for j in range(steps)])
    for _ in range(steps):
        gather_step(state, "context", n_ctx)
    inputs = in_sequence(joined(state))
    places = xor_blocks(positions[0], own_ctx, n_ctx, 0)
    named = jnp.sum(
        (routes[0][:, :, None] == jnp.arange(experts, dtype=jnp.int32)[None, None, :]).astype(f32), axis=1
    )
    w_out = lax.all_gather(after(w_output, inputs), "expert", axis=0, tiled=True)

    downs = []
    for e in range(EXP_DEV):
        points = cuts(expert_down.shape[1], steps)
        downs.append(
            gather_start([expert_down[e, points[j] : points[j + 1]] for j in range(steps)])
        )
    down_came = gather_step(downs[0], "context", n_ctx)

    pull = lax.all_gather(after(cotangent[0], down_came), "expert", axis=0, tiled=True)
    down_came = [gather_step(state, "context", n_ctx, down_came) for state in downs[1:]]
    down_came = [gather_step(downs[0], "context", n_ctx, down_came) for _ in range(steps - 1)]
    input_r = inverse_rms(inputs.astype(f32))
    projected, normed, squares = project(inputs, input_r, attn_scale[None], packed, columns)
    query_p, key_p = projected[:, :columns], projected[:, columns : 2 * columns]
    squares = sum_rows(after(squares, down_came))
    r_both = lax.rsqrt(squares / width + epsilon)
    down_came = [gather_step(state, "context", n_ctx, r_both) for _ in range(steps - 1) for state in downs[1:]]
    query_r, key_r = r_both[0][:, None], r_both[1][:, None]
    frequency = jnp.exp(
        jnp.arange(HEAD_DIM // 2, dtype=f32) * (-2.0 * math.log(rope_base) / HEAD_DIM)
    )
    angles = jnp.arange(sequence, dtype=f32)[:, None] * frequency[None, :]
    cosine, sine = jnp.cos(angles), jnp.sin(angles)
    cosine, sine = jnp.concatenate([cosine, cosine], 1), jnp.concatenate([-sine, sine], 1)
    stats = r_both.T
    scales = jnp.stack(
        [query_scale.reshape(heads, HEAD_DIM), key_scale.reshape(heads, HEAD_DIM)], axis=1
    )
    attended, query, keyv, log_total = attend(
        projected, stats, scales, cosine, sine, heads
    )
    branch = dot(attended, w_out, ((1,), (0,))).astype(bf16)
    branch = after(branch, down_came)
    branch_own = scatter_xor(per_device(branch), "context", n_ctx)
    middle = own_rows.astype(f32) + branch_own
    middle_r = inverse_rms(middle)
    mixed_own = (middle * middle_r * moe_scale).astype(bf16)

    own_probs = jax.nn.softmax(dot(mixed_own, router_full, ((1,), (0,)))[:, :experts], axis=-1)
    probs_high = own_probs.astype(bf16)
    probs_low = (own_probs - probs_high.astype(f32)).astype(bf16)
    beside = jnp.concatenate([probs_high, probs_low, named.astype(bf16)], axis=1)
    beside = jnp.pad(beside, ((0, 0), (0, EXTRA - beside.shape[1])))
    mixed_own = jnp.concatenate([xor_blocks(mixed_own, own_ctx, n_ctx, 1), beside], axis=1)
    mixed_wide = lax.all_gather(mixed_own, "expert", axis=0, tiled=True)

    own = own_ctx.astype(jnp.int32)[None]
    weights, first_came, backs, down_w = [], [], [], []
    for e in range(EXP_DEV):
        back, down = pull_down(own, after(pull, mixed_own, *backs), gathered(downs[e]))
        backs.append(back)
        down_w.append(down)
    links_free = [branch_own]
    for e in range(EXP_DEV):
        pair = gather_start([expert_gate[e], expert_up[e]])
        came = [gather_step(pair, "context", n_ctx, *links_free)]
        came += [gather_step(pair, "context", n_ctx) for _ in range(steps - 1)]
        weights.append(gathered(pair))
        first_came.append(came[0])
        links_free = [branch_own, came]
    mixed_wide = after(mixed_wide, backs)
    mixed, beside = mixed_wide[:, :width], mixed_wide[:, width:].astype(f32)
    router_x = xor_blocks(router_full, own_ctx, n_ctx, 0)
    router_probs = beside[:, :experts] + beside[:, experts : 2 * experts]
    named_all = beside[:, 2 * experts : 3 * experts]
    local = own_exp * EXP_DEV
    gates = lax.dynamic_slice_in_dim(router_probs * named_all, local, EXP_DEV, 1)
    def weight_grad(left, right):
        return dot(left, right, ((0,), (0,))).astype(bf16)

    def gate_up_grads(e, *first):
        grads = after(d_acts[e], *first)
        return weight_grad(mixed, grads[:, :ff]), weight_grad(mixed, grads[:, ff:])

    def owner_rows(grad):
        rows = ff // n_ctx
        return [lax.dynamic_slice_in_dim(grad, (own_ctx ^ k) * rows, rows, 0) for k in range(n_ctx)]

    def sums_of(state):
        return scatter_sums(state, last_came)

    ff = backs[0].shape[1]
    hidden_g, d_acts, d_gates, g_raw = [], [], [], []
    for e in range(EXP_DEV):
        rows_in = after(mixed_wide, g_raw, backs[e])
        for kept, made in zip(
            (hidden_g, d_acts, d_gates), run_experts(rows_in, backs[e], gates, *weights[e], e)
        ):
            kept.append(made)
        if e + 1 < EXP_DEV:
            g_raw.append(gate_up_grads(e, first_came[e + 1]))
    pairs = [scatter_state([jnp.split(grad, n_ctx) for grad in raw]) for raw in g_raw]
    pair_came = [scatter_step(pair, "context", n_ctx, 0) for pair in pairs]

    slots = jnp.arange(experts, dtype=jnp.int32)[None, :]
    drp = sum(
        jnp.where(slots == local + e, d_gates[e] * named_all, 0.0) for e in range(EXP_DEV)
    )
    d_logits = (
        router_probs * (drp - jnp.sum(router_probs * drp, axis=-1, keepdims=True))
    ).astype(bf16)
    d_logits = jnp.pad(d_logits, ((0, 0), (0, EXTRA - experts)))

    d_mixed_part = rows_back(d_acts, d_logits, weights, router_x)
    d_mixed_part = after(d_mixed_part, pair_came)
    pair_came = [
        scatter_step(pair, "context", n_ctx, step, pair_came) for pair in pairs for step in range(1, steps)
    ]
    d_mixed = lax.psum_scatter(d_mixed_part, "expert", scatter_dimension=0, tiled=True).astype(f32)
    d_mixed = xor_blocks(d_mixed, own_ctx, n_ctx, 1)

    raw = gate_up_grads(EXP_DEV - 1, d_mixed_part)
    pairs.append(scatter_state([jnp.split(grad, n_ctx) for grad in raw]))
    last_came = scatter_step(pairs[-1], "context", n_ctx, 0, pair_came)
    down_raw = [weight_grad(after(hidden_g[0], raw), pull)]
    out_part = combine(after(hidden_g, down_raw, pair_came), down_w)
    out_part = after(out_part, last_came)
    out_own = lax.psum_scatter(out_part, "expert", scatter_dimension=0, tiled=True).astype(f32)
    d_mixed = after(d_mixed, out_part)
    downs = [scatter_state(row_parts(owner_rows(down_raw[0]), steps))]
    down_came = scatter_step(downs[0], "context", n_ctx, 0, last_came)

    scaled = d_mixed * moe_scale
    g_moe = jnp.sum(d_mixed * middle * middle_r, axis=0)
    d_middle = (
        cotangent[0].astype(f32)
        + middle_r * scaled
        - middle * (middle_r**3 * jnp.mean(scaled * middle, axis=-1, keepdims=True))
    )
    points = cuts(tokens, steps)
    d_low = after(d_middle.astype(bf16), down_came)
    state = gather_start([d_low[points[j] : points[j + 1]] for j in range(steps)])
    for step in range(max(steps, EXP_DEV - 1)):
        if step < steps:
            gather_step(state, "context", n_ctx)
        if step + 1 < EXP_DEV:
            down_raw.append(weight_grad(after(hidden_g[step + 1], d_middle), pull))
    g_router = dot(mixed, after(d_logits, d_low), ((0,), (0,)))
    d_branch = after(in_sequence(joined(state)), down_raw, g_router)
    downs += [scatter_state(row_parts(owner_rows(grad), steps)) for grad in down_raw[1:]]
    last_came = [
        scatter_step(pairs[-1], "context", n_ctx, step, d_branch) for step in range(1, steps)
    ]

    d_attended = dot(d_branch, w_out, ((1,), (1,))).astype(bf16)
    d_query, d_key, d_value, inner_q, inner_k, g_heads = attend_back(
        projected, query, keyv, d_attended, log_total, stats, scales, cosine, sine, heads
    )
    result = (middle + after(out_own, d_query)).astype(bf16)
    inner_q, inner_k = jnp.sum(inner_q[:, :, 0], axis=0), jnp.sum(inner_k[:, :, 0], axis=0)
    inner_both = after(jnp.stack([inner_q, inner_k]), last_came)
    inner_both = sum_rows(inner_both) / width
    g_side = side_grads(normed, after(d_value, inner_both), attended, d_branch, n_exp, n_ctx)
    g_heads = g_heads.transpose(1, 0, 2).reshape(2, columns)
    d_query_p = query_r * (query_scale * d_query) - query_p * (query_r**3 * inner_both[0][:, None])
    d_key_p = key_r * (key_scale * d_key) - key_p * (key_r**3 * inner_both[1][:, None])
    d_projected = jnp.concatenate(
        [d_query_p.astype(bf16), d_key_p.astype(bf16), d_value], axis=1
    )
    spread = lax.dynamic_update_slice(
        jnp.zeros((2, width), f32), g_heads, (jnp.zeros_like(own_ctx), own_ctx * columns)
    )
    g_router = xor_blocks(g_router[:, :experts], own_ctx, n_ctx, 0)
    beside = jnp.concatenate([jnp.zeros((width, 1), f32), g_moe[:, None], spread.T, g_router], axis=1)
    beside = jnp.pad(beside, ((0, 0), (0, EXTRA - beside.shape[1])))
    g_side_sum = lax.psum_scatter(g_side.reshape(width, 2 * columns), "expert", scatter_dimension=0, tiled=True)
    d_projected = after(d_projected, g_side)
    d_normed_part, g_packed = project_back(d_projected, packed, inputs, input_r, normed, beside)
    down_came = [scatter_step(down, "context", n_ctx, 0, inner_both) for down in downs[1:]]
    g_packed = after(g_packed, down_came)
    d_normed = scatter_state(row_parts(per_device(d_normed_part), steps))
    last_came = scatter_step(d_normed, "context", n_ctx, 0)
    for step in range(1, steps):
        scatter_step(d_normed, "context", n_ctx, step)
        for down in downs:
            scatter_step(down, "context", n_ctx, step)
    d_normed = jnp.concatenate(scatter_sums(d_normed))
    own_in = own_rows.astype(f32)
    own_r = inverse_rms(own_in)
    scaled_in = d_normed * attn_scale
    input_grad = (
        d_middle
        + own_r * scaled_in
        - own_in * (own_r**3 * jnp.mean(scaled_in * own_in, axis=-1, keepdims=True))
    )

    def to_owners(grads):
        grads = xor_blocks(grads.reshape(n_ctx, part, -1), own_ctx, n_ctx, 0)
        grads = jnp.stack(trade([grads[k] for k in range(n_ctx)])).astype(f32)
        return xor_blocks(grads, own_ctx, n_ctx, 0)

    def full_rows(grads):
        return grads.transpose(1, 0, 2).reshape(part, width)

    g_packed = g_packed.reshape(width, 2 * columns + EXTRA)
    g_packed = lax.psum_scatter(g_packed, "expert", scatter_dimension=0, tiled=True)
    g_packed = to_owners(jnp.concatenate([g_packed, g_side_sum[:, :columns]], axis=1))
    g_small = jnp.sum(g_packed[:, :, 2 * columns : 2 * columns + EXTRA], axis=0)
    return (
        result[None],
        input_grad[None],
        full_rows(g_packed[:, :, :columns]),
        full_rows(g_packed[:, :, columns : 2 * columns]),
        full_rows(g_packed[:, :, 2 * columns + EXTRA :]),
        full_rows(g_side_sum[:, columns:].astype(f32).reshape(n_ctx, part, columns)),
        g_small[:, 4 : 4 + experts],
        g_small[:, 0],
        g_small[:, 2],
        g_small[:, 3],
        g_small[:, 1],
        jnp.stack([sums_of(pair)[0] for pair in pairs]),
        jnp.stack([sums_of(pair)[1] for pair in pairs]),
        jnp.stack([jnp.concatenate(sums_of(down)) for down in downs]),
    )


def solution(mesh):
    rows = P("expert", "context", None)
    split = P(("context", "expert"), None)
    line = P(("context", "expert"))
    return jax.shard_map(
        shards,
        mesh=mesh,
        in_specs=(rows, P("expert", None), rows, rows) + (split,) * 5 + (line,) * 4 + (rows,) * 3,
        out_specs=(rows, rows) + (split,) * 5 + (line,) * 4 + (rows,) * 3,
        check_vma=False,
    )
```
